32 devices in a mesh: rows: 8 (over z, x), cols: 4 (over y, core).
Axes of the slice: x: 2, y: 2, z: 4, core: 2. Of those that a mesh axis runs over, the one named last changes fastest.
Arguments:
- x_img: bfloat16 [8, 1024, 1536], P('rows', None, 'cols'), may hold values from -6 to 6
- x_txt: bfloat16 [8, 154, 1536], P('rows', None, 'cols'), may hold values from -6 to 6
- cond: float32 [8, 1536], P(None, 'rows'), may hold values from -6 to 6
- back_img: bfloat16 [8, 1024, 1536], P('rows', None, 'cols'), may hold values from -6 to 6
- back_txt: bfloat16 [8, 154, 1536], P('rows', None, 'cols'), may hold values from -6 to 6
- w_mod: float32 [1536, 2, 6, 1536], P('rows', None, None, 'cols'), may hold values from -0.15625 to 0.15625
- w_qkv: float32 [1536, 2, 3, 1536], P('rows', None, None, 'cols'), may hold values from -1 to 1
- w_proj: float32 [1536, 2, 1536], P('rows', None, 'cols'), may hold values from -0.4375 to 0.4375
- w_up: float32 [1536, 2, 4, 1536], P('rows', None, None, 'cols'), may hold values from -0.15625 to 0.15625
- w_down: float32 [1536, 2, 4, 1536], P('rows', None, None, 'cols'), may hold values from -0.078125 to 0.078125
- biases: float32 [2, 14, 1536], P(None, None, 'cols'), may hold values from -0.3 to 0.3
- moments_mod: float32 [2, 1536, 2, 6, 1536], P(None, 'rows', None, None, 'cols'), may hold values from -8192 to 8192, as said below
- moments_qkv: float32 [2, 1536, 2, 3, 1536], P(None, 'rows', None, None, 'cols'), may hold values from -8192 to 8192, as said below
- moments_proj: float32 [2, 1536, 2, 1536], P(None, 'rows', None, 'cols'), may hold values from -8192 to 8192, as said below
- moments_up: float32 [2, 1536, 2, 4, 1536], P(None, 'rows', None, None, 'cols'), may hold values from -8192 to 8192, as said below
- moments_down: float32 [2, 1536, 2, 4, 1536], P(None, 'rows', None, None, 'cols'), may hold values from -8192 to 8192, as said below
- moments_bias: float32 [2, 2, 14, 1536], P(None, None, None, 'cols'), may hold values from -8192 to 8192, as said below
Outputs:
- out_img: bfloat16 [8, 1024, 1536], P('rows', None, 'cols')
- out_txt: bfloat16 [8, 154, 1536], P('rows', None, 'cols')
- grad_img: float32 [8, 1024, 1536], P('rows', None, 'cols')
- grad_txt: float32 [8, 154, 1536], P('rows', None, 'cols')
- grad_cond: float32 [8, 1536], P(None, 'rows')
- grad_mod: float32 [1536, 2, 6, 1536], P('rows', None, None, 'cols')
- grad_qkv: float32 [1536, 2, 3, 1536], P('rows', None, None, 'cols')
- grad_proj: float32 [1536, 2, 1536], P('rows', None, 'cols')
- grad_up: float32 [1536, 2, 4, 1536], P('rows', None, None, 'cols')
- grad_down: float32 [1536, 2, 4, 1536], P('rows', None, None, 'cols')
- grad_bias: float32 [2, 14, 1536], P(None, None, 'cols')
- next_mod: float32 [1536, 2, 6, 1536], P('rows', None, None, 'cols')
- next_qkv: float32 [1536, 2, 3, 1536], P('rows', None, None, 'cols')
- next_proj: float32 [1536, 2, 1536], P('rows', None, 'cols')
- next_up: float32 [1536, 2, 4, 1536], P('rows', None, None, 'cols')
- next_down: float32 [1536, 2, 4, 1536], P('rows', None, None, 'cols')
- next_bias: float32 [2, 14, 1536], P(None, None, 'cols')
- next_first_mod: float32 [1536, 2, 6, 1536], P('rows', None, None, 'cols')
- next_second_mod: float32 [1536, 2, 6, 1536], P('rows', None, None, 'cols')
- next_moments_qkv: float32 [2, 1536, 2, 3, 1536], P(None, 'rows', None, None, 'cols')
- next_moments_proj: float32 [2, 1536, 2, 1536], P(None, 'rows', None, 'cols')
- next_moments_up: float32 [2, 1536, 2, 4, 1536], P(None, 'rows', None, None, 'cols')
- next_moments_down: float32 [2, 1536, 2, 4, 1536], P(None, 'rows', None, None, 'cols')
- next_first_bias: float32 [2, 14, 1536], P(None, None, 'cols')
- next_second_bias: float32 [2, 14, 1536], P(None, None, 'cols')
The draws below stay inside these ranges and needn't reach their ends.
Inputs may be any that keep to these rules, and one draw needn't show every extreme that they name: `moments_mod`: entries at index 1 of the first dimension are positive. `moments_qkv`: entries at index 1 of the first dimension are positive. `moments_proj`: entries at index 1 of the first dimension are positive. `moments_up`: entries at index 1 of the first dimension are positive. `moments_down`: entries at index 1 of the first dimension are positive. `moments_bias`: entries at index 1 of the first dimension are positive.
All inputs are finite; a program needn't handle non-finite values.
Results may differ from the reference program's by a relative error of at most 0.012.
Values may be sent and summed in bfloat16 or wider, within the bound.
No kernel may reach another device: no remote copies, remote signals or barrier semaphores. Data moves between devices by JAX's collectives and lax.ppermute only.
A program may use at most 384 MiB of HBM per device.

```python
import math
import jax
import jax.numpy as jnp
from jax import lax

D = 1536
HEAD_FEATURES = 64
IMAGE_TOKENS = 1024
TXT = 154
STEP = 2
SEQS = 8


def moment_draw(key, array_shape, stream_axis):
    first_key = jax.random.fold_in(key, 11)
    second_key = jax.random.fold_in(key, 12)
    scale_shape = [1] * len(array_shape)
    scale_shape[stream_axis] = 2
    token_stream = jnp.array([SEQS * IMAGE_TOKENS, SEQS * TXT], jnp.float32).reshape(scale_shape)
    base_draw = jax.random.truncated_normal(first_key, -6.0, 6.0, array_shape, jnp.float32)
    first_moment = 0.05 * jnp.sqrt(token_stream) * base_draw
    spread_draw = jax.random.uniform(second_key, array_shape, jnp.float32, math.log(0.3), math.log(3.0))
    second_moment = 0.0125 * token_stream * jnp.exp(spread_draw)
    return jnp.stack([first_moment, second_moment])


def draw_moments_mod(key, part):
    key = jax.random.fold_in(key, 41)
    return moment_draw(key, (D, 2, 6, D), 1)


def draw_moments_qkv(key, part):
    key = jax.random.fold_in(key, 42)
    return moment_draw(key, (D, 2, 3, D), 1)


def draw_moments_proj(key, part):
    key = jax.random.fold_in(key, 43)
    return moment_draw(key, (D, 2, D), 1)


def draw_moments_up(key, part):
    key = jax.random.fold_in(key, 44)
    return moment_draw(key, (D, 2, 4, D), 1)


def draw_moments_down(key, part):
    key = jax.random.fold_in(key, 45)
    return moment_draw(key, (D, 2, 4, D), 1)


def draw_moments_bias(key, part):
    key = jax.random.fold_in(key, 46)
    return moment_draw(key, (2, 14, D), 0)


def draw_x_img(key, part):
    key = jax.random.fold_in(key, 5)
    array_shape = (SEQS, IMAGE_TOKENS, D)
    base_draw = jax.random.truncated_normal(key, -6.0, 6.0, array_shape, jnp.float32)
    return base_draw.astype(jnp.bfloat16)


def draw_w_qkv(key, part):
    key = jax.random.fold_in(key, 6)
    array_shape = (D, 2, 3, D)
    base_draw = jax.random.truncated_normal(key, -6.0, 6.0, array_shape, jnp.float32) / D ** 0.5
    return base_draw


def with_spikes(drawn, key, source, target, blocks, factor):
    owner, partner = [(jnp.arange(drawn.shape[axis_at]) // (drawn.shape[axis_at] // blocks)).reshape([-1 if axis == axis_at else 1 for axis in range(drawn.ndim)]) for axis_at in (source, target)]
    chosen = jax.random.permutation(key, blocks)[partner]
    strong = (owner == chosen) | (owner == (partner + blocks // 2) % blocks)
    return jnp.where(strong, factor * drawn, drawn)


def levels(stream_key, dims, pieces, low, top_value):
    factor_of, own = 1.0, jax.random.fold_in(stream_key, 6)
    for axis_at, blocks in pieces:
        heights = jnp.exp(jax.random.uniform(jax.random.fold_in(own, axis_at), (blocks,), jnp.float32, low / len(pieces), top_value / len(pieces)))
        factor_of = factor_of * jnp.repeat(heights, dims[axis_at] // blocks).reshape([-1 if axis == axis_at else 1 for axis in range(len(dims))])
    return factor_of


def noise(stream_key, shape, spread, bound, cuts=(), kind=jnp.bfloat16):
    level = levels(stream_key, shape, cuts, -0.22, 0.18) if cuts else 1.0
    values = jax.random.normal(stream_key, shape, jnp.float32) * spread * level
    return jnp.minimum(jnp.maximum(values, -bound), bound).astype(kind)


def noise_with(own_key, extent, deviation, most, cuts, heavy, dtype=jnp.bfloat16):
    entries = deviation * jax.random.normal(own_key, extent, jnp.float32)
    if cuts:
        entries = entries * levels(own_key, extent, cuts, -0.22, 0.18)
    return jnp.clip(with_spikes(entries, jax.random.fold_in(own_key, 3), *heavy), -most, most).astype(dtype)


def setup_inputs(seed: int = 0) -> dict:
    seeds = jax.random.split(jax.random.key(seed), 18)
    return {
        "x_img": draw_x_img(jax.random.fold_in(seeds[17], 71), 0),
        "x_txt": noise(seeds[1], (SEQS, TXT, D), 1.0, 6.0, ((0, 8), (2, 4))),
        "cond": noise(seeds[2], (SEQS, D), 1.0, 6.0, ((1, 8),), jnp.float32),
        "back_img": noise_with(seeds[3], (SEQS, IMAGE_TOKENS, D), 1.0, 6.0, ((0, 8), (2, 4)), (0, 2, 8, 2.0)),
        "back_txt": noise_with(seeds[4], (SEQS, TXT, D), 1.0, 6.0, ((0, 8), (2, 4)), (0, 2, 8, 2.0)),
        "w_mod": noise(seeds[5], (D, 2, 6, D), D ** -0.5, 0.15625, ((0, 8), (3, 4)), jnp.float32),
        "w_qkv": draw_w_qkv(jax.random.fold_in(seeds[17], 71), 0),
        "w_proj": noise(seeds[7], (D, 2, D), (D // 8) ** -0.5, 0.4375, ((0, 8), (2, 4)), jnp.float32),
        "w_up": noise(seeds[8], (D, 2, 4, D), D ** -0.5, 0.15625, ((0, 8), (3, 4)), jnp.float32),
        "w_down": noise(seeds[9], (D, 2, 4, D), (4 * D) ** -0.5, 0.078125, ((0, 8), (3, 4)), jnp.float32),
        "biases": noise(seeds[10], (2, 14, D), 0.05, 0.3, ((2, 4),), jnp.float32),
        "moments_mod": draw_moments_mod(jax.random.fold_in(seeds[17], 71), 0),
        "moments_qkv": draw_moments_qkv(jax.random.fold_in(seeds[17], 71), 0),
        "moments_proj": draw_moments_proj(jax.random.fold_in(seeds[17], 71), 0),
        "moments_up": draw_moments_up(jax.random.fold_in(seeds[17], 71), 0),
        "moments_down": draw_moments_down(jax.random.fold_in(seeds[17], 71), 0),
        "moments_bias": draw_moments_bias(jax.random.fold_in(seeds[17], 71), 0),
    }


BETA_ONE = 0.9
BETA_TWO = 0.95
LEARN_RATE = 0.02
DECAY_RATE = 0.1
ADAM_EPS = 1e-08
NORM_EPS = 1e-06
GELU_COEF = 0.7978845608028654
GELU_CUBE = 0.044715

def narrow(values):
    return values.astype(jnp.bfloat16)

def broaden(values):
    return values.astype(jnp.float32)

def rounded(values):
    return broaden(lax.optimization_barrier(narrow(values)))

def gelu_value(inputs):
    return 0.5 * inputs * (1.0 + jnp.tanh(GELU_COEF * (inputs + GELU_CUBE * inputs * inputs * inputs)))

def gelu_slope(inputs):
    tangent = jnp.tanh(GELU_COEF * (inputs + GELU_CUBE * inputs * inputs * inputs))
    return 0.5 * (1.0 + tangent) + 0.5 * inputs * (1.0 - tangent * tangent) * GELU_COEF * (1.0 + 3.0 * GELU_CUBE * inputs * inputs)

def layer_stats(values):
    center = lax.optimization_barrier(jnp.mean(values, axis=-1, keepdims=True))
    inverse = lax.rsqrt(lax.optimization_barrier(jnp.mean(values * values, axis=-1, keepdims=True)) - center * center + NORM_EPS)
    return ((values - center) * inverse, inverse)

def layer_back(grad_unit, unit_rows, inverse):
    return inverse * (grad_unit - lax.optimization_barrier(jnp.mean(grad_unit, axis=-1, keepdims=True)) - unit_rows * lax.optimization_barrier(jnp.mean(grad_unit * unit_rows, axis=-1, keepdims=True)))

def head_split(values):
    return broaden(values).reshape(values.shape[0], D // HEAD_FEATURES, HEAD_FEATURES)

def joint_scores(triple):
    queries = head_split(triple[:, 0])
    keys_all = head_split(triple[:, 1])
    return (queries, keys_all, jnp.einsum('qhe,khe->hqk', queries, keys_all) * HEAD_FEATURES ** (-0.5))

def attention_apply(triple):
    queries, keys_all, scores = joint_scores(triple)
    values_all = head_split(triple[:, 2])
    highest = lax.optimization_barrier(jnp.max(scores, axis=-1, keepdims=True))
    log_total = highest + jnp.log(lax.optimization_barrier(jnp.sum(jnp.exp(scores - highest), axis=-1, keepdims=True)))
    soft_weights = rounded(jnp.exp(scores - log_total))
    mixture = jnp.einsum('hqk,khe->qhe', soft_weights, values_all)
    return (narrow(mixture.reshape(triple.shape[0], D)), log_total)

def attend_back(triple, log_total, grad_mix):
    queries, keys_all, scores = joint_scores(triple)
    values_all = head_split(triple[:, 2])
    grad_heads = head_split(grad_mix)
    soft_full = jnp.exp(scores - log_total)
    soft_round = rounded(soft_full)
    value_gradients = jnp.einsum('hqk,qhe->khe', soft_round, grad_heads)
    grad_soft = jnp.einsum('qhe,khe->hqk', grad_heads, values_all)
    delta_row = lax.optimization_barrier(jnp.sum(soft_full * grad_soft, axis=-1, keepdims=True))
    score_round = rounded(soft_full * (grad_soft - delta_row))
    scale_factor = HEAD_FEATURES ** (-0.5)
    grad_queries = jnp.einsum('hqk,khe->qhe', score_round, keys_all) * scale_factor
    grad_keys = jnp.einsum('hqk,qhe->khe', score_round, queries) * scale_factor
    length = triple.shape[0]
    return jnp.stack([grad_queries.reshape(length, D), grad_keys.reshape(length, D), value_gradients.reshape(length, D)], axis=1)

def adam_step(param, moments, gradient):
    first_moment = BETA_ONE * moments[0] + (1.0 - BETA_ONE) * gradient
    second_moment = BETA_TWO * moments[1] + (1.0 - BETA_TWO) * gradient * gradient
    update = first_moment / (1.0 - BETA_ONE ** STEP) / (jnp.sqrt(second_moment / (1.0 - BETA_TWO ** STEP)) + ADAM_EPS)
    return (param - LEARN_RATE * (update + DECAY_RATE * param), jnp.stack([first_moment, second_moment]))

def reference(x_img, x_txt, cond, back_img, back_txt, w_mod, w_qkv, w_proj, w_up, w_down, biases, moments_mod, moments_qkv, moments_proj, moments_up, moments_down, moments_bias):
    silu_cond = narrow(jax.nn.silu(cond))
    mod_round = narrow(w_mod)
    qkv_round = narrow(w_qkv)
    proj_round = narrow(w_proj)
    up_round = narrow(w_up)
    down_round = narrow(w_down)
    modulation = jnp.stack([jnp.dot(silu_cond, mod_round[:, stream].reshape(D, 6 * D), preferred_element_type=jnp.float32).reshape(SEQS, 6, D) for stream in range(2)], axis=1) + biases[None, :, 0:6]
    mats_qkv = [qkv_round[:, stream].reshape(D, 3 * D) for stream in range(2)]
    mats_proj = [proj_round[:, stream] for stream in range(2)]
    mats_up = [up_round[:, stream].reshape(D, 4 * D) for stream in range(2)]
    mats_down = [down_round[:, stream].reshape(D, 4 * D) for stream in range(2)]

    def sequence_step(carry, inputs):
        image_rows, text_rows, back_image, back_text, table = inputs
        stream_inputs = (image_rows, text_rows)
        stream_back = (back_image, back_text)
        first_pass = []
        triples = []
        for stream in range(2):
            source = broaden(stream_inputs[stream])
            length = source.shape[0]
            unit_one, inverse_one = layer_stats(source)
            normed_one = narrow(unit_one * (1.0 + table[stream, 1]) + table[stream, 0])
            triple = jnp.dot(normed_one, mats_qkv[stream], preferred_element_type=jnp.float32).reshape(length, 3, D)
            triple = triple + jnp.stack([biases[stream, 6], jnp.zeros((D,), jnp.float32), biases[stream, 7]])
            triples.append(narrow(triple))
            first_pass.append((source, unit_one, inverse_one, normed_one))
        joint = jnp.concatenate(triples, axis=0)
        attended, log_total = attention_apply(joint)
        grad_attended = []
        second_pass = []
        outputs = []
        for stream in range(2):
            source, unit_one, inverse_one, normed_one = first_pass[stream]
            length = source.shape[0]
            attn_part = attended[:IMAGE_TOKENS] if stream == 0 else attended[IMAGE_TOKENS:]
            projected = jnp.dot(attn_part, mats_proj[stream].T, preferred_element_type=jnp.float32) + biases[stream, 8]
            residual = source + table[stream, 2] * projected
            unit_two, inverse_two = layer_stats(residual)
            normed_two = narrow(unit_two * (1.0 + table[stream, 4]) + table[stream, 3])
            hidden_pre = jnp.dot(normed_two, mats_up[stream], preferred_element_type=jnp.float32).reshape(length, 4, D) + biases[stream, 9:13]
            hidden_act = narrow(gelu_value(hidden_pre)).reshape(length, 4 * D)
            lowered = jnp.dot(hidden_act, mats_down[stream].T, preferred_element_type=jnp.float32) + biases[stream, 13]
            outputs.append(narrow(residual + table[stream, 5] * lowered))
            cotangent = broaden(stream_back[stream])
            grad_lowered = table[stream, 5] * cotangent
            gate_two = lax.optimization_barrier(jnp.sum(cotangent * lowered, axis=0))
            lowered_round = narrow(grad_lowered)
            grad_down_part = jnp.dot(lowered_round.T, hidden_act, preferred_element_type=jnp.float32).reshape(D, 4, D)
            grad_hidden = jnp.dot(lowered_round, mats_down[stream], preferred_element_type=jnp.float32).reshape(length, 4, D) * gelu_slope(hidden_pre)
            hidden_round = narrow(grad_hidden).reshape(length, 4 * D)
            grad_up_part = jnp.dot(normed_two.T, hidden_round, preferred_element_type=jnp.float32).reshape(D, 4, D)
            grad_normed_two = jnp.dot(hidden_round, mats_up[stream].T, preferred_element_type=jnp.float32)
            shift_two = lax.optimization_barrier(jnp.sum(grad_normed_two, axis=0))
            scale_two = lax.optimization_barrier(jnp.sum(grad_normed_two * unit_two, axis=0))
            grad_residual = cotangent + layer_back(grad_normed_two * (1.0 + table[stream, 4]), unit_two, inverse_two)
            grad_projected = table[stream, 2] * grad_residual
            gate_one = lax.optimization_barrier(jnp.sum(grad_residual * projected, axis=0))
            projected_round = narrow(grad_projected)
            grad_proj_part = jnp.dot(projected_round.T, attn_part, preferred_element_type=jnp.float32)
            grad_attended.append(narrow(jnp.dot(projected_round, mats_proj[stream], preferred_element_type=jnp.float32)))
            second_pass.append((grad_residual, gate_two, shift_two, scale_two, gate_one, grad_down_part, grad_up_part, grad_proj_part, lax.optimization_barrier(jnp.sum(grad_projected, axis=0)), lax.optimization_barrier(jnp.sum(grad_hidden, axis=0)), lax.optimization_barrier(jnp.sum(grad_lowered, axis=0))))
        grad_triple = attend_back(joint, log_total, jnp.concatenate(grad_attended, axis=0))
        grads_input = []
        tables_back = []
        parts_qkv = []
        parts_bias = []
        for stream in range(2):
            source, unit_one, inverse_one, normed_one = first_pass[stream]
            grad_residual, gate_two, shift_two, scale_two, gate_one, grad_down_part, grad_up_part, grad_proj_part, bias_proj, bias_hidden, bias_lowered = second_pass[stream]
            length = source.shape[0]
            grad_part = grad_triple[:IMAGE_TOKENS] if stream == 0 else grad_triple[IMAGE_TOKENS:]
            triple_round = narrow(grad_part).reshape(length, 3 * D)
            parts_qkv.append(jnp.dot(normed_one.T, triple_round, preferred_element_type=jnp.float32).reshape(D, 3, D))
            gradient_first_normalized = jnp.dot(triple_round, mats_qkv[stream].T, preferred_element_type=jnp.float32)
            shift_one = lax.optimization_barrier(jnp.sum(gradient_first_normalized, axis=0))
            scale_one = lax.optimization_barrier(jnp.sum(gradient_first_normalized * unit_one, axis=0))
            grads_input.append(grad_residual + layer_back(gradient_first_normalized * (1.0 + table[stream, 1]), unit_one, inverse_one))
            tables_back.append(jnp.stack([shift_one, scale_one, gate_one, shift_two, scale_two, gate_two]))
            parts_bias.append(jnp.concatenate([lax.optimization_barrier(jnp.sum(grad_part[:, 0], axis=0))[None], lax.optimization_barrier(jnp.sum(grad_part[:, 2], axis=0))[None], bias_proj[None], bias_hidden, bias_lowered[None]], axis=0))
        acc_qkv, acc_proj, acc_up, acc_down, acc_bias = carry
        acc_qkv = acc_qkv + jnp.stack(parts_qkv, axis=1)
        acc_proj = acc_proj + jnp.stack([second_pass[0][7], second_pass[1][7]], axis=1)
        acc_up = acc_up + jnp.stack([second_pass[0][6], second_pass[1][6]], axis=1)
        acc_down = acc_down + jnp.stack([second_pass[0][5], second_pass[1][5]], axis=1)
        acc_bias = acc_bias + jnp.stack(parts_bias, axis=0)
        return ((acc_qkv, acc_proj, acc_up, acc_down, acc_bias), (outputs[0], outputs[1], grads_input[0], grads_input[1], jnp.stack(tables_back)))
    initial = (jnp.zeros((D, 2, 3, D), jnp.float32), jnp.zeros((D, 2, D), jnp.float32), jnp.zeros((D, 2, 4, D), jnp.float32), jnp.zeros((D, 2, 4, D), jnp.float32), jnp.zeros((2, 8, D), jnp.float32))
    sums_final, per_sequence = lax.scan(sequence_step, initial, (x_img, x_txt, back_img, back_txt, modulation))
    grad_qkv, grad_proj, grad_up, grad_down, bias_rest = sums_final
    out_img, out_txt, grad_img, grad_txt, table_all = per_sequence
    table_round = narrow(table_all)
    grad_mod = jnp.stack([jnp.dot(silu_cond.T, table_round[:, stream].reshape(SEQS, 6 * D), preferred_element_type=jnp.float32).reshape(D, 6, D) for stream in range(2)], axis=1)
    grad_bias = jnp.concatenate([lax.optimization_barrier(jnp.sum(table_all, axis=0)), bias_rest], axis=1)
    grad_silu = jnp.dot(table_round[:, 0].reshape(SEQS, 6 * D), mod_round[:, 0].reshape(D, 6 * D).T, preferred_element_type=jnp.float32)
    grad_silu = grad_silu + jnp.dot(table_round[:, 1].reshape(SEQS, 6 * D), mod_round[:, 1].reshape(D, 6 * D).T, preferred_element_type=jnp.float32)
    sigmoid_cond = jax.nn.sigmoid(cond)
    grad_cond = grad_silu * sigmoid_cond * (1.0 + cond * (1.0 - sigmoid_cond))
    next_mod, moments_mod_next = adam_step(w_mod, moments_mod, grad_mod)
    next_qkv, moments_qkv_next = adam_step(w_qkv, moments_qkv, grad_qkv)
    next_proj, moments_proj_next = adam_step(w_proj, moments_proj, grad_proj)
    next_up, moments_up_next = adam_step(w_up, moments_up, grad_up)
    next_down, moments_down_next = adam_step(w_down, moments_down, grad_down)
    next_bias, moments_bias_next = adam_step(biases, moments_bias, grad_bias)
    return (out_img, out_txt, grad_img, grad_txt, grad_cond, grad_mod, grad_qkv, grad_proj, grad_up, grad_down, grad_bias, next_mod, next_qkv, next_proj, next_up, next_down, next_bias, moments_mod_next[0], moments_mod_next[1], moments_qkv_next, moments_proj_next, moments_up_next, moments_down_next, moments_bias_next[0], moments_bias_next[1])
```

```python
import jax
import jax.numpy as jnp
from jax import lax
from jax.experimental import pallas as pl
from jax.experimental.pallas import tpu as pltpu
from jax.sharding import PartitionSpec as P

D = 1536
HEAD_FEATURES = 64
IMAGE_TOKENS = 1024
TXT = 154
STEP = 2


BETA_ONE = 0.9
BETA_TWO = 0.95
LEARN_RATE = 0.02
DECAY_RATE = 0.1
ADAM_EPS = 1e-08
NORM_EPS = 1e-06
GELU_COEF = 0.7978845608028654
GELU_CUBE = 0.044715
PADDED = IMAGE_TOKENS + (TXT + 15) // 16 * 16
TOKENS = IMAGE_TOKENS + TXT
STREAM_ROWS = ((0, 0, IMAGE_TOKENS), (1, IMAGE_TOKENS, PADDED))
PAIR = 2 * HEAD_FEATURES
VMEM_BYTES = 56 * 1024 * 1024
F32 = jnp.float32
BF16 = jnp.bfloat16


def narrow(values):
    return values.astype(jnp.bfloat16)


def gelu_value(inputs):
    return (
        0.5 * inputs * (1.0 + jnp.tanh(GELU_COEF * (inputs + GELU_CUBE * inputs * inputs * inputs)))
    )


def gelu_slope(inputs):
    tangent = jnp.tanh(GELU_COEF * (inputs + GELU_CUBE * inputs * inputs * inputs))
    return 0.5 * (1.0 + tangent) + 0.5 * inputs * (1.0 - tangent * tangent) * GELU_COEF * (
        1.0 + 3.0 * GELU_CUBE * inputs * inputs
    )


def adam_step(param, moments, gradient):
    first_moment = BETA_ONE * moments[0] + (1.0 - BETA_ONE) * gradient
    second_moment = BETA_TWO * moments[1] + (1.0 - BETA_TWO) * gradient * gradient
    update = (
        first_moment
        / (1.0 - BETA_ONE**STEP)
        / (jnp.sqrt(second_moment / (1.0 - BETA_TWO**STEP)) + ADAM_EPS)
    )
    return (param - LEARN_RATE * (update + DECAY_RATE * param), first_moment, second_moment)


def kernel_params():
    return pltpu.CompilerParams(vmem_limit_bytes=VMEM_BYTES)


def cost(flops, nbytes, transcendentals=0):
    return pl.CostEstimate(flops=flops, bytes_accessed=nbytes, transcendentals=transcendentals)


def whole(shape):
    return pl.BlockSpec(shape, lambda j: (0,) * len(shape))


def matmul_rows(acts, weight, epilogue, extras, extra_specs, out_types, out_specs, tile=384):
    rows, depth = acts.shape
    width = weight.shape[2]
    tile = min(tile, width)

    def kernel(acts_ref, weight_ref, *refs):
        for stream, low, high in STREAM_ROWS:
            product = jnp.dot(
                acts_ref[low:high], weight_ref[stream], preferred_element_type=F32
            )
            epilogue(product, stream, low, high, *refs)

    return pl.pallas_call(
        kernel,
        grid=(width // tile,),
        in_specs=[
            whole((rows, depth)),
            pl.BlockSpec((2, depth, tile), lambda j: (0, 0, j)),
            *extra_specs,
        ],
        out_specs=out_specs,
        out_shape=out_types,
        compiler_params=kernel_params(),
        cost_estimate=cost(
            2 * rows * depth * width, 2 * (rows * depth + 2 * depth * width + rows * width)
        ),
    )(acts, weight, *extras)


def column_spec(leading, tile=384):
    return pl.BlockSpec((leading, tile), lambda j: (0, j))


def project_triple(acts, weight, bias):
    def epilogue(product, stream, low, high, bias_ref, out_ref):
        out_ref[low:high] = (product + bias_ref[stream : stream + 1]).astype(BF16)

    rows, width = (acts.shape[0], weight.shape[2])
    return matmul_rows(
        acts,
        weight,
        epilogue,
        [bias],
        [column_spec(2)],
        jax.ShapeDtypeStruct((rows, width), BF16),
        column_spec(rows),
    )


def raise_hidden(acts, weight, bias):
    def epilogue(product, stream, low, high, bias_ref, act_ref, slope_ref):
        inputs = product + bias_ref[stream : stream + 1]
        square = inputs * inputs
        tangent = jnp.tanh(GELU_COEF * inputs * (1.0 + GELU_CUBE * square))
        act_ref[low:high] = (0.5 * inputs * (1.0 + tangent)).astype(BF16)
        slope_ref[low:high] = 0.5 * (1.0 + tangent) + 0.5 * inputs * (
            1.0 - tangent * tangent
        ) * GELU_COEF * (1.0 + 3.0 * GELU_CUBE * square)

    rows, width = (acts.shape[0], weight.shape[2])
    return matmul_rows(
        acts,
        weight,
        epilogue,
        [bias],
        [column_spec(2)],
        [jax.ShapeDtypeStruct((rows, width), BF16), jax.ShapeDtypeStruct((rows, width), F32)],
        [column_spec(rows), column_spec(rows)],
    )


def hidden_gradient(acts, weight, slope):
    def epilogue(product, stream, low, high, slope_ref, out_ref, sum_ref):
        gradient = product * slope_ref[low:high]
        out_ref[low:high] = gradient.astype(BF16)
        sum_ref[stream : stream + 1] = jnp.sum(gradient, axis=0, keepdims=True)

    rows, width = (acts.shape[0], weight.shape[2])
    return matmul_rows(
        acts,
        weight,
        epilogue,
        [slope],
        [column_spec(rows)],
        [jax.ShapeDtypeStruct((rows, width), BF16), jax.ShapeDtypeStruct((2, width), F32)],
        [column_spec(rows), column_spec(2)],
    )


def attended_gradient(acts, weight):
    def epilogue(product, stream, low, high, out_ref):
        out_ref[low:high] = product.astype(BF16)

    rows, width = (acts.shape[0], weight.shape[2])
    return matmul_rows(
        acts,
        weight,
        epilogue,
        [],
        [],
        jax.ShapeDtypeStruct((rows, width), BF16),
        column_spec(rows),
    )


def matmul_back(acts, weight, parity):
    rows, depth = acts.shape
    tile = weight.shape[1] // 4

    def kernel(acts_ref, weight_ref, out_ref):
        for stream, low, high in STREAM_ROWS:
            out_ref[low:high] = lax.dot_general(
                acts_ref[low:high],
                weight_ref[stream],
                (((1,), (1,)), ((), ())),
                preferred_element_type=F32,
            ).astype(BF16)

    return pl.pallas_call(
        kernel,
        grid=(2,),
        in_specs=[
            whole((rows, depth)),
            pl.BlockSpec((2, tile, depth), lambda j: (0, 2 * j + parity, 0)),
        ],
        out_specs=column_spec(rows, tile),
        out_shape=jax.ShapeDtypeStruct((rows, 2 * tile), BF16),
        compiler_params=kernel_params(),
        cost_estimate=cost(
            4 * rows * depth * tile, 2 * (rows * depth + 4 * depth * tile + 2 * rows * tile)
        ),
    )(acts, weight)


def weight_gradient(outer, inner, tile=384):
    rows, height = outer.shape
    width = inner.shape[1]

    def kernel(outer_ref, inner_ref, out_ref):
        for stream, low, high in STREAM_ROWS:
            out_ref[stream] = lax.dot_general(
                outer_ref[low:high],
                inner_ref[low:high],
                (((0,), (0,)), ((), ())),
                preferred_element_type=F32,
            ).astype(BF16)

    return pl.pallas_call(
        kernel,
        grid=(height // tile,),
        in_specs=[column_spec(rows, tile), whole((rows, width))],
        out_specs=pl.BlockSpec((2, tile, width), lambda j: (0, j, 0)),
        out_shape=jax.ShapeDtypeStruct((2, height, width), BF16),
        compiler_params=kernel_params(),
        cost_estimate=cost(
            2 * rows * height * width, 2 * (rows * height + rows * width + 2 * height * width)
        ),
    )(outer, inner)


def row_chunks(rows, size=256):
    return [(low, min(low + size, rows)) for low in range(0, rows, size)]


def attention(triple):
    rows, width = triple.shape
    pairs = width // (3 * PAIR)
    scale = HEAD_FEATURES ** (-0.5)

    def kernel(triple_ref, out_ref, total_ref):
        lane = lax.broadcasted_iota(jnp.int32, (1, PAIR), 1) // HEAD_FEATURES
        feature = lax.broadcasted_iota(jnp.int32, (PAIR, 1), 0) // HEAD_FEATURES
        key_index = lax.broadcasted_iota(jnp.int32, (rows, 1), 0)
        keys = triple_ref[:, PAIR : 2 * PAIR]
        values_turned = triple_ref[:, 2 * PAIR : 3 * PAIR].T
        for low, high in row_chunks(rows):
            queries = triple_ref[low:high, 0:PAIR] * jnp.asarray(scale, BF16)
            mixed = []
            for head in range(2):
                own = jnp.where(lane == head, queries, jnp.zeros_like(queries))
                scores = lax.dot_general(
                    keys, own, (((1,), (1,)), ((), ())), preferred_element_type=F32
                )
                scores = jnp.where(key_index < TOKENS, scores, -1e30)
                highest = jnp.max(scores, axis=0, keepdims=True)
                weights = jnp.exp(scores - highest)
                total = jnp.sum(weights, axis=0, keepdims=True)
                total_ref[0, head : head + 1, low:high] = highest + jnp.log(total)
                mixed.append(
                    jnp.dot(values_turned, weights.astype(BF16), preferred_element_type=F32)
                    / total
                )
            out_ref[low:high] = jnp.where(feature == 0, mixed[0], mixed[1]).T.astype(BF16)

    return pl.pallas_call(
        kernel,
        grid=(pairs,),
        in_specs=[pl.BlockSpec((rows, 3 * PAIR), lambda p: (0, p))],
        out_specs=[
            pl.BlockSpec((rows, PAIR), lambda p: (0, p)),
            pl.BlockSpec((1, 2, rows), lambda p: (p, 0, 0)),
        ],
        out_shape=[
            jax.ShapeDtypeStruct((rows, pairs * PAIR), BF16),
            jax.ShapeDtypeStruct((pairs, 2, rows), F32),
        ],
        compiler_params=kernel_params(),
        cost_estimate=cost(
            16 * pairs * PAIR * rows * rows, 8 * rows * width, 2 * pairs * rows * rows
        ),
    )(triple)


def attention_back(triple, totals, grad_mix):
    rows, width = triple.shape
    pairs = width // (3 * PAIR)
    scale = HEAD_FEATURES ** (-0.5)

    def kernel(triple_ref, total_ref, grad_ref, out_ref, sum_ref, key_acc, value_acc):
        lane = lax.broadcasted_iota(jnp.int32, (1, PAIR), 1) // HEAD_FEATURES
        feature = lax.broadcasted_iota(jnp.int32, (PAIR, 1), 0) // HEAD_FEATURES
        key_index = lax.broadcasted_iota(jnp.int32, (rows, 1), 0)
        keys = triple_ref[:, PAIR : 2 * PAIR]
        values = triple_ref[:, 2 * PAIR : 3 * PAIR]
        keys_turned = keys.T
        query_sums = [jnp.zeros((1, PAIR), F32), jnp.zeros((1, PAIR), F32)]
        for step, (low, high) in enumerate(row_chunks(rows)):
            queries = triple_ref[low:high, 0:PAIR] * jnp.asarray(scale, BF16)
            grads = grad_ref[low:high]
            turned = []
            for head in range(2):
                own = jnp.where(lane == head, queries, jnp.zeros_like(queries))
                own_grad = jnp.where(lane == head, grads, jnp.zeros_like(grads))
                scores = lax.dot_general(
                    keys, own, (((1,), (1,)), ((), ())), preferred_element_type=F32
                )
                soft = jnp.exp(scores - total_ref[0, head : head + 1, low:high])
                soft = jnp.where(key_index < TOKENS, soft, 0.0)
                grad_soft = lax.dot_general(
                    values, own_grad, (((1,), (1,)), ((), ())), preferred_element_type=F32
                )
                delta = jnp.sum(soft * grad_soft, axis=0, keepdims=True)
                score_round = (soft * (grad_soft - delta)).astype(BF16)
                turned.append(jnp.dot(keys_turned, score_round, preferred_element_type=F32))
                key_part = jnp.dot(score_round, own, preferred_element_type=F32)
                value_part = jnp.dot(soft.astype(BF16), own_grad, preferred_element_type=F32)
                if step == 0 and head == 0:
                    key_acc[...] = key_part
                    value_acc[...] = value_part
                else:
                    key_acc[...] += key_part
                    value_acc[...] += value_part
            grad_query = (jnp.where(feature == 0, turned[0], turned[1]) * scale).T
            out_ref[low:high, 0:PAIR] = grad_query.astype(BF16)
            stream = 0 if high <= IMAGE_TOKENS else 1
            query_sums[stream] += jnp.sum(grad_query, axis=0, keepdims=True)
        out_ref[:, PAIR : 2 * PAIR] = key_acc[...].astype(BF16)
        out_ref[:, 2 * PAIR : 3 * PAIR] = value_acc[...].astype(BF16)
        for stream, low, high in STREAM_ROWS:
            sum_ref[0, stream : stream + 1, 0:PAIR] = query_sums[stream]
            sum_ref[0, stream : stream + 1, PAIR : 2 * PAIR] = jnp.sum(
                value_acc[low:high], axis=0, keepdims=True
            )

    return pl.pallas_call(
        kernel,
        grid=(pairs,),
        in_specs=[
            pl.BlockSpec((rows, 3 * PAIR), lambda p: (0, p)),
            pl.BlockSpec((1, 2, rows), lambda p: (p, 0, 0)),
            pl.BlockSpec((rows, PAIR), lambda p: (0, p)),
        ],
        out_specs=[
            pl.BlockSpec((rows, 3 * PAIR), lambda p: (0, p)),
            pl.BlockSpec((1, 2, 2 * PAIR), lambda p: (p, 0, 0)),
        ],
        out_shape=[
            jax.ShapeDtypeStruct((rows, width), BF16),
            jax.ShapeDtypeStruct((pairs, 2, 2 * PAIR), F32),
        ],
        scratch_shapes=[pltpu.VMEM((rows, PAIR), F32), pltpu.VMEM((rows, PAIR), F32)],
        compiler_params=kernel_params(),
        cost_estimate=cost(
            40 * pairs * PAIR * rows * rows, 8 * rows * width, 2 * pairs * rows * rows
        ),
    )(triple, totals, grad_mix)


def per_token(table):
    row = lax.broadcasted_iota(jnp.int32, (PADDED, 1), 0)
    return jnp.where(row < IMAGE_TOKENS, table[0][None], table[1][None])


def stream_sums(values):
    return jnp.stack([jnp.sum(values[low:high], axis=0) for _, low, high in STREAM_ROWS])


def row_stats(total, square):
    center = total / D
    return (center, lax.rsqrt(square / D - center * center + NORM_EPS))


def join_tokens(image, text):
    blank = jnp.zeros((PADDED - TOKENS, image.shape[2]), image.dtype)
    return jnp.concatenate([image[0], text[0], blank], axis=0)


def make_shards(row_count, col_count):
    order = list(range(0, row_count, 2)) + list(range(row_count - 1, 0, -2))
    place = [order.index(device) for device in range(row_count)]
    ahead = [(order[i], order[(i + 1) % row_count]) for i in range(row_count)]
    behind = [(target, sender) for sender, target in ahead]
    near = [(device, device ^ 1) for device in range(col_count)]
    far = [(device, device ^ 2) for device in range(col_count)]
    share = row_count // col_count
    long_way = row_count // 2
    short_way = row_count - 1 - long_way

    def near_swap(values):
        return lax.ppermute(values, "cols", near)

    def far_swap(values):
        return lax.ppermute(values, "cols", far)

    def column_total(parts):
        parts = parts + near_swap(parts)
        return parts + far_swap(parts)

    def gather_width(values):
        away = far_swap(values)
        return jnp.concatenate([values, near_swap(values), away, near_swap(away)], axis=-1)

    def expand_rows(acts, weight):
        leaving = matmul_back(acts, weight, 1)
        arrived = near_swap(leaving)
        kept = matmul_back(acts, weight, 0)
        total = kept.astype(F32) + arrived.astype(F32)
        half = total.shape[1] // 2
        away = far_swap(narrow(total[:, half:]))
        return total[:, :half] + away.astype(F32)

    def owner(offset):
        here = jnp.asarray(place, jnp.int32)[lax.axis_index("rows")]
        return jnp.asarray(order, jnp.int32)[(here + offset) % row_count]

    def slot(offset):
        row = owner(offset)
        return (row // share ^ lax.axis_index("cols")) * share + row % share

    def ring_gather(block, forward_long):
        height = block.shape[1]
        complete = jnp.zeros((2, row_count * height, block.shape[2]), block.dtype)

        def put(state, piece, offset):
            return lax.dynamic_update_slice(state, piece, (0, slot(offset) * height, 0))

        complete = put(complete, block, 0)
        forward_hops, back_hops = (
            (long_way, short_way) if forward_long else (short_way, long_way)
        )
        forward = back = block
        for hop in range(1, long_way + 1):
            if hop <= forward_hops:
                forward = lax.ppermute(forward, "rows", ahead)
                complete = put(complete, forward, -hop)
            if hop <= back_hops:
                back = lax.ppermute(back, "rows", behind)
                complete = put(complete, back, hop)
        return complete

    def ring_scatter(partial, forward_long):
        height = partial.shape[1] // row_count

        def take(offset):
            return lax.dynamic_slice(
                partial, (0, slot(offset) * height, 0), (2, height, partial.shape[2])
            )

        forward_hops, back_hops = (
            (long_way, short_way) if forward_long else (short_way, long_way)
        )
        forward = take(forward_hops)
        back = take(-back_hops)
        for hop in range(1, long_way + 1):
            if hop <= forward_hops:
                forward = lax.ppermute(forward, "rows", ahead).astype(F32)
                forward = forward + take(forward_hops - hop).astype(F32)
                if hop < forward_hops:
                    forward = narrow(forward)
            if hop <= back_hops:
                back = lax.ppermute(back, "rows", behind)
                if hop < back_hops:
                    back = narrow(back.astype(F32) + take(hop - back_hops).astype(F32))
        return forward + back.astype(F32)

    def shards(
        x_img,
        x_txt,
        cond,
        back_img,
        back_txt,
        w_mod,
        w_qkv,
        w_proj,
        w_up,
        w_down,
        biases,
        moments_mod,
        moments_qkv,
        moments_proj,
        moments_up,
        moments_down,
        moments_bias,
    ):
        local_rows = w_qkv.shape[0]
        width = w_qkv.shape[3]
        pairs = width // PAIR

        def stream_major(weight):
            return narrow(weight).swapaxes(0, 1).reshape(2, local_rows, -1)

        qkv_local = (
            narrow(w_qkv)
            .reshape(local_rows, 2, 3, pairs, PAIR)
            .transpose(1, 0, 3, 2, 4)
            .reshape(2, local_rows, 3 * width)
        )
        triple_weight = ring_gather(qkv_local, True)
        project_weight = ring_gather(stream_major(w_proj), False)
        raise_weight = ring_gather(stream_major(w_up), True)
        lower_weight = ring_gather(stream_major(w_down), False)

        silu_cond = narrow(jax.nn.silu(cond))
        mod_round = narrow(w_mod)
        mod_parts = lax.all_to_all(
            jnp.einsum("bd,dsic->bsic", silu_cond, mod_round, preferred_element_type=F32),
            "rows",
            0,
            0,
            tiled=True,
        )
        modulation = jnp.sum(mod_parts, axis=0) + biases[:, 0:6]
        modulation_full = gather_width(modulation)
        scale_one, gate_one, scale_two, gate_two = [
            per_token(modulation[:, slot_index]) for slot_index in (1, 2, 4, 5)
        ]
        shift_two = per_token(modulation[:, 3])

        source_round = join_tokens(x_img, x_txt)
        source = source_round.astype(F32)
        source_full = gather_width(source_round).astype(F32)
        center_one, inverse_one = row_stats(
            jnp.sum(source_full, axis=1, keepdims=True),
            jnp.sum(source_full * source_full, axis=1, keepdims=True),
        )
        unit_one = (source - center_one) * inverse_one
        normed_one = narrow(
            (source_full - center_one)
            * inverse_one
            * (1.0 + per_token(modulation_full[:, 1]))
            + per_token(modulation_full[:, 0])
        )
        cotangent_round = join_tokens(back_img, back_txt)
        cotangent = cotangent_round.astype(F32)
        lowered_full = narrow(
            gather_width(cotangent_round).astype(F32) * per_token(modulation_full[:, 5])
        )

        triple_bias = (
            jnp.stack([biases[:, 6], jnp.zeros_like(biases[:, 6]), biases[:, 7]], axis=1)
            .reshape(2, 3, pairs, PAIR)
            .swapaxes(1, 2)
            .reshape(2, 3 * width)
        )
        triple = project_triple(normed_one, triple_weight, triple_bias)
        attended, log_totals = attention(triple)
        projected = expand_rows(attended, project_weight) + per_token(biases[:, 8])
        residual = source + gate_one * projected
        totals_two = column_total(
            jnp.stack([jnp.sum(residual, axis=1), jnp.sum(residual * residual, axis=1)])
        )
        center_two, inverse_two = row_stats(totals_two[0][:, None], totals_two[1][:, None])
        unit_two = (residual - center_two) * inverse_two
        normed_two = gather_width(narrow(unit_two * (1.0 + scale_two) + shift_two))
        hidden_act, hidden_slope = raise_hidden(
            normed_two, raise_weight, biases[:, 9:13].reshape(2, 4 * width)
        )
        grad_down = ring_scatter(weight_gradient(lowered_full, hidden_act), True)
        lowered = expand_rows(hidden_act, lower_weight) + per_token(biases[:, 13])
        output = narrow(residual + gate_two * lowered)
        grad_lowered = gate_two * cotangent

        hidden_round, hidden_sums = hidden_gradient(lowered_full, lower_weight, hidden_slope)
        grad_up = ring_scatter(weight_gradient(normed_two, hidden_round), False)
        grad_normed_two = expand_rows(hidden_round, raise_weight)

        def normalize_back(grad_unit, unit_rows, inverse):
            totals = column_total(
                jnp.stack([jnp.sum(grad_unit, axis=1), jnp.sum(grad_unit * unit_rows, axis=1)])
            )
            return inverse * (
                grad_unit - totals[0][:, None] / D - unit_rows * (totals[1][:, None] / D)
            )

        grad_residual = cotangent + normalize_back(
            grad_normed_two * (1.0 + scale_two), unit_two, inverse_two
        )
        grad_projected = gate_one * grad_residual
        projected_full = gather_width(narrow(grad_projected))
        grad_proj = ring_scatter(weight_gradient(projected_full, attended), True)
        grad_attended = attended_gradient(projected_full, project_weight)
        triple_round, triple_sums = attention_back(triple, log_totals, grad_attended)
        grad_qkv = ring_scatter(weight_gradient(normed_one, triple_round), False)
        grad_normed_one = expand_rows(triple_round, triple_weight)
        grad_source = grad_residual + normalize_back(
            grad_normed_one * (1.0 + scale_one), unit_one, inverse_one
        )

        head_sums = triple_sums.reshape(pairs, 2, 2, PAIR).transpose(1, 2, 0, 3)
        part = jnp.concatenate(
            [
                stream_sums(grad_normed_one)[:, None],
                stream_sums(grad_normed_one * unit_one)[:, None],
                stream_sums(grad_residual * projected)[:, None],
                stream_sums(grad_normed_two)[:, None],
                stream_sums(grad_normed_two * unit_two)[:, None],
                stream_sums(cotangent * lowered)[:, None],
                head_sums.reshape(2, 2, width),
                stream_sums(grad_projected)[:, None],
                hidden_sums.reshape(2, 4, width),
                stream_sums(grad_lowered)[:, None],
            ],
            axis=1,
        )
        part_all = lax.all_gather(part[None], "rows", axis=0, tiled=True)
        table_round = narrow(part_all[:, :, 0:6])
        grad_bias = jnp.sum(part_all, axis=0)
        grad_mod = jnp.einsum(
            "bd,bsic->dsic", silu_cond, table_round, preferred_element_type=F32
        )
        grad_silu = column_total(
            jnp.einsum("bsic,dsic->bd", table_round, mod_round, preferred_element_type=F32)
        )
        sigmoid_cond = jax.nn.sigmoid(cond)
        grad_cond = grad_silu * sigmoid_cond * (1.0 + cond * (1.0 - sigmoid_cond))
        grad_qkv = (
            grad_qkv.reshape(2, local_rows, pairs, 3, PAIR)
            .transpose(1, 0, 3, 2, 4)
            .reshape(w_qkv.shape)
        )
        grad_proj, grad_up, grad_down = [
            grad.swapaxes(0, 1).reshape(weight.shape)
            for grad, weight in ((grad_proj, w_proj), (grad_up, w_up), (grad_down, w_down))
        ]
        next_mod, first_mod, second_mod = adam_step(w_mod, moments_mod, grad_mod)
        next_qkv, first_qkv, second_qkv = adam_step(w_qkv, moments_qkv, grad_qkv)
        next_proj, first_proj, second_proj = adam_step(w_proj, moments_proj, grad_proj)
        next_up, first_up, second_up = adam_step(w_up, moments_up, grad_up)
        next_down, first_down, second_down = adam_step(w_down, moments_down, grad_down)
        next_bias, first_bias, second_bias = adam_step(biases, moments_bias, grad_bias)
        return (
            output[None, :IMAGE_TOKENS],
            output[None, IMAGE_TOKENS:TOKENS],
            grad_source[None, :IMAGE_TOKENS],
            grad_source[None, IMAGE_TOKENS:TOKENS],
            grad_cond,
            grad_mod,
            grad_qkv,
            grad_proj,
            grad_up,
            grad_down,
            grad_bias,
            next_mod,
            next_qkv,
            next_proj,
            next_up,
            next_down,
            next_bias,
            first_mod,
            second_mod,
            jnp.stack([first_qkv, second_qkv]),
            jnp.stack([first_proj, second_proj]),
            jnp.stack([first_up, second_up]),
            jnp.stack([first_down, second_down]),
            first_bias,
            second_bias,
        )

    return shards


def solution(mesh):
    in_specs = (
        P("rows", None, "cols"),
        P("rows", None, "cols"),
        P(None, "rows"),
        P("rows", None, "cols"),
        P("rows", None, "cols"),
        P("rows", None, None, "cols"),
        P("rows", None, None, "cols"),
        P("rows", None, "cols"),
        P("rows", None, None, "cols"),
        P("rows", None, None, "cols"),
        P(None, None, "cols"),
        P(None, "rows", None, None, "cols"),
        P(None, "rows", None, None, "cols"),
        P(None, "rows", None, "cols"),
        P(None, "rows", None, None, "cols"),
        P(None, "rows", None, None, "cols"),
        P(None, None, None, "cols"),
    )
    out_specs = (
        P("rows", None, "cols"),
        P("rows", None, "cols"),
        P("rows", None, "cols"),
        P("rows", None, "cols"),
        P(None, "rows"),
        P("rows", None, None, "cols"),
        P("rows", None, None, "cols"),
        P("rows", None, "cols"),
        P("rows", None, None, "cols"),
        P("rows", None, None, "cols"),
        P(None, None, "cols"),
        P("rows", None, None, "cols"),
        P("rows", None, None, "cols"),
        P("rows", None, "cols"),
        P("rows", None, None, "cols"),
        P("rows", None, None, "cols"),
        P(None, None, "cols"),
        P("rows", None, None, "cols"),
        P("rows", None, None, "cols"),
        P(None, "rows", None, None, "cols"),
        P(None, "rows", None, "cols"),
        P(None, "rows", None, None, "cols"),
        P(None, "rows", None, None, "cols"),
        P(None, None, "cols"),
        P(None, None, "cols"),
    )
    shards = make_shards(mesh.shape["rows"], mesh.shape["cols"])
    return jax.shard_map(shards, mesh=mesh, in_specs=in_specs, out_specs=out_specs, check_vma=False)
```

```python
import jax
import jax.numpy as jnp
from jax import lax
from jax.experimental import pallas as pl
from jax.experimental.pallas import tpu as pltpu
from jax.sharding import PartitionSpec as P

D = 1536
HEAD_FEATURES = 64
IMAGE_TOKENS = 1024
TXT = 154
STEP = 2


BETA_ONE = 0.9
BETA_TWO = 0.95
LEARN_RATE = 0.02
DECAY_RATE = 0.1
ADAM_EPS = 1e-08
NORM_EPS = 1e-06
GELU_COEF = 0.7978845608028654
GELU_CUBE = 0.044715
PADDED = IMAGE_TOKENS + (TXT + 15) // 16 * 16
TOKENS = IMAGE_TOKENS + TXT
STREAM_ROWS = ((0, 0, IMAGE_TOKENS), (1, IMAGE_TOKENS, PADDED))
PAIR = 2 * HEAD_FEATURES
VMEM_BYTES = 56 * 1024 * 1024
F32 = jnp.float32
BF16 = jnp.bfloat16
COST_SHARE = 1000


def narrow(values):
    return values.astype(jnp.bfloat16)


def gelu_value(inputs):
    return (
        0.5 * inputs * (1.0 + jnp.tanh(GELU_COEF * (inputs + GELU_CUBE * inputs * inputs * inputs)))
    )


def gelu_slope(inputs):
    tangent = jnp.tanh(GELU_COEF * (inputs + GELU_CUBE * inputs * inputs * inputs))
    return 0.5 * (1.0 + tangent) + 0.5 * inputs * (1.0 - tangent * tangent) * GELU_COEF * (
        1.0 + 3.0 * GELU_CUBE * inputs * inputs
    )


def adam_step(param, moments, gradient):
    first_moment = BETA_ONE * moments[0] + (1.0 - BETA_ONE) * gradient
    second_moment = BETA_TWO * moments[1] + (1.0 - BETA_TWO) * gradient * gradient
    update = (
        first_moment
        / (1.0 - BETA_ONE**STEP)
        / (jnp.sqrt(second_moment / (1.0 - BETA_TWO**STEP)) + ADAM_EPS)
    )
    return (param - LEARN_RATE * (update + DECAY_RATE * param), first_moment, second_moment)


STEP_ROWS = 48


def pieces(kind, index):
    if kind == "triple":
        return [((3 * pair + index) * PAIR, pair * PAIR, PAIR) for pair in range(3)]
    if kind == "attended":
        return [(9 * PAIR, 0, 3 * PAIR)]
    return [(index * 3 * PAIR, 0, 3 * PAIR)]


def plane(kind, stream, index):
    return (stream, index) if kind == "hidden" else (index, stream)


def row_view(kind, weight):
    if kind == "attended":
        return jnp.expand_dims(weight, -3)
    return weight if kind == "hidden" else jnp.swapaxes(weight, -3, -2)


def row_unview(kind, weight):
    if kind == "attended":
        return jnp.squeeze(weight, -3)
    return weight if kind == "hidden" else jnp.swapaxes(weight, -3, -2)


def travel_rows(kinds, weights):
    views = [row_view(kind, weight) for kind, weight in zip(kinds, weights)]
    height = views[0].shape[0]

    def kernel(*refs):
        out_ref = refs[-1]
        for kind, ref in zip(kinds, refs):
            for stream in range(2):
                for index in range(ref.shape[1 if kind != "hidden" else 2]):
                    one, two = plane(kind, stream, index)
                    for there, here, size in pieces(kind, index):
                        out_ref[stream, :, there : there + size] = ref[
                            :, one, two, here : here + size
                        ].astype(BF16)

    total = 12 * PAIR
    return pl.pallas_call(
        kernel,
        grid=(height // STEP_ROWS,),
        in_specs=[
            pl.BlockSpec((STEP_ROWS, *view.shape[1:]), lambda i: (i, 0, 0, 0)) for view in views
        ],
        out_specs=pl.BlockSpec((2, STEP_ROWS, total), lambda i: (0, i, 0)),
        out_shape=jax.ShapeDtypeStruct((2, height, total), BF16),
        compiler_params=kernel_params(),
        cost_estimate=cost(2 * height * total, 12 * height * total),
    )(*views)


def adam_rows(kind, param, moments, slot, partial, arrived):
    view, moment_view = (row_view(kind, param), row_view(kind, moments))
    height = view.shape[0]
    counts = view.shape[1:3]
    parts = height // STEP_ROWS

    def kernel(slot_ref, param_ref, moment_ref, *refs):
        grad_refs, (next_ref, grad_ref, moved_ref) = refs[:3], refs[3:]
        for stream in range(2):
            for index in range(counts[1] if kind == "hidden" else counts[0]):
                one, two = plane(kind, stream, index)
                gradient = jnp.concatenate(
                    [
                        sum(ref[stream, :, there : there + size].astype(F32) for ref in grad_refs)
                        for there, _, size in pieces(kind, index)
                    ],
                    axis=1,
                )
                result, first_moment, second_moment = adam_step(
                    param_ref[:, one, two],
                    (moment_ref[0, :, one, two], moment_ref[1, :, one, two]),
                    gradient,
                )
                next_ref[:, one, two] = result
                grad_ref[:, one, two] = gradient
                moved_ref[0, :, one, two] = first_moment
                moved_ref[1, :, one, two] = second_moment

    param_spec = pl.BlockSpec((STEP_ROWS, *counts, view.shape[3]), lambda i, slot: (i, 0, 0, 0))
    moment_spec = pl.BlockSpec(
        (2, STEP_ROWS, *counts, view.shape[3]), lambda i, slot: (0, i, 0, 0, 0)
    )
    total = partial.shape[2]
    grad_spec = pl.BlockSpec((2, STEP_ROWS, total), lambda i, slot: (0, i, 0))
    own_spec = pl.BlockSpec((2, STEP_ROWS, total), lambda i, slot: (0, slot[0] * parts + i, 0))
    next_param, grad, moved = pl.pallas_call(
        kernel,
        grid_spec=pltpu.PrefetchScalarGridSpec(
            num_scalar_prefetch=1,
            grid=(parts,),
            in_specs=[param_spec, moment_spec, own_spec, grad_spec, grad_spec],
            out_specs=[param_spec, param_spec, moment_spec],
        ),
        out_shape=[
            jax.ShapeDtypeStruct(view.shape, F32),
            jax.ShapeDtypeStruct(view.shape, F32),
            jax.ShapeDtypeStruct(moment_view.shape, F32),
        ],
        compiler_params=kernel_params(),
        cost_estimate=cost(20 * view.size, 40 * view.size),
    )(slot, view, moment_view, partial, *arrived)
    return [row_unview(kind, one) for one in (next_param, grad, moved)]


def adam_modulation(param, moments, rows, table):
    view, moment_view = (row_view("modulation", param), row_view("modulation", moments))
    height, count, streams, width = view.shape
    turned = jnp.swapaxes(table, 1, 2).reshape(table.shape[0], count * streams * width)

    def kernel(rows_ref, table_ref, param_ref, moment_ref, next_ref, grad_ref, *moved_refs):
        for index in range(count):
            for stream in range(streams):
                low = (index * streams + stream) * width
                gradient = jnp.dot(
                    rows_ref[...], table_ref[:, low : low + width], preferred_element_type=F32
                )
                result, first_moment, second_moment = adam_step(
                    param_ref[:, index, stream],
                    (moment_ref[0, :, index, stream], moment_ref[1, :, index, stream]),
                    gradient,
                )
                next_ref[:, index, stream] = result
                grad_ref[:, index, stream] = gradient
                moved_refs[0][:, index, stream] = first_moment
                moved_refs[1][:, index, stream] = second_moment

    param_spec = pl.BlockSpec((STEP_ROWS, count, streams, width), lambda i: (i, 0, 0, 0))
    moment_spec = pl.BlockSpec((2, STEP_ROWS, count, streams, width), lambda i: (0, i, 0, 0, 0))
    shape = jax.ShapeDtypeStruct(view.shape, F32)
    results = pl.pallas_call(
        kernel,
        grid=(height // STEP_ROWS,),
        in_specs=[
            pl.BlockSpec((STEP_ROWS, rows.shape[0]), lambda i: (i, 0)),
            whole(turned.shape),
            param_spec,
            moment_spec,
        ],
        out_specs=[param_spec] * 4,
        out_shape=[shape] * 4,
        compiler_params=kernel_params(),
        cost_estimate=cost(20 * view.size, 40 * view.size),
    )(rows.T, turned, view, moment_view)
    return [row_unview("modulation", one) for one in results]


def kernel_params():
    return pltpu.CompilerParams(vmem_limit_bytes=VMEM_BYTES)


def cost(flops, nbytes, transcendentals=0):
    return pl.CostEstimate(flops=flops // COST_SHARE, bytes_accessed=nbytes // COST_SHARE, transcendentals=transcendentals)


def whole(shape):
    return pl.BlockSpec(shape, lambda j: (0,) * len(shape))


def matmul_rows(acts, blocks, slots, span, epilogue, extras, extra_specs, out_types, out_specs):
    rows, depth = acts.shape
    count = len(blocks)
    height = blocks[0].shape[1]
    first, width = (span[0], span[1] - span[0])
    tile = 384
    tiles = width // tile

    def kernel(slots_ref, acts_ref, *refs):
        block_refs, refs = refs[:count], refs[count:]
        refs, weight, arrivals = refs[:-2], refs[-2], refs[-1]

        def copy(index, part):
            return pltpu.make_async_copy(
                block_refs[index].at[:, :, pl.ds(first + part * tile, tile)],
                weight.at[
                    part, :, pl.ds(pl.multiple_of(slots_ref[index] * height, height), height), :
                ],
                arrivals.at[part, index],
            )

        step = pl.program_id(0)

        @pl.when(step == 0)
        def _():
            for part in range(tiles):
                for index in range(count):
                    copy(index, part).start()

        for part in range(tiles):

            @pl.when(step == part)
            def _():
                for index in range(count):
                    copy(index, part).wait()

        for stream, low, high in STREAM_ROWS:
            product = jnp.dot(
                acts_ref[low:high], weight[step, stream], preferred_element_type=F32
            )
            epilogue(product, stream, low, high, *refs)

    return pl.pallas_call(
        kernel,
        grid=(tiles,),
        in_specs=[
            pl.BlockSpec(memory_space=pltpu.SMEM),
            whole((rows, depth)),
            *[pl.BlockSpec(memory_space=pl.ANY)] * count,
            *extra_specs,
        ],
        out_specs=out_specs,
        out_shape=out_types,
        scratch_shapes=[
            pltpu.VMEM((tiles, 2, depth, tile), BF16),
            pltpu.SemaphoreType.DMA((tiles, count)),
        ],
        compiler_params=kernel_params(),
        cost_estimate=cost(
            2 * rows * depth * width, 2 * (rows * depth + 2 * depth * width + rows * width)
        ),
    )(slots, acts, *blocks, *extras)


def column_spec(leading, tile=384):
    return pl.BlockSpec((leading, tile), lambda j: (0, j))


def project_triple(acts, blocks, slots, span, bias):
    def epilogue(product, stream, low, high, bias_ref, out_ref):
        out_ref[low:high] = (product + bias_ref[stream : stream + 1]).astype(BF16)

    rows, width = (acts.shape[0], span[1] - span[0])
    return matmul_rows(
        acts,
        blocks,
        slots,
        span,
        epilogue,
        [bias],
        [column_spec(2)],
        jax.ShapeDtypeStruct((rows, width), BF16),
        column_spec(rows),
    )


def raise_hidden(acts, blocks, slots, span, bias):
    def epilogue(product, stream, low, high, bias_ref, act_ref, slope_ref):
        inputs = product + bias_ref[stream : stream + 1]
        square = inputs * inputs
        tangent = jnp.tanh(GELU_COEF * inputs * (1.0 + GELU_CUBE * square))
        act_ref[low:high] = (0.5 * inputs * (1.0 + tangent)).astype(BF16)
        slope_ref[low:high] = 0.5 * (1.0 + tangent) + 0.5 * inputs * (
            1.0 - tangent * tangent
        ) * GELU_COEF * (1.0 + 3.0 * GELU_CUBE * square)

    rows, width = (acts.shape[0], span[1] - span[0])
    return matmul_rows(
        acts,
        blocks,
        slots,
        span,
        epilogue,
        [bias],
        [column_spec(2)],
        [jax.ShapeDtypeStruct((rows, width), BF16), jax.ShapeDtypeStruct((rows, width), F32)],
        [column_spec(rows), column_spec(rows)],
    )


def hidden_gradient(acts, blocks, slots, span, slope):
    def epilogue(product, stream, low, high, slope_ref, out_ref, sum_ref):
        gradient = product * slope_ref[low:high]
        out_ref[low:high] = gradient.astype(BF16)
        sum_ref[stream : stream + 1] = jnp.sum(gradient, axis=0, keepdims=True)

    rows, width = (acts.shape[0], span[1] - span[0])
    return matmul_rows(
        acts,
        blocks,
        slots,
        span,
        epilogue,
        [slope],
        [column_spec(rows)],
        [jax.ShapeDtypeStruct((rows, width), BF16), jax.ShapeDtypeStruct((2, width), F32)],
        [column_spec(rows), column_spec(2)],
    )


def attended_gradient(acts, blocks, slots, span):
    def epilogue(product, stream, low, high, out_ref):
        out_ref[low:high] = product.astype(BF16)

    rows, width = (acts.shape[0], span[1] - span[0])
    return matmul_rows(
        acts,
        blocks,
        slots,
        span,
        epilogue,
        [],
        [],
        jax.ShapeDtypeStruct((rows, width), BF16),
        column_spec(rows),
    )


def matmul_back(acts, blocks, slots, span, parity):
    rows, depth = acts.shape
    count = len(blocks)
    height = blocks[0].shape[1]
    share = count // 4
    tile = share * height

    def kernel(slots_ref, acts_ref, *refs):
        block_refs, (*out_refs, weight, arrivals) = refs[:count], refs[count:]

        def copy(index):
            slot = slots_ref[index]
            row = pl.multiple_of(slot % share * height, height)
            return pltpu.make_async_copy(
                block_refs[index].at[:, :, pl.ds(span[0], depth)],
                weight.at[slot // share // 2, :, pl.ds(row, height), :],
                arrivals.at[index],
            )

        def each(action, wanted):
            for index in range(count):
                pl.when(wanted(slots_ref[index] // share))(lambda index=index: action(copy(index)))

        step = pl.program_id(0)

        @pl.when(step == 0)
        def _():
            for part in range(2):
                each(lambda job: job.start(), lambda group: group == 2 * part + parity)

        each(lambda job: job.wait(), lambda group: group == 2 * step + parity)
        for part, out_ref in enumerate(out_refs):

            @pl.when(step == part)
            def _():
                for stream, low, high in STREAM_ROWS:
                    out_ref[low:high] = lax.dot_general(
                        acts_ref[low:high],
                        weight[part, stream],
                        (((1,), (1,)), ((), ())),
                        preferred_element_type=F32,
                    ).astype(BF16)

    return pl.pallas_call(
        kernel,
        grid=(2,),
        in_specs=[
            pl.BlockSpec(memory_space=pltpu.SMEM),
            whole((rows, depth)),
            *[pl.BlockSpec(memory_space=pl.ANY)] * count,
        ],
        out_specs=[whole((rows, tile))] * 2,
        out_shape=[jax.ShapeDtypeStruct((rows, tile), BF16)] * 2,
        scratch_shapes=[
            pltpu.VMEM((2, 2, tile, depth), BF16),
            pltpu.SemaphoreType.DMA((count,)),
        ],
        compiler_params=kernel_params(),
        cost_estimate=cost(
            4 * rows * depth * tile, 2 * (rows * depth + 4 * depth * tile + 2 * rows * tile)
        ),
    )(slots, acts, *blocks)


def weight_gradient(outer, inner, full_width, first=0, *so_far, tile=384):
    rows, height = outer.shape
    width = inner.shape[1]

    def kernel(outer_ref, inner_ref, *refs):
        out_ref = refs[-1]
        for stream, low, high in STREAM_ROWS:
            out_ref[stream] = lax.dot_general(
                outer_ref[low:high],
                inner_ref[low:high],
                (((0,), (0,)), ((), ())),
                preferred_element_type=F32,
            ).astype(BF16)

    return pl.pallas_call(
        kernel,
        grid=(height // tile,),
        in_specs=[
            column_spec(rows, tile),
            whole((rows, width)),
            *[pl.BlockSpec(memory_space=pl.ANY)] * len(so_far),
        ],
        out_specs=pl.BlockSpec((2, tile, width), lambda j: (0, j, first // width)),
        out_shape=jax.ShapeDtypeStruct((2, height, full_width), BF16),
        input_output_aliases={2 + index: index for index in range(len(so_far))},
        compiler_params=kernel_params(),
        cost_estimate=cost(
            2 * rows * height * width, 2 * (rows * height + rows * width + 2 * height * width)
        ),
    )(outer, inner, *so_far)


def row_chunks(rows, size=256):
    return [(low, min(low + size, rows)) for low in range(0, rows, size)]


def attention(triple, first, last, *so_far):
    rows, width = triple.shape
    pairs = width // (3 * PAIR)
    scale = HEAD_FEATURES ** (-0.5)

    def kernel(triple_ref, *refs):
        out_ref, total_ref = refs[-2:]
        lane = lax.broadcasted_iota(jnp.int32, (1, PAIR), 1) // HEAD_FEATURES
        feature = lax.broadcasted_iota(jnp.int32, (PAIR, 1), 0) // HEAD_FEATURES
        key_index = lax.broadcasted_iota(jnp.int32, (rows, 1), 0)
        keys = triple_ref[:, PAIR : 2 * PAIR]
        values_turned = triple_ref[:, 2 * PAIR : 3 * PAIR].T
        for low, high in row_chunks(rows):
            queries = triple_ref[low:high, 0:PAIR] * jnp.asarray(scale, BF16)
            mixed = []
            for head in range(2):
                own = jnp.where(lane == head, queries, jnp.zeros_like(queries))
                scores = lax.dot_general(
                    keys, own, (((1,), (1,)), ((), ())), preferred_element_type=F32
                )
                scores = jnp.where(key_index < TOKENS, scores, -1e30)
                highest = jnp.max(scores, axis=0, keepdims=True)
                weights = jnp.exp(scores - highest)
                total = jnp.sum(weights, axis=0, keepdims=True)
                total_ref[0, head : head + 1, low:high] = highest + jnp.log(total)
                mixed.append(
                    jnp.dot(values_turned, weights.astype(BF16), preferred_element_type=F32)
                    / total
                )
            out_ref[low:high] = jnp.where(feature == 0, mixed[0], mixed[1]).T.astype(BF16)

    return pl.pallas_call(
        kernel,
        grid=(last - first,),
        in_specs=[
            pl.BlockSpec((rows, 3 * PAIR), lambda p: (0, p + first)),
            *[pl.BlockSpec(memory_space=pl.ANY)] * len(so_far),
        ],
        input_output_aliases={1 + index: index for index in range(len(so_far))},
        out_specs=[
            pl.BlockSpec((rows, PAIR), lambda p: (0, p + first)),
            pl.BlockSpec((1, 2, rows), lambda p: (p + first, 0, 0)),
        ],
        out_shape=[
            jax.ShapeDtypeStruct((rows, pairs * PAIR), BF16),
            jax.ShapeDtypeStruct((pairs, 2, rows), F32),
        ],
        compiler_params=kernel_params(),
        cost_estimate=cost(
            16 * pairs * PAIR * rows * rows, 8 * rows * width, 2 * pairs * rows * rows
        ),
    )(triple, *so_far)


def attention_back(triple, totals, grad_mix, first, last, *so_far):
    rows, width = triple.shape
    pairs = width // (3 * PAIR)
    scale = HEAD_FEATURES ** (-0.5)

    def kernel(triple_ref, total_ref, grad_ref, *refs):
        out_ref, sum_ref, key_acc, value_acc = refs[-4:]
        lane = lax.broadcasted_iota(jnp.int32, (1, PAIR), 1) // HEAD_FEATURES
        feature = lax.broadcasted_iota(jnp.int32, (PAIR, 1), 0) // HEAD_FEATURES
        key_index = lax.broadcasted_iota(jnp.int32, (rows, 1), 0)
        keys = triple_ref[:, PAIR : 2 * PAIR]
        values = triple_ref[:, 2 * PAIR : 3 * PAIR]
        keys_turned = keys.T
        query_sums = [jnp.zeros((1, PAIR), F32), jnp.zeros((1, PAIR), F32)]
        for step, (low, high) in enumerate(row_chunks(rows)):
            queries = triple_ref[low:high, 0:PAIR] * jnp.asarray(scale, BF16)
            grads = grad_ref[low:high]
            turned = []
            for head in range(2):
                own = jnp.where(lane == head, queries, jnp.zeros_like(queries))
                own_grad = jnp.where(lane == head, grads, jnp.zeros_like(grads))
                scores = lax.dot_general(
                    keys, own, (((1,), (1,)), ((), ())), preferred_element_type=F32
                )
                soft = jnp.exp(scores - total_ref[0, head : head + 1, low:high])
                soft = jnp.where(key_index < TOKENS, soft, 0.0)
                grad_soft = lax.dot_general(
                    values, own_grad, (((1,), (1,)), ((), ())), preferred_element_type=F32
                )
                delta = jnp.sum(soft * grad_soft, axis=0, keepdims=True)
                score_round = (soft * (grad_soft - delta)).astype(BF16)
                turned.append(jnp.dot(keys_turned, score_round, preferred_element_type=F32))
                key_part = jnp.dot(score_round, own, preferred_element_type=F32)
                value_part = jnp.dot(soft.astype(BF16), own_grad, preferred_element_type=F32)
                if step == 0 and head == 0:
                    key_acc[...] = key_part
                    value_acc[...] = value_part
                else:
                    key_acc[...] += key_part
                    value_acc[...] += value_part
            grad_query = (jnp.where(feature == 0, turned[0], turned[1]) * scale).T
            out_ref[low:high, 0:PAIR] = grad_query.astype(BF16)
            stream = 0 if high <= IMAGE_TOKENS else 1
            query_sums[stream] += jnp.sum(grad_query, axis=0, keepdims=True)
        out_ref[:, PAIR : 2 * PAIR] = key_acc[...].astype(BF16)
        out_ref[:, 2 * PAIR : 3 * PAIR] = value_acc[...].astype(BF16)
        for stream, low, high in STREAM_ROWS:
            sum_ref[0, stream : stream + 1, 0:PAIR] = query_sums[stream]
            sum_ref[0, stream : stream + 1, PAIR : 2 * PAIR] = jnp.sum(
                value_acc[low:high], axis=0, keepdims=True
            )

    return pl.pallas_call(
        kernel,
        grid=(last - first,),
        in_specs=[
            pl.BlockSpec((rows, 3 * PAIR), lambda p: (0, p + first)),
            pl.BlockSpec((1, 2, rows), lambda p: (p + first, 0, 0)),
            pl.BlockSpec((rows, PAIR), lambda p: (0, p + first)),
            *[pl.BlockSpec(memory_space=pl.ANY)] * len(so_far),
        ],
        input_output_aliases={3 + index: index for index in range(len(so_far))},
        out_specs=[
            pl.BlockSpec((rows, 3 * PAIR), lambda p: (0, p + first)),
            pl.BlockSpec((1, 2, 2 * PAIR), lambda p: (p + first, 0, 0)),
        ],
        out_shape=[
            jax.ShapeDtypeStruct((rows, width), BF16),
            jax.ShapeDtypeStruct((pairs, 2, 2 * PAIR), F32),
        ],
        scratch_shapes=[pltpu.VMEM((rows, PAIR), F32), pltpu.VMEM((rows, PAIR), F32)],
        compiler_params=kernel_params(),
        cost_estimate=cost(
            40 * pairs * PAIR * rows * rows, 8 * rows * width, 2 * pairs * rows * rows
        ),
    )(triple, totals, grad_mix, *so_far)


def per_token(table):
    row = lax.broadcasted_iota(jnp.int32, (PADDED, 1), 0)
    return jnp.where(row < IMAGE_TOKENS, table[0][None], table[1][None])


def stream_sums(values):
    return jnp.stack([jnp.sum(values[low:high], axis=0) for _, low, high in STREAM_ROWS])


def row_stats(total, square):
    center = total / D
    return (center, lax.rsqrt(square / D - center * center + NORM_EPS))


def join_tokens(image, text):
    blank = jnp.zeros((PADDED - TOKENS, image.shape[2]), image.dtype)
    return jnp.concatenate([image[0], text[0], blank], axis=0)


def add_halves(kept, arrived):
    own, other = [one.astype(F32) + two.astype(F32) for one, two in zip(kept, arrived)]
    return (own, narrow(other))


def make_shards(row_count, col_count):
    order = list(range(0, row_count, 2)) + list(range(row_count - 1, 0, -2))
    place = [order.index(device) for device in range(row_count)]
    ahead = [(order[i], order[(i + 1) % row_count]) for i in range(row_count)]
    behind = [(target, sender) for sender, target in ahead]
    near = [(device, device ^ 1) for device in range(col_count)]
    far = [(device, device ^ 2) for device in range(col_count)]
    across = [(device, device ^ 3) for device in range(col_count)]
    share = row_count // col_count
    long_way = row_count // 2
    short_way = row_count - 1 - long_way

    slots = [
        [
            [
                (row // share ^ col) * share + row % share
                for row in (order[(place[here] + offset) % row_count] for offset in range(row_count))
            ]
            for col in range(col_count)
        ]
        for here in range(row_count)
    ]

    class Order:
        def __init__(self):
            self.last = []

        def tie(self, *values):
            if self.last:
                values, _ = lax.optimization_barrier((values, tuple(self.last)))
            return values

        def mark(self, *values):
            self.last = list(values)

        def add(self, *values):
            self.last += values

        def run(self, step, *values):
            result = step(*self.tie(*values))
            self.mark(*jax.tree.leaves(result))
            return result

    class Swap:
        def __init__(self, steps, value, pairs):
            (value,) = steps.tie(value)
            self.steps = steps
            self.value = lax.ppermute(value, "cols", pairs)

        def land(self):
            (self.value,) = self.steps.tie(self.value)
            self.steps.mark(self.value)
            return self.value

    def shift_pairs(offset):
        return [(row, (row + offset) % row_count) for row in range(row_count)]

    def rotate(values, start):
        return lax.dynamic_slice_in_dim(
            jnp.concatenate([values, values]), start, values.shape[0], 0
        )

    class Ring:
        def __init__(self, order_of_steps, slot_row, hops):
            self.steps = order_of_steps
            self.slot_row = slot_row
            self.hops = dict(zip((1, -1), hops))
            self.done = {1: 0, -1: 0}
            self.held = {}

        def send(self, ways=(1, -1)):
            for way in ways:
                if self.done[way] < self.hops[way]:
                    (value,) = self.steps.tie(self.held[way])
                    pairs = ahead if way == 1 else behind
                    self.held[way] = lax.ppermute(value, "rows", pairs)

        def land(self, ways=(1, -1)):
            here = [way for way in ways if self.done[way] < self.hops[way]]
            if not here:
                return
            values = self.steps.tie(*[self.held[way] for way in here])
            self.steps.mark(*values)
            for way, value in zip(here, values):
                self.held[way] = value
                self.done[way] += 1
                self.take(way)

        def left(self):
            return max(self.hops[way] - self.done[way] for way in (1, -1))

        def step(self, ways=(1, -1)):
            self.land(ways)
            self.send(ways)

        def finish(self):
            while self.left():
                self.step()

        def slot(self, offset):
            return self.slot_row[offset % row_count]

    class Lanes:
        def __init__(self):
            self.queue = {1: [], -1: []}
            self.flying = {}

        def push(self, ring, ahead_of=None):
            for way in (1, -1):
                queue = self.queue[way]
                place_at = queue.index(ahead_of) if ahead_of in queue else len(queue)
                queue[place_at:place_at] = [ring] * ring.hops[way]

        def tick(self):
            landed = list(self.flying.items())
            if landed:
                steps = landed[0][1].steps
                values = steps.tie(*[ring.held[way] for way, ring in landed])
                steps.mark(*values)
                for (way, ring), value in zip(landed, values):
                    ring.held[way] = value
                    ring.done[way] += 1
                for way, ring in landed:
                    ring.take(way)
            self.flying = {}
            for way in (1, -1):
                if self.queue[way]:
                    self.flying[way] = self.queue[way].pop(0)
                    self.flying[way].send((way,))

        def until(self, ring, left=0):
            while ring.left() > left:
                self.tick()

    class RingGather(Ring):
        def __init__(self, order_of_steps, slot_row, block, hops):
            super().__init__(order_of_steps, slot_row, hops)
            self.blocks = [block] * row_count
            self.held = {1: block, -1: block}

        def take(self, way):
            self.blocks[-way * self.done[way] % row_count] = self.held[way]

    class RingScatter(Ring):
        def __init__(self, order_of_steps, slot_row, partial, hops):
            super().__init__(order_of_steps, slot_row, hops)
            self.partial = partial
            self.height = partial.shape[1] // row_count
            self.held = {way: self.part(way * self.hops[way]) for way in (1, -1)}

        def part(self, offset):
            return lax.dynamic_slice(
                self.partial,
                (0, self.slot(offset) * self.height, 0),
                (2, self.height, self.partial.shape[2]),
            )

        def take(self, way):
            left = self.hops[way] - self.done[way]
            if left:
                self.held[way] = narrow(
                    self.held[way].astype(F32) + self.part(way * left).astype(F32)
                )
                self.steps.add(self.held[way])

    def shards(
        x_img,
        x_txt,
        cond,
        back_img,
        back_txt,
        w_mod,
        w_qkv,
        w_proj,
        w_up,
        w_down,
        biases,
        moments_mod,
        moments_qkv,
        moments_proj,
        moments_up,
        moments_down,
        moments_bias,
    ):
        local_rows = w_qkv.shape[0]
        width = w_qkv.shape[3]
        pairs = width // PAIR
        slot_row = lax.dynamic_slice(
            jnp.asarray(slots, jnp.int32),
            (lax.axis_index("rows"), lax.axis_index("cols"), 0),
            (1, 1, row_count),
        )[0, 0]
        slot_list = [slot_row[offset] for offset in range(row_count)]
        steps = Order()
        more_ahead, more_behind = ((long_way, short_way), (short_way, long_way))

        def gather(block, hops):
            return RingGather(steps, slot_list, block, hops)

        def scatter(partial, hops):
            return RingScatter(steps, slot_list, partial, hops)

        def update(kind, ring, param, moments):
            return steps.run(
                lambda *values: adam_rows(
                    kind, *values[:2], ring.slot(0).reshape(1), values[2], values[3:]
                ),
                param,
                moments,
                ring.partial,
                ring.held[1],
                ring.held[-1],
            )

        def far_swap(value):
            return Swap(steps, value, far)

        def near_swap(value):
            return Swap(steps, value, near)

        def send_around(value):
            return [value] + [Swap(steps, value, pairs) for pairs in (near, far, across)]

        def land_around(parts):
            return [parts[0]] + [part.land() for part in parts[1:]]

        def total_around(parts):
            one, two, three, four = land_around(parts)
            return (one + two) + (three + four)

        triple_span, attended_span, hidden_span = (
            (0, 3 * width),
            (3 * width, 4 * width),
            (0, 4 * width),
        )

        def run(step, acts, ring, span, *rest):
            return steps.run(
                lambda acts, *rest: step(acts, ring.blocks, slot_row, span, *rest), acts, *rest
            )

        def weight_part(outer, inner, *rest):
            return steps.run(
                lambda a, b, *so_far: weight_gradient(a, b, 4 * width, *rest[:1], *so_far),
                outer,
                inner,
                *rest[1:],
            )

        def send_halves(acts, ring, span, between=lambda: None):
            leaving = run(lambda *args: matmul_back(*args, 1), acts, ring, span)
            between()
            arriving = [near_swap(half) for half in leaving]
            return run(lambda *args: matmul_back(*args, 0), acts, ring, span), arriving

        def send_away(kept, arriving):
            own, other = steps.run(add_halves, kept, [half.land() for half in arriving])
            return own, far_swap(other)

        def start_width(value):
            return (value, far_swap(value), near_swap(value))

        def middle_width(parts):
            return (*parts, near_swap(parts[1].land()))

        def end_width(parts):
            value, away, beside, diagonal = parts
            diagonal.land()
            beside.land()
            return jnp.concatenate(
                [value, beside.value, away.value, diagonal.value], axis=-1
            )

        lanes = Lanes()

        def queued(ring, ahead_of=None):
            lanes.push(ring, ahead_of)
            return ring

        source_round = steps.run(join_tokens, x_img, x_txt)
        source_parts = start_width(source_round)
        silu_cond = narrow(jax.nn.silu(cond))
        mod_round = narrow(w_mod)
        (mod_terms,) = steps.tie(
            jnp.einsum("bd,dsic->bsic", silu_cond, mod_round, preferred_element_type=F32)
        )
        mod_parts = lax.all_to_all(mod_terms, "rows", 0, 0, tiled=True)
        first_local = travel_rows(("triple", "attended"), (w_qkv, w_proj))
        steps.mark(mod_parts, first_local)
        ring_first = queued(gather(first_local, more_ahead))
        lanes.tick()
        modulation = jnp.sum(mod_parts, axis=0) + biases[:, 0:6]
        mod_around = send_around(modulation)
        ring_up = queued(
            gather(steps.run(lambda w: travel_rows(("hidden",), (w,)), w_up), more_behind)
        )
        cotangent_round = steps.run(join_tokens, back_img, back_txt)
        lanes.tick()
        modulation_full = jnp.concatenate(land_around(mod_around), axis=-1)
        source_parts = middle_width(source_parts)
        cotangent_parts = start_width(cotangent_round)
        source_full = end_width(source_parts).astype(F32)
        scale_one, gate_one, scale_two, gate_two = [
            per_token(modulation[:, slot_index]) for slot_index in (1, 2, 4, 5)
        ]
        shift_two = per_token(modulation[:, 3])
        source = source_round.astype(F32)
        cotangent = cotangent_round.astype(F32)

        def first_norm(full, full_modulation):
            center, inverse = row_stats(
                jnp.sum(full, axis=1, keepdims=True),
                jnp.sum(full * full, axis=1, keepdims=True),
            )
            normed = narrow(
                (full - center) * inverse * (1.0 + per_token(full_modulation[:, 1]))
                + per_token(full_modulation[:, 0])
            )
            return center, inverse, normed

        center_one, inverse_one, normed_one = steps.run(first_norm, source_full, modulation_full)
        unit_one = (source - center_one) * inverse_one
        ring_down = queued(
            gather(steps.run(lambda w: travel_rows(("hidden",), (w,)), w_down), more_ahead)
        )
        lanes.tick()
        cotangent_parts = middle_width(cotangent_parts)
        lanes.until(ring_first)
        cotangent_full = end_width(cotangent_parts)
        triple_bias = (
            jnp.stack([biases[:, 6], jnp.zeros_like(biases[:, 6]), biases[:, 7]], axis=1)
            .reshape(2, 3, pairs, PAIR)
            .swapaxes(1, 2)
            .reshape(2, 3 * width)
        )
        triple = run(project_triple, normed_one, ring_first, triple_span, triple_bias)
        so_far = ()
        for pair in range(pairs):
            so_far = steps.run(
                lambda t, *rest, pair=pair: attention(t, pair, pair + 1, *rest), triple, *so_far
            )
            if pair == 0:
                lanes.tick()
        attended, log_totals = so_far
        halves = send_halves(attended, ring_first, attended_span)
        lanes.tick()
        own, away = send_away(*halves)
        lanes.tick()

        def residual_terms(own, away, source):
            projected = own + away.astype(F32) + per_token(biases[:, 8])
            residual = source + gate_one * projected
            sums = jnp.stack([jnp.sum(residual, axis=1), jnp.sum(residual * residual, axis=1)])
            return projected, residual, sums

        projected, residual, sums = steps.run(residual_terms, own, away.land(), source)
        sums_around = send_around(sums)
        lanes.tick()
        totals_two = total_around(sums_around)
        center_two, inverse_two = row_stats(totals_two[0][:, None], totals_two[1][:, None])
        unit_two = (residual - center_two) * inverse_two
        normed_own = narrow(unit_two * (1.0 + scale_two) + shift_two)
        steps.mark(normed_own)
        normed_parts = start_width(normed_own)
        lanes.tick()
        lanes.until(ring_up)
        lowered_full = steps.run(
            lambda full, gate: narrow(full.astype(F32) * per_token(gate)),
            cotangent_full,
            modulation_full[:, 5],
        )
        normed_two = end_width(middle_width(normed_parts))
        hidden_act, hidden_slope = run(
            raise_hidden, normed_two, ring_up, hidden_span, biases[:, 9:13].reshape(2, 4 * width)
        )
        lanes.tick()
        ring_grad_down = queued(
            scatter(weight_part(lowered_full, hidden_act), more_behind)
        )
        lanes.until(ring_down)
        hidden_round, hidden_sums = run(
            hidden_gradient, lowered_full, ring_down, hidden_span, hidden_slope
        )
        halves = send_halves(hidden_round, ring_up, hidden_span, lanes.tick)
        own, away = send_away(*halves)
        lanes.tick()
        ring_grad_up = queued(
            scatter(weight_part(normed_two, hidden_round), more_ahead)
        )

        def back_sums(grad_unit, unit_rows):
            return jnp.stack([jnp.sum(grad_unit, axis=1), jnp.sum(grad_unit * unit_rows, axis=1)])

        def normalize_back(grad_unit, unit_rows, inverse, totals):
            return inverse * (
                grad_unit - totals[0][:, None] / D - unit_rows * (totals[1][:, None] / D)
            )

        grad_normed_two = own + away.land().astype(F32)
        grad_unit_two = grad_normed_two * (1.0 + scale_two)
        sums = back_sums(grad_unit_two, unit_two)
        steps.mark(sums)
        sums_around = send_around(sums)
        lanes.tick()
        totals = total_around(sums_around)
        grad_residual = cotangent + normalize_back(grad_unit_two, unit_two, inverse_two, totals)
        grad_projected = gate_one * grad_residual
        projected_own = narrow(grad_projected)
        steps.mark(projected_own)
        projected_parts = start_width(projected_own)
        lowered_leaving = run(
            lambda *args: matmul_back(*args, 1), hidden_act, ring_down, hidden_span
        )
        lowered_kept = run(
            lambda *args: matmul_back(*args, 0), hidden_act, ring_down, hidden_span
        )
        arriving = [near_swap(half) for half in lowered_leaving]
        lanes.tick()
        projected_full = end_width(middle_width(projected_parts))
        grad_attended = run(attended_gradient, projected_full, ring_first, attended_span)
        partial_first = weight_part(projected_full, attended, 3 * width)
        own_lowered, away_lowered = send_away(lowered_kept, arriving)
        lanes.tick()
        so_far = ()
        for pair in range(pairs):
            so_far = steps.run(
                lambda t, l, g, *rest, pair=pair: attention_back(t, l, g, pair, pair + 1, *rest),
                triple,
                log_totals,
                grad_attended,
                *so_far,
            )
            if pair == pairs - 2:
                lanes.tick()
        triple_round, triple_sums = so_far
        partial_first = weight_part(normed_one, triple_round, 0, partial_first)
        ring_grad_first = queued(scatter(partial_first, more_behind))
        lanes.tick()
        halves = send_halves(triple_round, ring_first, triple_span)
        own, away = send_away(*halves)
        lowered = own_lowered + away_lowered.land().astype(F32) + per_token(biases[:, 13])
        output = narrow(residual + gate_two * lowered)
        grad_lowered = gate_two * cotangent
        steps.add(output)
        next_down, grad_down, moved_down = update(
            "hidden", ring_grad_down, w_down, moments_down
        )
        lanes.tick()
        grad_normed_one = own + away.land().astype(F32)
        grad_unit_one = grad_normed_one * (1.0 + scale_one)
        sums = back_sums(grad_unit_one, unit_one)
        steps.mark(sums)
        sums_around = send_around(sums)
        head_sums = triple_sums.reshape(pairs, 2, 2, PAIR).transpose(1, 2, 0, 3)
        part = jnp.concatenate(
            [
                stream_sums(grad_normed_one)[:, None],
                stream_sums(grad_normed_one * unit_one)[:, None],
                stream_sums(grad_residual * projected)[:, None],
                stream_sums(grad_normed_two)[:, None],
                stream_sums(grad_normed_two * unit_two)[:, None],
                stream_sums(cotangent * lowered)[:, None],
                head_sums.reshape(2, 2, width),
                stream_sums(grad_projected)[:, None],
                hidden_sums.reshape(2, 4, width),
                stream_sums(grad_lowered)[:, None],
            ],
            axis=1,
        )
        steps.mark(part)
        lanes.tick()
        (part,) = steps.tie(part)
        part_all = lax.all_to_all(
            jnp.broadcast_to(part[None], (row_count,) + part.shape), "rows", 0, 0, tiled=True
        )
        steps.mark(part_all)
        totals = total_around(sums_around)
        grad_source = grad_residual + normalize_back(grad_unit_one, unit_one, inverse_one, totals)
        steps.add(grad_source)
        table_round = narrow(part_all[:, :, 0:6])
        grad_bias = jnp.sum(part_all, axis=0)
        silu_terms = jnp.einsum("bsic,dsic->bd", table_round, mod_round, preferred_element_type=F32)
        steps.mark(silu_terms)
        silu_around = send_around(silu_terms)
        lanes.until(ring_grad_up)
        next_up, grad_up, moved_up = update("hidden", ring_grad_up, w_up, moments_up)
        lanes.until(ring_grad_first, 1)
        grad_silu = total_around(silu_around)
        sigmoid_cond = jax.nn.sigmoid(cond)
        grad_cond = grad_silu * sigmoid_cond * (1.0 + cond * (1.0 - sigmoid_cond))
        next_mod, grad_mod, first_mod, second_mod = steps.run(
            adam_modulation, w_mod, moments_mod, silu_cond, table_round
        )
        next_bias, first_bias, second_bias = adam_step(biases, moments_bias, grad_bias)
        steps.add(next_bias, first_bias, second_bias, grad_cond)
        lanes.until(ring_grad_first)
        next_qkv, grad_qkv, moved_qkv = update("triple", ring_grad_first, w_qkv, moments_qkv)
        next_proj, grad_proj, moved_proj = update(
            "attended", ring_grad_first, w_proj, moments_proj
        )
        return (
            output[None, :IMAGE_TOKENS],
            output[None, IMAGE_TOKENS:TOKENS],
            grad_source[None, :IMAGE_TOKENS],
            grad_source[None, IMAGE_TOKENS:TOKENS],
            grad_cond,
            grad_mod,
            grad_qkv,
            grad_proj,
            grad_up,
            grad_down,
            grad_bias,
            next_mod,
            next_qkv,
            next_proj,
            next_up,
            next_down,
            next_bias,
            first_mod,
            second_mod,
            moved_qkv,
            moved_proj,
            moved_up,
            moved_down,
            first_bias,
            second_bias,
        )

    return shards


def solution(mesh):
    in_specs = (
        P("rows", None, "cols"),
        P("rows", None, "cols"),
        P(None, "rows"),
        P("rows", None, "cols"),
        P("rows", None, "cols"),
        P("rows", None, None, "cols"),
        P("rows", None, None, "cols"),
        P("rows", None, "cols"),
        P("rows", None, None, "cols"),
        P("rows", None, None, "cols"),
        P(None, None, "cols"),
        P(None, "rows", None, None, "cols"),
        P(None, "rows", None, None, "cols"),
        P(None, "rows", None, "cols"),
        P(None, "rows", None, None, "cols"),
        P(None, "rows", None, None, "cols"),
        P(None, None, None, "cols"),
    )
    out_specs = (
        P("rows", None, "cols"),
        P("rows", None, "cols"),
        P("rows", None, "cols"),
        P("rows", None, "cols"),
        P(None, "rows"),
        P("rows", None, None, "cols"),
        P("rows", None, None, "cols"),
        P("rows", None, "cols"),
        P("rows", None, None, "cols"),
        P("rows", None, None, "cols"),
        P(None, None, "cols"),
        P("rows", None, None, "cols"),
        P("rows", None, None, "cols"),
        P("rows", None, "cols"),
        P("rows", None, None, "cols"),
        P("rows", None, None, "cols"),
        P(None, None, "cols"),
        P("rows", None, None, "cols"),
        P("rows", None, None, "cols"),
        P(None, "rows", None, None, "cols"),
        P(None, "rows", None, "cols"),
        P(None, "rows", None, None, "cols"),
        P(None, "rows", None, None, "cols"),
        P(None, None, "cols"),
        P(None, None, "cols"),
    )
    shards = make_shards(mesh.shape["rows"], mesh.shape["cols"])
    return jax.shard_map(shards, mesh=mesh, in_specs=in_specs, out_specs=out_specs, check_vma=False)
```

```python
import jax
import jax.numpy as jnp
from jax import lax
from jax.experimental import pallas as pl
from jax.experimental.pallas import tpu as pltpu
from jax.sharding import PartitionSpec as P

D = 1536
HEAD_FEATURES = 64
IMAGE_TOKENS = 1024
TXT = 154
STEP = 2


BETA_ONE = 0.9
BETA_TWO = 0.95
LEARN_RATE = 0.02
DECAY_RATE = 0.1
ADAM_EPS = 1e-08
NORM_EPS = 1e-06
GELU_COEF = 0.7978845608028654
GELU_CUBE = 0.044715
PADDED = IMAGE_TOKENS + (TXT + 15) // 16 * 16
TOKENS = IMAGE_TOKENS + TXT
STREAM_ROWS = ((0, 0, IMAGE_TOKENS), (1, IMAGE_TOKENS, PADDED))
PAIR = 2 * HEAD_FEATURES
VMEM_BYTES = 56 * 1024 * 1024
F32 = jnp.float32
BF16 = jnp.bfloat16
COST_SHARE = 1000


def narrow(values):
    return values.astype(jnp.bfloat16)


def gelu_value(inputs):
    return (
        0.5 * inputs * (1.0 + jnp.tanh(GELU_COEF * (inputs + GELU_CUBE * inputs * inputs * inputs)))
    )


def gelu_slope(inputs):
    tangent = jnp.tanh(GELU_COEF * (inputs + GELU_CUBE * inputs * inputs * inputs))
    return 0.5 * (1.0 + tangent) + 0.5 * inputs * (1.0 - tangent * tangent) * GELU_COEF * (
        1.0 + 3.0 * GELU_CUBE * inputs * inputs
    )


def adam_step(param, moments, gradient):
    first_moment = BETA_ONE * moments[0] + (1.0 - BETA_ONE) * gradient
    second_moment = BETA_TWO * moments[1] + (1.0 - BETA_TWO) * gradient * gradient
    update = (
        first_moment
        / (1.0 - BETA_ONE**STEP)
        / (jnp.sqrt(second_moment / (1.0 - BETA_TWO**STEP)) + ADAM_EPS)
    )
    return (param - LEARN_RATE * (update + DECAY_RATE * param), first_moment, second_moment)


STEP_ROWS = 48


def pieces(kind, index):
    if kind == "triple":
        return [((3 * pair + index) * PAIR, pair * PAIR, PAIR) for pair in range(3)]
    if kind == "attended":
        return [(9 * PAIR, 0, 3 * PAIR)]
    return [(index * 3 * PAIR, 0, 3 * PAIR)]


def plane(kind, stream, index):
    return (stream, index) if kind == "hidden" else (index, stream)


def row_view(kind, weight):
    if kind == "attended":
        return jnp.expand_dims(weight, -3)
    return weight if kind == "hidden" else jnp.swapaxes(weight, -3, -2)


def row_unview(kind, weight):
    if kind == "attended":
        return jnp.squeeze(weight, -3)
    return weight if kind == "hidden" else jnp.swapaxes(weight, -3, -2)


def travel_rows(kinds, weights):
    views = [row_view(kind, weight) for kind, weight in zip(kinds, weights)]
    height = views[0].shape[0]

    def kernel(*refs):
        out_ref = refs[-1]
        for kind, ref in zip(kinds, refs):
            for stream in range(2):
                for index in range(ref.shape[1 if kind != "hidden" else 2]):
                    one, two = plane(kind, stream, index)
                    for there, here, size in pieces(kind, index):
                        out_ref[stream, :, there : there + size] = ref[
                            :, one, two, here : here + size
                        ].astype(BF16)

    total = 12 * PAIR
    return pl.pallas_call(
        kernel,
        grid=(height // STEP_ROWS,),
        in_specs=[
            pl.BlockSpec((STEP_ROWS, *view.shape[1:]), lambda i: (i, 0, 0, 0)) for view in views
        ],
        out_specs=pl.BlockSpec((2, STEP_ROWS, total), lambda i: (0, i, 0)),
        out_shape=jax.ShapeDtypeStruct((2, height, total), BF16),
        compiler_params=kernel_params(),
        cost_estimate=cost(2 * height * total, 12 * height * total),
    )(*views)


def adam_rows(kinds, params, moments, slot, partial, arrived):
    count = len(kinds)
    views = [row_view(kind, one) for kind, one in zip(kinds, params)]
    moment_views = [row_view(kind, one) for kind, one in zip(kinds, moments)]
    parts = views[0].shape[0] // STEP_ROWS

    def kernel(slot_ref, *refs):
        param_refs, refs = refs[:count], refs[count:]
        moment_refs, refs = refs[:count], refs[count:]
        grad_refs, refs = refs[:3], refs[3:]
        for place, kind in enumerate(kinds):
            next_ref, grad_ref, moved_ref = refs[3 * place : 3 * place + 3]
            param_ref, moment_ref = param_refs[place], moment_refs[place]
            for stream in range(2):
                for index in range(param_ref.shape[2 if kind == "hidden" else 1]):
                    one, two = plane(kind, stream, index)
                    gradient = jnp.concatenate(
                        [
                            sum(
                                ref[stream, :, there : there + size].astype(F32)
                                for ref in grad_refs
                            )
                            for there, _, size in pieces(kind, index)
                        ],
                        axis=1,
                    )
                    result, first_moment, second_moment = adam_step(
                        param_ref[:, one, two],
                        (moment_ref[0, :, one, two], moment_ref[1, :, one, two]),
                        gradient,
                    )
                    next_ref[:, one, two] = result
                    grad_ref[:, one, two] = gradient
                    moved_ref[0, :, one, two] = first_moment
                    moved_ref[1, :, one, two] = second_moment

    param_specs = [
        pl.BlockSpec((STEP_ROWS, *view.shape[1:]), lambda i, slot: (i, 0, 0, 0)) for view in views
    ]
    moment_specs = [
        pl.BlockSpec((2, STEP_ROWS, *view.shape[1:]), lambda i, slot: (0, i, 0, 0, 0))
        for view in views
    ]
    total = partial.shape[2]
    grad_spec = pl.BlockSpec((2, STEP_ROWS, total), lambda i, slot: (0, i, 0))
    own_spec = pl.BlockSpec((2, STEP_ROWS, total), lambda i, slot: (0, slot[0] * parts + i, 0))
    out_specs, out_shape = [], []
    for place, view in enumerate(views):
        out_specs += [param_specs[place], param_specs[place], moment_specs[place]]
        out_shape += [
            jax.ShapeDtypeStruct(one.shape, F32) for one in (view, view, moment_views[place])
        ]
    size = sum(view.size for view in views)
    results = pl.pallas_call(
        kernel,
        grid_spec=pltpu.PrefetchScalarGridSpec(
            num_scalar_prefetch=1,
            grid=(parts,),
            in_specs=[*param_specs, *moment_specs, own_spec, grad_spec, grad_spec],
            out_specs=out_specs,
        ),
        out_shape=out_shape,
        compiler_params=kernel_params(),
        cost_estimate=cost(20 * size, 40 * size),
    )(slot, *views, *moment_views, partial, *arrived)
    return [
        [row_unview(kind, one) for one in results[3 * place : 3 * place + 3]]
        for place, kind in enumerate(kinds)
    ]


def adam_modulation(param, moments, rows, table):
    view, moment_view = (row_view("modulation", param), row_view("modulation", moments))
    height, count, streams, width = view.shape
    turned = jnp.swapaxes(table, 1, 2).reshape(table.shape[0], count * streams * width)

    def kernel(rows_ref, table_ref, param_ref, moment_ref, next_ref, grad_ref, *moved_refs):
        for index in range(count):
            for stream in range(streams):
                low = (index * streams + stream) * width
                gradient = jnp.dot(
                    rows_ref[...], table_ref[:, low : low + width], preferred_element_type=F32
                )
                result, first_moment, second_moment = adam_step(
                    param_ref[:, index, stream],
                    (moment_ref[0, :, index, stream], moment_ref[1, :, index, stream]),
                    gradient,
                )
                next_ref[:, index, stream] = result
                grad_ref[:, index, stream] = gradient
                moved_refs[0][:, index, stream] = first_moment
                moved_refs[1][:, index, stream] = second_moment

    param_spec = pl.BlockSpec((STEP_ROWS, count, streams, width), lambda i: (i, 0, 0, 0))
    moment_spec = pl.BlockSpec((2, STEP_ROWS, count, streams, width), lambda i: (0, i, 0, 0, 0))
    shape = jax.ShapeDtypeStruct(view.shape, F32)
    results = pl.pallas_call(
        kernel,
        grid=(height // STEP_ROWS,),
        in_specs=[
            pl.BlockSpec((STEP_ROWS, rows.shape[0]), lambda i: (i, 0)),
            whole(turned.shape),
            param_spec,
            moment_spec,
        ],
        out_specs=[param_spec] * 4,
        out_shape=[shape] * 4,
        compiler_params=kernel_params(),
        cost_estimate=cost(20 * view.size, 40 * view.size),
    )(rows.T, turned, view, moment_view)
    return [row_unview("modulation", one) for one in results]


def kernel_params():
    return pltpu.CompilerParams(vmem_limit_bytes=VMEM_BYTES)


def cost(flops, nbytes, transcendentals=0):
    return pl.CostEstimate(flops=flops // COST_SHARE, bytes_accessed=nbytes // COST_SHARE, transcendentals=transcendentals)


def whole(shape):
    return pl.BlockSpec(shape, lambda j: (0,) * len(shape))


def arrivals_of(refs):
    count = len(refs) - 1
    half_way = count // 2
    offsets = [offset for offset in range(count) if offset != half_way]
    moves = [(offset, ref, 0, 2) for offset, ref in zip(offsets, refs)]
    return moves + [(half_way, refs[-2], 0, 1), (half_way, refs[-1], 1, 1)]


def matmul_rows(acts, blocks, slots, span, epilogue, extras, extra_specs, out_types, out_specs):
    rows, depth = acts.shape
    count = len(blocks)
    height = blocks[0].shape[1]
    first, width = (span[0], span[1] - span[0])
    tile = 384
    tiles = width // tile

    def kernel(slots_ref, acts_ref, *refs):
        block_refs, refs = refs[:count], refs[count:]
        refs, weight, arrivals = refs[:-2], refs[-2], refs[-1]

        moves = arrivals_of(block_refs)

        def copy(index, part):
            offset, ref, stream, streams = moves[index]
            row = pl.multiple_of(slots_ref[offset] * height, height)
            return pltpu.make_async_copy(
                ref.at[:, :, pl.ds(first + part * tile, tile)],
                weight.at[part, pl.ds(stream, streams), pl.ds(row, height), :],
                arrivals.at[part, index],
            )

        step = pl.program_id(0)

        @pl.when(step == 0)
        def _():
            for part in range(tiles):
                for index in range(count):
                    copy(index, part).start()

        for part in range(tiles):

            @pl.when(step == part)
            def _():
                for index in range(count):
                    copy(index, part).wait()

        for stream, low, high in STREAM_ROWS:
            product = jnp.dot(
                acts_ref[low:high], weight[step, stream], preferred_element_type=F32
            )
            epilogue(product, stream, low, high, *refs)

    return pl.pallas_call(
        kernel,
        grid=(tiles,),
        in_specs=[
            pl.BlockSpec(memory_space=pltpu.SMEM),
            whole((rows, depth)),
            *[pl.BlockSpec(memory_space=pl.ANY)] * count,
            *extra_specs,
        ],
        out_specs=out_specs,
        out_shape=out_types,
        scratch_shapes=[
            pltpu.VMEM((tiles, 2, depth, tile), BF16),
            pltpu.SemaphoreType.DMA((tiles, count)),
        ],
        compiler_params=kernel_params(),
        cost_estimate=cost(
            2 * rows * depth * width, 2 * (rows * depth + 2 * depth * width + rows * width)
        ),
    )(slots, acts, *blocks, *extras)


def column_spec(leading, tile=384):
    return pl.BlockSpec((leading, tile), lambda j: (0, j))


def project_triple(acts, blocks, slots, span, bias):
    def epilogue(product, stream, low, high, bias_ref, out_ref):
        out_ref[low:high] = (product + bias_ref[stream : stream + 1]).astype(BF16)

    rows, width = (acts.shape[0], span[1] - span[0])
    return matmul_rows(
        acts,
        blocks,
        slots,
        span,
        epilogue,
        [bias],
        [column_spec(2)],
        jax.ShapeDtypeStruct((rows, width), BF16),
        column_spec(rows),
    )


def raise_hidden(acts, blocks, slots, span, bias):
    def epilogue(product, stream, low, high, bias_ref, act_ref, slope_ref):
        inputs = product + bias_ref[stream : stream + 1]
        square = inputs * inputs
        tangent = jnp.tanh(GELU_COEF * inputs * (1.0 + GELU_CUBE * square))
        act_ref[low:high] = (0.5 * inputs * (1.0 + tangent)).astype(BF16)
        slope_ref[low:high] = 0.5 * (1.0 + tangent) + 0.5 * inputs * (
            1.0 - tangent * tangent
        ) * GELU_COEF * (1.0 + 3.0 * GELU_CUBE * square)

    rows, width = (acts.shape[0], span[1] - span[0])
    return matmul_rows(
        acts,
        blocks,
        slots,
        span,
        epilogue,
        [bias],
        [column_spec(2)],
        [jax.ShapeDtypeStruct((rows, width), BF16), jax.ShapeDtypeStruct((rows, width), F32)],
        [column_spec(rows), column_spec(rows)],
    )


def hidden_gradient(acts, blocks, slots, span, slope):
    def epilogue(product, stream, low, high, slope_ref, out_ref, sum_ref):
        gradient = product * slope_ref[low:high]
        out_ref[low:high] = gradient.astype(BF16)
        sum_ref[stream : stream + 1] = jnp.sum(gradient, axis=0, keepdims=True)

    rows, width = (acts.shape[0], span[1] - span[0])
    return matmul_rows(
        acts,
        blocks,
        slots,
        span,
        epilogue,
        [slope],
        [column_spec(rows)],
        [jax.ShapeDtypeStruct((rows, width), BF16), jax.ShapeDtypeStruct((2, width), F32)],
        [column_spec(rows), column_spec(2)],
    )


def attended_gradient(acts, blocks, slots, span):
    def epilogue(product, stream, low, high, out_ref):
        out_ref[low:high] = product.astype(BF16)

    rows, width = (acts.shape[0], span[1] - span[0])
    return matmul_rows(
        acts,
        blocks,
        slots,
        span,
        epilogue,
        [],
        [],
        jax.ShapeDtypeStruct((rows, width), BF16),
        column_spec(rows),
    )


def matmul_back(acts, blocks, slots, span, parity):
    rows, depth = acts.shape
    count = len(blocks)
    height = blocks[0].shape[1]
    share = (count - 1) // 4
    tile = share * height

    def kernel(slots_ref, acts_ref, *refs):
        block_refs, (*out_refs, weight, arrivals) = refs[:count], refs[count:]

        moves = arrivals_of(block_refs)

        def copy(index):
            offset, ref, stream, streams = moves[index]
            slot = slots_ref[offset]
            row = pl.multiple_of(slot % share * height, height)
            return pltpu.make_async_copy(
                ref.at[:, :, pl.ds(span[0], depth)],
                weight.at[slot // share // 2, pl.ds(stream, streams), pl.ds(row, height), :],
                arrivals.at[index],
            )

        def each(action, wanted):
            for index in range(count):
                pl.when(wanted(slots_ref[moves[index][0]] // share))(
                    lambda index=index: action(copy(index))
                )

        step = pl.program_id(0)

        @pl.when(step == 0)
        def _():
            for part in range(2):
                each(lambda job: job.start(), lambda group: group == 2 * part + parity)

        each(lambda job: job.wait(), lambda group: group == 2 * step + parity)
        for part, out_ref in enumerate(out_refs):

            @pl.when(step == part)
            def _():
                for stream, low, high in STREAM_ROWS:
                    out_ref[low:high] = lax.dot_general(
                        acts_ref[low:high],
                        weight[part, stream],
                        (((1,), (1,)), ((), ())),
                        preferred_element_type=F32,
                    ).astype(BF16)

    return pl.pallas_call(
        kernel,
        grid=(2,),
        in_specs=[
            pl.BlockSpec(memory_space=pltpu.SMEM),
            whole((rows, depth)),
            *[pl.BlockSpec(memory_space=pl.ANY)] * count,
        ],
        out_specs=[whole((rows, tile))] * 2,
        out_shape=[jax.ShapeDtypeStruct((rows, tile), BF16)] * 2,
        scratch_shapes=[
            pltpu.VMEM((2, 2, tile, depth), BF16),
            pltpu.SemaphoreType.DMA((count,)),
        ],
        compiler_params=kernel_params(),
        cost_estimate=cost(
            4 * rows * depth * tile, 2 * (rows * depth + 4 * depth * tile + 2 * rows * tile)
        ),
    )(slots, acts, *blocks)


def weight_gradient(outer, inner, full_width, first=0, *so_far, tile=384):
    rows, height = outer.shape
    width = inner.shape[1]

    def kernel(outer_ref, inner_ref, *refs):
        out_ref = refs[-1]
        for stream, low, high in STREAM_ROWS:
            out_ref[stream] = lax.dot_general(
                outer_ref[low:high],
                inner_ref[low:high],
                (((0,), (0,)), ((), ())),
                preferred_element_type=F32,
            ).astype(BF16)

    return pl.pallas_call(
        kernel,
        grid=(height // tile,),
        in_specs=[
            column_spec(rows, tile),
            whole((rows, width)),
            *[pl.BlockSpec(memory_space=pl.ANY)] * len(so_far),
        ],
        out_specs=pl.BlockSpec((2, tile, width), lambda j: (0, j, first // width)),
        out_shape=jax.ShapeDtypeStruct((2, height, full_width), BF16),
        input_output_aliases={2 + index: index for index in range(len(so_far))},
        compiler_params=kernel_params(),
        cost_estimate=cost(
            2 * rows * height * width, 2 * (rows * height + rows * width + 2 * height * width)
        ),
    )(outer, inner, *so_far)


def row_chunks(rows, size=256):
    return [(low, min(low + size, rows)) for low in range(0, rows, size)]


def attention(triple, first, last, *so_far):
    rows, width = triple.shape
    pairs = width // (3 * PAIR)
    scale = HEAD_FEATURES ** (-0.5)

    def kernel(triple_ref, *refs):
        out_ref, total_ref = refs[-2:]
        lane = lax.broadcasted_iota(jnp.int32, (1, PAIR), 1) // HEAD_FEATURES
        feature = lax.broadcasted_iota(jnp.int32, (PAIR, 1), 0) // HEAD_FEATURES
        key_index = lax.broadcasted_iota(jnp.int32, (rows, 1), 0)
        keys = triple_ref[:, PAIR : 2 * PAIR]
        values_turned = triple_ref[:, 2 * PAIR : 3 * PAIR].T
        for low, high in row_chunks(rows):
            queries = triple_ref[low:high, 0:PAIR] * jnp.asarray(scale, BF16)
            mixed = []
            for head in range(2):
                own = jnp.where(lane == head, queries, jnp.zeros_like(queries))
                scores = lax.dot_general(
                    keys, own, (((1,), (1,)), ((), ())), preferred_element_type=F32
                )
                scores = jnp.where(key_index < TOKENS, scores, -1e30)
                highest = jnp.max(scores, axis=0, keepdims=True)
                weights = jnp.exp(scores - highest)
                total = jnp.sum(weights, axis=0, keepdims=True)
                total_ref[0, head : head + 1, low:high] = highest + jnp.log(total)
                mixed.append(
                    jnp.dot(values_turned, weights.astype(BF16), preferred_element_type=F32)
                    / total
                )
            out_ref[low:high] = jnp.where(feature == 0, mixed[0], mixed[1]).T.astype(BF16)

    return pl.pallas_call(
        kernel,
        grid=(last - first,),
        in_specs=[
            pl.BlockSpec((rows, 3 * PAIR), lambda p: (0, p + first)),
            *[pl.BlockSpec(memory_space=pl.ANY)] * len(so_far),
        ],
        input_output_aliases={1 + index: index for index in range(len(so_far))},
        out_specs=[
            pl.BlockSpec((rows, PAIR), lambda p: (0, p + first)),
            pl.BlockSpec((1, 2, rows), lambda p: (p + first, 0, 0)),
        ],
        out_shape=[
            jax.ShapeDtypeStruct((rows, pairs * PAIR), BF16),
            jax.ShapeDtypeStruct((pairs, 2, rows), F32),
        ],
        compiler_params=kernel_params(),
        cost_estimate=cost(
            16 * pairs * PAIR * rows * rows, 8 * rows * width, 2 * pairs * rows * rows
        ),
    )(triple, *so_far)


def attention_back(triple, totals, grad_mix, first, last, *so_far):
    rows, width = triple.shape
    pairs = width // (3 * PAIR)
    scale = HEAD_FEATURES ** (-0.5)

    def kernel(triple_ref, total_ref, grad_ref, *refs):
        out_ref, sum_ref, key_acc, value_acc = refs[-4:]
        lane = lax.broadcasted_iota(jnp.int32, (1, PAIR), 1) // HEAD_FEATURES
        feature = lax.broadcasted_iota(jnp.int32, (PAIR, 1), 0) // HEAD_FEATURES
        key_index = lax.broadcasted_iota(jnp.int32, (rows, 1), 0)
        keys = triple_ref[:, PAIR : 2 * PAIR]
        values = triple_ref[:, 2 * PAIR : 3 * PAIR]
        keys_turned = keys.T
        query_sums = [jnp.zeros((1, PAIR), F32), jnp.zeros((1, PAIR), F32)]
        for step, (low, high) in enumerate(row_chunks(rows)):
            queries = triple_ref[low:high, 0:PAIR] * jnp.asarray(scale, BF16)
            grads = grad_ref[low:high]
            turned = []
            for head in range(2):
                own = jnp.where(lane == head, queries, jnp.zeros_like(queries))
                own_grad = jnp.where(lane == head, grads, jnp.zeros_like(grads))
                scores = lax.dot_general(
                    keys, own, (((1,), (1,)), ((), ())), preferred_element_type=F32
                )
                soft = jnp.exp(scores - total_ref[0, head : head + 1, low:high])
                soft = jnp.where(key_index < TOKENS, soft, 0.0)
                grad_soft = lax.dot_general(
                    values, own_grad, (((1,), (1,)), ((), ())), preferred_element_type=F32
                )
                delta = jnp.sum(soft * grad_soft, axis=0, keepdims=True)
                score_round = (soft * (grad_soft - delta)).astype(BF16)
                turned.append(jnp.dot(keys_turned, score_round, preferred_element_type=F32))
                key_part = jnp.dot(score_round, own, preferred_element_type=F32)
                value_part = jnp.dot(soft.astype(BF16), own_grad, preferred_element_type=F32)
                if step == 0 and head == 0:
                    key_acc[...] = key_part
                    value_acc[...] = value_part
                else:
                    key_acc[...] += key_part
                    value_acc[...] += value_part
            grad_query = (jnp.where(feature == 0, turned[0], turned[1]) * scale).T
            out_ref[low:high, 0:PAIR] = grad_query.astype(BF16)
            stream = 0 if high <= IMAGE_TOKENS else 1
            query_sums[stream] += jnp.sum(grad_query, axis=0, keepdims=True)
        out_ref[:, PAIR : 2 * PAIR] = key_acc[...].astype(BF16)
        out_ref[:, 2 * PAIR : 3 * PAIR] = value_acc[...].astype(BF16)
        for stream, low, high in STREAM_ROWS:
            sum_ref[0, stream : stream + 1, 0:PAIR] = query_sums[stream]
            sum_ref[0, stream : stream + 1, PAIR : 2 * PAIR] = jnp.sum(
                value_acc[low:high], axis=0, keepdims=True
            )

    return pl.pallas_call(
        kernel,
        grid=(last - first,),
        in_specs=[
            pl.BlockSpec((rows, 3 * PAIR), lambda p: (0, p + first)),
            pl.BlockSpec((1, 2, rows), lambda p: (p + first, 0, 0)),
            pl.BlockSpec((rows, PAIR), lambda p: (0, p + first)),
            *[pl.BlockSpec(memory_space=pl.ANY)] * len(so_far),
        ],
        input_output_aliases={3 + index: index for index in range(len(so_far))},
        out_specs=[
            pl.BlockSpec((rows, 3 * PAIR), lambda p: (0, p + first)),
            pl.BlockSpec((1, 2, 2 * PAIR), lambda p: (p + first, 0, 0)),
        ],
        out_shape=[
            jax.ShapeDtypeStruct((rows, width), BF16),
            jax.ShapeDtypeStruct((pairs, 2, 2 * PAIR), F32),
        ],
        scratch_shapes=[pltpu.VMEM((rows, PAIR), F32), pltpu.VMEM((rows, PAIR), F32)],
        compiler_params=kernel_params(),
        cost_estimate=cost(
            40 * pairs * PAIR * rows * rows, 8 * rows * width, 2 * pairs * rows * rows
        ),
    )(triple, totals, grad_mix, *so_far)


def per_token(table):
    row = lax.broadcasted_iota(jnp.int32, (PADDED, 1), 0)
    return jnp.where(row < IMAGE_TOKENS, table[0][None], table[1][None])


def stream_sums(values):
    return jnp.stack([jnp.sum(values[low:high], axis=0) for _, low, high in STREAM_ROWS])


def row_stats(total, square):
    center = total / D
    return (center, lax.rsqrt(square / D - center * center + NORM_EPS))


def join_tokens(image, text):
    blank = jnp.zeros((PADDED - TOKENS, image.shape[2]), image.dtype)
    return jnp.concatenate([image[0], text[0], blank], axis=0)


def add_halves(kept, arrived):
    own, other = [one.astype(F32) + two.astype(F32) for one, two in zip(kept, arrived)]
    return (own, narrow(other))


def make_shards(row_count, col_count):
    order = list(range(0, row_count, 2)) + list(range(row_count - 1, 0, -2))
    place = [order.index(device) for device in range(row_count)]
    ahead = [(order[i], order[(i + 1) % row_count]) for i in range(row_count)]
    behind = [(target, sender) for sender, target in ahead]
    near = [(device, device ^ 1) for device in range(col_count)]
    far = [(device, device ^ 2) for device in range(col_count)]
    across = [(device, device ^ 3) for device in range(col_count)]
    share = row_count // col_count
    half_way = row_count // 2

    slots = [
        [
            [
                (row // share ^ col) * share + row % share
                for row in (order[(place[here] + offset) % row_count] for offset in range(row_count))
            ]
            for col in range(col_count)
        ]
        for here in range(row_count)
    ]

    class Order:
        def __init__(self):
            self.last = []

        def tie(self, *values):
            if self.last:
                values, _ = lax.optimization_barrier((values, tuple(self.last)))
            return values

        def mark(self, *values):
            self.last = list(values)

        def add(self, *values):
            self.last += values

        def run(self, step, *values):
            result = step(*self.tie(*values))
            self.mark(*jax.tree.leaves(result))
            return result

    class Swap:
        def __init__(self, steps, value, pairs):
            (value,) = steps.tie(value)
            self.steps = steps
            self.value = lax.ppermute(value, "cols", pairs)

        def land(self):
            (self.value,) = self.steps.tie(self.value)
            self.steps.mark(self.value)
            return self.value

    def shift_pairs(offset):
        return [(row, (row + offset) % row_count) for row in range(row_count)]

    def rotate(values, start):
        return lax.dynamic_slice_in_dim(
            jnp.concatenate([values, values]), start, values.shape[0], 0
        )

    class Ring:
        def __init__(self, order_of_steps, slot_row):
            self.steps = order_of_steps
            self.slot_row = slot_row
            self.hops = {1: half_way, -1: half_way}
            self.done = {1: 0, -1: 0}
            self.held = {}

        def send(self, way):
            (value,) = self.steps.tie(self.held[way])
            self.held[way] = lax.ppermute(value, "rows", ahead if way == 1 else behind)

        def land(self, way, value):
            self.held[way] = value
            self.done[way] += 1
            self.take(way)

        def left(self):
            return max(self.hops[way] - self.done[way] for way in (1, -1))

        def slot(self, offset):
            return self.slot_row[offset % row_count]

    class Lanes:
        def __init__(self):
            self.queue = {1: [], -1: []}
            self.flying = {}

        def push(self, ring, ahead_of=None):
            for way in (1, -1):
                queue = self.queue[way]
                place_at = queue.index(ahead_of) if ahead_of in queue else len(queue)
                queue[place_at:place_at] = [ring] * ring.hops[way]

        def tick(self):
            flying, self.flying = list(self.flying.items()), {}
            if flying:
                steps = flying[0][1].steps
                values = steps.tie(*[ring.held[way] for way, ring in flying])
                steps.mark(*values)
                for (way, ring), value in zip(flying, values):
                    ring.land(way, value)
            for way in (1, -1):
                if self.queue[way]:
                    self.flying[way] = self.queue[way].pop(0)
                    self.flying[way].send(way)

        def until(self, ring, left=0):
            while ring.left() > left:
                self.tick()

    class RingGather(Ring):
        def __init__(self, order_of_steps, slot_row, block):
            super().__init__(order_of_steps, slot_row)
            self.blocks = [block] * row_count
            self.halves = {}
            self.held = {1: block, -1: block}

        def take(self, way):
            if self.done[way] == half_way:
                self.halves[way] = self.held[way]
                return
            self.blocks[-way * self.done[way] % row_count] = self.held[way]
            if self.done[way] == half_way - 1:
                stream = 0 if way == 1 else 1
                self.held[way] = self.held[way][stream : stream + 1]

        def arrays(self):
            whole_blocks = self.blocks[:half_way] + self.blocks[half_way + 1 :]
            return [*whole_blocks, self.halves[1], self.halves[-1]]

    class RingScatter(Ring):
        def __init__(self, order_of_steps, slot_row, partial, long_way=None):
            super().__init__(order_of_steps, slot_row)
            self.partial = partial
            self.height = partial.shape[1] // row_count
            self.halved = long_way is None
            if self.halved:
                starts = (self.part(half_way, 0, 1), self.part(-half_way, 1, 1))
            else:
                self.hops[-long_way] -= 1
                starts = [self.part(way * self.hops[way]) for way in (1, -1)]
            starts = self.steps.tie(*starts)
            self.steps.mark(*starts)
            self.held = dict(zip((1, -1), starts))

        def part(self, offset, stream=0, streams=2):
            return lax.dynamic_slice(
                self.partial,
                (stream, self.slot(offset) * self.height, 0),
                (streams, self.height, self.partial.shape[2]),
            )

        def take(self, way):
            left = self.hops[way] - self.done[way]
            if not left:
                return
            own = self.part(way * left).astype(F32)
            arrived = self.held[way].astype(F32)
            if self.halved and self.done[way] == 1:
                stream = 0 if way == 1 else 1
                with_arrived = own[stream : stream + 1] + arrived
                other = own[1 - stream : 2 - stream]
                pair = (with_arrived, other) if stream == 0 else (other, with_arrived)
                self.held[way] = narrow(jnp.concatenate(pair))
            else:
                self.held[way] = narrow(own + arrived)
            self.steps.add(self.held[way])

    def shards(
        x_img,
        x_txt,
        cond,
        back_img,
        back_txt,
        w_mod,
        w_qkv,
        w_proj,
        w_up,
        w_down,
        biases,
        moments_mod,
        moments_qkv,
        moments_proj,
        moments_up,
        moments_down,
        moments_bias,
    ):
        local_rows = w_qkv.shape[0]
        width = w_qkv.shape[3]
        pairs = width // PAIR
        slot_row = lax.dynamic_slice(
            jnp.asarray(slots, jnp.int32),
            (lax.axis_index("rows"), lax.axis_index("cols"), 0),
            (1, 1, row_count),
        )[0, 0]
        slot_list = [slot_row[offset] for offset in range(row_count)]
        steps = Order()

        def gather(block):
            return RingGather(steps, slot_list, block)

        def scatter(partial, long_way=None):
            return RingScatter(steps, slot_list, partial, long_way)

        def update(kinds, ring, params, moments):
            return steps.run(
                lambda params, moments, *values: adam_rows(
                    kinds, params, moments, ring.slot(0).reshape(1), values[0], values[1:]
                ),
                params,
                moments,
                ring.partial,
                ring.held[1],
                ring.held[-1],
            )

        def far_swap(value):
            return Swap(steps, value, far)

        def near_swap(value):
            return Swap(steps, value, near)

        def send_around(value):
            return [value] + [Swap(steps, value, pairs) for pairs in (near, far, across)]

        def land_around(parts):
            return [parts[0]] + [part.land() for part in parts[1:]]

        def total_around(parts):
            one, two, three, four = land_around(parts)
            return (one + two) + (three + four)

        triple_span, attended_span, hidden_span = (
            (0, 3 * width),
            (3 * width, 4 * width),
            (0, 4 * width),
        )

        def run(step, acts, ring, span, *rest):
            return steps.run(
                lambda acts, *rest: step(acts, ring.arrays(), slot_row, span, *rest), acts, *rest
            )

        def weight_part(outer, inner, *rest):
            return steps.run(
                lambda a, b, *so_far: weight_gradient(a, b, 4 * width, *rest[:1], *so_far),
                outer,
                inner,
                *rest[1:],
            )

        def send_halves(acts, ring, span, between=lambda: None):
            leaving = run(lambda *args: matmul_back(*args, 1), acts, ring, span)
            between()
            arriving = [near_swap(half) for half in leaving]
            return run(lambda *args: matmul_back(*args, 0), acts, ring, span), arriving

        def send_away(kept, arriving):
            own, other = steps.run(add_halves, kept, [half.land() for half in arriving])
            return own, far_swap(other)

        def start_width(value):
            return (value, far_swap(value), near_swap(value))

        def middle_width(parts):
            return (*parts, near_swap(parts[1].land()))

        def end_width(parts):
            value, away, beside, diagonal = parts
            diagonal.land()
            beside.land()
            return jnp.concatenate(
                [value, beside.value, away.value, diagonal.value], axis=-1
            )

        lanes = Lanes()

        def queued(ring, ahead_of=None):
            lanes.push(ring, ahead_of)
            return ring

        source_round = steps.run(join_tokens, x_img, x_txt)
        source_parts = start_width(source_round)
        silu_cond = narrow(jax.nn.silu(cond))
        mod_round = narrow(w_mod)
        (mod_terms,) = steps.tie(
            jnp.einsum("bd,dsic->bsic", silu_cond, mod_round, preferred_element_type=F32)
        )
        mod_parts = lax.all_to_all(mod_terms, "rows", 0, 0, tiled=True)
        first_local = travel_rows(("triple", "attended"), (w_qkv, w_proj))
        steps.mark(mod_parts, first_local)
        ring_first = queued(gather(first_local))
        lanes.tick()
        modulation = jnp.sum(mod_parts, axis=0) + biases[:, 0:6]
        mod_around = send_around(modulation)
        lanes.tick()
        modulation_full = jnp.concatenate(land_around(mod_around), axis=-1)
        source_parts = middle_width(source_parts)
        source_full = end_width(source_parts).astype(F32)
        scale_one, gate_one, scale_two, gate_two = [
            per_token(modulation[:, slot_index]) for slot_index in (1, 2, 4, 5)
        ]
        shift_two = per_token(modulation[:, 3])
        source = source_round.astype(F32)

        def first_norm(full, full_modulation):
            center, inverse = row_stats(
                jnp.sum(full, axis=1, keepdims=True),
                jnp.sum(full * full, axis=1, keepdims=True),
            )
            normed = narrow(
                (full - center) * inverse * (1.0 + per_token(full_modulation[:, 1]))
                + per_token(full_modulation[:, 0])
            )
            return center, inverse, normed

        center_one, inverse_one, normed_one = steps.run(first_norm, source_full, modulation_full)
        cotangent_round = steps.run(join_tokens, back_img, back_txt)
        cotangent = cotangent_round.astype(F32)
        unit_one = (source - center_one) * inverse_one
        lanes.tick()
        cotangent_parts = start_width(cotangent_round)
        ring_up = queued(
            gather(steps.run(lambda w: travel_rows(("hidden",), (w,)), w_up))
        )
        ring_down = queued(
            gather(steps.run(lambda w: travel_rows(("hidden",), (w,)), w_down))
        )
        lanes.tick()
        cotangent_parts = middle_width(cotangent_parts)
        lanes.until(ring_first)
        cotangent_full = end_width(cotangent_parts)
        triple_bias = (
            jnp.stack([biases[:, 6], jnp.zeros_like(biases[:, 6]), biases[:, 7]], axis=1)
            .reshape(2, 3, pairs, PAIR)
            .swapaxes(1, 2)
            .reshape(2, 3 * width)
        )
        triple = run(project_triple, normed_one, ring_first, triple_span, triple_bias)
        so_far = ()
        for pair in range(pairs):
            so_far = steps.run(
                lambda t, *rest, pair=pair: attention(t, pair, pair + 1, *rest), triple, *so_far
            )
            if pair == 0:
                lanes.tick()
        attended, log_totals = so_far
        halves = send_halves(attended, ring_first, attended_span)
        lanes.tick()
        own, away = send_away(*halves)
        lanes.tick()

        def residual_terms(own, away, source):
            projected = own + away.astype(F32) + per_token(biases[:, 8])
            residual = source + gate_one * projected
            sums = jnp.stack([jnp.sum(residual, axis=1), jnp.sum(residual * residual, axis=1)])
            return projected, residual, sums

        projected, residual, sums = steps.run(residual_terms, own, away.land(), source)
        sums_around = send_around(sums)
        lanes.tick()
        totals_two = total_around(sums_around)
        center_two, inverse_two = row_stats(totals_two[0][:, None], totals_two[1][:, None])
        unit_two = (residual - center_two) * inverse_two
        normed_own = narrow(unit_two * (1.0 + scale_two) + shift_two)
        steps.mark(normed_own)
        normed_parts = start_width(normed_own)
        lanes.tick()
        lanes.until(ring_up)
        lowered_full = steps.run(
            lambda full, gate: narrow(full.astype(F32) * per_token(gate)),
            cotangent_full,
            modulation_full[:, 5],
        )
        normed_two = end_width(middle_width(normed_parts))
        hidden_act, hidden_slope = run(
            raise_hidden, normed_two, ring_up, hidden_span, biases[:, 9:13].reshape(2, 4 * width)
        )
        lanes.tick()
        ring_grad_down = queued(
            scatter(weight_part(lowered_full, hidden_act), 1)
        )
        lanes.until(ring_down)
        hidden_round, hidden_sums = run(
            hidden_gradient, lowered_full, ring_down, hidden_span, hidden_slope
        )
        halves = send_halves(hidden_round, ring_up, hidden_span, lanes.tick)
        own, away = send_away(*halves)
        ring_grad_up = queued(
            scatter(weight_part(normed_two, hidden_round), -1)
        )
        lanes.tick()

        def back_sums(grad_unit, unit_rows):
            return jnp.stack([jnp.sum(grad_unit, axis=1), jnp.sum(grad_unit * unit_rows, axis=1)])

        def normalize_back(grad_unit, unit_rows, inverse, totals):
            return inverse * (
                grad_unit - totals[0][:, None] / D - unit_rows * (totals[1][:, None] / D)
            )

        grad_normed_two = own + away.land().astype(F32)
        grad_unit_two = grad_normed_two * (1.0 + scale_two)
        sums = back_sums(grad_unit_two, unit_two)
        steps.mark(sums)
        sums_around = send_around(sums)
        lanes.tick()
        totals = total_around(sums_around)
        grad_residual = cotangent + normalize_back(grad_unit_two, unit_two, inverse_two, totals)
        grad_projected = gate_one * grad_residual
        projected_own = narrow(grad_projected)
        steps.mark(projected_own)
        projected_parts = start_width(projected_own)
        lowered_leaving = run(
            lambda *args: matmul_back(*args, 1), hidden_act, ring_down, hidden_span
        )
        lowered_kept = run(
            lambda *args: matmul_back(*args, 0), hidden_act, ring_down, hidden_span
        )
        arriving = [near_swap(half) for half in lowered_leaving]
        lanes.tick()
        projected_full = end_width(middle_width(projected_parts))
        grad_attended = run(attended_gradient, projected_full, ring_first, attended_span)
        so_far = ()
        for pair in range(pairs):
            so_far = steps.run(
                lambda t, l, g, *rest, pair=pair: attention_back(t, l, g, pair, pair + 1, *rest),
                triple,
                log_totals,
                grad_attended,
                *so_far,
            )
            if pair == 0:
                own_lowered, away_lowered = send_away(lowered_kept, arriving)
                lanes.tick()
        lowered_away = away_lowered.land()
        lanes.tick()
        triple_round, triple_sums = so_far
        partial_first = weight_part(normed_one, triple_round, 0)
        partial_first = weight_part(projected_full, attended, 3 * width, partial_first)
        ring_grad_first = queued(scatter(partial_first), ring_grad_up)
        halves = send_halves(triple_round, ring_first, triple_span, lanes.tick)
        own, away = send_away(*halves)
        lanes.tick()
        ((next_down, grad_down, moved_down),) = update(
            ("hidden",), ring_grad_down, (w_down,), (moments_down,)
        )
        lanes.until(ring_grad_up)
        ((next_up, grad_up, moved_up),) = update(
            ("hidden",), ring_grad_up, (w_up,), (moments_up,)
        )
        lowered = own_lowered + lowered_away.astype(F32) + per_token(biases[:, 13])
        grad_lowered = gate_two * cotangent
        grad_normed_one = own + away.land().astype(F32)
        grad_unit_one = grad_normed_one * (1.0 + scale_one)
        sums = back_sums(grad_unit_one, unit_one)
        steps.mark(sums)
        sums_around = send_around(sums)
        head_sums = triple_sums.reshape(pairs, 2, 2, PAIR).transpose(1, 2, 0, 3)
        part = jnp.concatenate(
            [
                stream_sums(grad_normed_one)[:, None],
                stream_sums(grad_normed_one * unit_one)[:, None],
                stream_sums(grad_residual * projected)[:, None],
                stream_sums(grad_normed_two)[:, None],
                stream_sums(grad_normed_two * unit_two)[:, None],
                stream_sums(cotangent * lowered)[:, None],
                head_sums.reshape(2, 2, width),
                stream_sums(grad_projected)[:, None],
                hidden_sums.reshape(2, 4, width),
                stream_sums(grad_lowered)[:, None],
            ],
            axis=1,
        )
        steps.mark(part)
        lanes.tick()
        (part,) = steps.tie(part)
        part_all = lax.all_to_all(
            jnp.broadcast_to(part[None], (row_count,) + part.shape), "rows", 0, 0, tiled=True
        )
        steps.mark(part_all)
        totals = total_around(sums_around)
        grad_source = grad_residual + normalize_back(grad_unit_one, unit_one, inverse_one, totals)
        steps.add(grad_source)
        table_round = narrow(part_all[:, :, 0:6])
        grad_bias = jnp.sum(part_all, axis=0)
        silu_terms = jnp.einsum("bsic,dsic->bd", table_round, mod_round, preferred_element_type=F32)
        steps.mark(silu_terms)
        silu_around = send_around(silu_terms)
        grad_silu = total_around(silu_around)
        sigmoid_cond = jax.nn.sigmoid(cond)
        grad_cond = grad_silu * sigmoid_cond * (1.0 + cond * (1.0 - sigmoid_cond))
        next_bias, first_bias, second_bias = adam_step(biases, moments_bias, grad_bias)
        steps.add(next_bias, first_bias, second_bias, grad_cond)
        next_mod, grad_mod, first_mod, second_mod = steps.run(
            adam_modulation, w_mod, moments_mod, silu_cond, table_round
        )
        lanes.until(ring_grad_first, 1)
        own_lowered, lowered_away = steps.tie(own_lowered, lowered_away)
        output = narrow(
            residual
            + gate_two * (own_lowered + lowered_away.astype(F32) + per_token(biases[:, 13]))
        )
        steps.add(output)
        lanes.until(ring_grad_first)
        (next_qkv, grad_qkv, moved_qkv), (next_proj, grad_proj, moved_proj) = update(
            ("triple", "attended"),
            ring_grad_first,
            (w_qkv, w_proj),
            (moments_qkv, moments_proj),
        )
        return (
            output[None, :IMAGE_TOKENS],
            output[None, IMAGE_TOKENS:TOKENS],
            grad_source[None, :IMAGE_TOKENS],
            grad_source[None, IMAGE_TOKENS:TOKENS],
            grad_cond,
            grad_mod,
            grad_qkv,
            grad_proj,
            grad_up,
            grad_down,
            grad_bias,
            next_mod,
            next_qkv,
            next_proj,
            next_up,
            next_down,
            next_bias,
            first_mod,
            second_mod,
            moved_qkv,
            moved_proj,
            moved_up,
            moved_down,
            first_bias,
            second_bias,
        )

    return shards


def solution(mesh):
    in_specs = (
        P("rows", None, "cols"),
        P("rows", None, "cols"),
        P(None, "rows"),
        P("rows", None, "cols"),
        P("rows", None, "cols"),
        P("rows", None, None, "cols"),
        P("rows", None, None, "cols"),
        P("rows", None, "cols"),
        P("rows", None, None, "cols"),
        P("rows", None, None, "cols"),
        P(None, None, "cols"),
        P(None, "rows", None, None, "cols"),
        P(None, "rows", None, None, "cols"),
        P(None, "rows", None, "cols"),
        P(None, "rows", None, None, "cols"),
        P(None, "rows", None, None, "cols"),
        P(None, None, None, "cols"),
    )
    out_specs = (
        P("rows", None, "cols"),
        P("rows", None, "cols"),
        P("rows", None, "cols"),
        P("rows", None, "cols"),
        P(None, "rows"),
        P("rows", None, None, "cols"),
        P("rows", None, None, "cols"),
        P("rows", None, "cols"),
        P("rows", None, None, "cols"),
        P("rows", None, None, "cols"),
        P(None, None, "cols"),
        P("rows", None, None, "cols"),
        P("rows", None, None, "cols"),
        P("rows", None, "cols"),
        P("rows", None, None, "cols"),
        P("rows", None, None, "cols"),
        P(None, None, "cols"),
        P("rows", None, None, "cols"),
        P("rows", None, None, "cols"),
        P(None, "rows", None, None, "cols"),
        P(None, "rows", None, "cols"),
        P(None, "rows", None, None, "cols"),
        P(None, "rows", None, None, "cols"),
        P(None, None, "cols"),
        P(None, None, "cols"),
    )
    shards = make_shards(mesh.shape["rows"], mesh.shape["cols"])
    return jax.shard_map(shards, mesh=mesh, in_specs=in_specs, out_specs=out_specs, check_vma=False)
```

```python
import jax
import jax.numpy as jnp
from jax import lax
from jax.experimental import pallas as pl
from jax.experimental.pallas import tpu as pltpu
from jax.sharding import PartitionSpec as P

D = 1536
HEAD_FEATURES = 64
IMAGE_TOKENS = 1024
TXT = 154
STEP = 2


BETA_ONE = 0.9
BETA_TWO = 0.95
LEARN_RATE = 0.02
DECAY_RATE = 0.1
ADAM_EPS = 1e-08
NORM_EPS = 1e-06
GELU_COEF = 0.7978845608028654
GELU_CUBE = 0.044715
PADDED = IMAGE_TOKENS + (TXT + 15) // 16 * 16
TOKENS = IMAGE_TOKENS + TXT
STREAM_ROWS = ((0, 0, IMAGE_TOKENS), (1, IMAGE_TOKENS, PADDED))
PAIR = 2 * HEAD_FEATURES
VMEM_BYTES = 56 * 1024 * 1024
F32 = jnp.float32
BF16 = jnp.bfloat16
COST_SHARE = 1000


def narrow(values):
    return values.astype(jnp.bfloat16)


def gelu_value(inputs):
    return (
        0.5 * inputs * (1.0 + jnp.tanh(GELU_COEF * (inputs + GELU_CUBE * inputs * inputs * inputs)))
    )


def gelu_slope(inputs):
    tangent = jnp.tanh(GELU_COEF * (inputs + GELU_CUBE * inputs * inputs * inputs))
    return 0.5 * (1.0 + tangent) + 0.5 * inputs * (1.0 - tangent * tangent) * GELU_COEF * (
        1.0 + 3.0 * GELU_CUBE * inputs * inputs
    )


def adam_step(param, moments, gradient):
    first_moment = BETA_ONE * moments[0] + (1.0 - BETA_ONE) * gradient
    second_moment = BETA_TWO * moments[1] + (1.0 - BETA_TWO) * gradient * gradient
    update = (
        first_moment
        / (1.0 - BETA_ONE**STEP)
        / (jnp.sqrt(second_moment / (1.0 - BETA_TWO**STEP)) + ADAM_EPS)
    )
    return (param - LEARN_RATE * (update + DECAY_RATE * param), first_moment, second_moment)


STEP_ROWS = 48


def pieces(kind, index):
    if kind == "triple":
        return [((3 * pair + index) * PAIR, pair * PAIR, PAIR) for pair in range(3)]
    if kind == "attended":
        return [(9 * PAIR, 0, 3 * PAIR)]
    return [(index * 3 * PAIR, 0, 3 * PAIR)]


def plane(kind, stream, index):
    return (stream, index) if kind == "hidden" else (index, stream)


def row_view(kind, weight):
    if kind == "attended":
        return jnp.expand_dims(weight, -3)
    return weight if kind == "hidden" else jnp.swapaxes(weight, -3, -2)


def row_unview(kind, weight):
    if kind == "attended":
        return jnp.squeeze(weight, -3)
    return weight if kind == "hidden" else jnp.swapaxes(weight, -3, -2)


def travel_rows(kinds, weights):
    views = [row_view(kind, weight) for kind, weight in zip(kinds, weights)]
    height = views[0].shape[0]

    def kernel(*refs):
        out_ref = refs[-1]
        for kind, ref in zip(kinds, refs):
            for stream in range(2):
                for index in range(ref.shape[1 if kind != "hidden" else 2]):
                    one, two = plane(kind, stream, index)
                    for there, here, size in pieces(kind, index):
                        out_ref[stream, :, there : there + size] = ref[
                            :, one, two, here : here + size
                        ].astype(BF16)

    total = 12 * PAIR
    return pl.pallas_call(
        kernel,
        grid=(height // STEP_ROWS,),
        in_specs=[
            pl.BlockSpec((STEP_ROWS, *view.shape[1:]), lambda i: (i, 0, 0, 0)) for view in views
        ],
        out_specs=pl.BlockSpec((2, STEP_ROWS, total), lambda i: (0, i, 0)),
        out_shape=jax.ShapeDtypeStruct((2, height, total), BF16),
        compiler_params=kernel_params(),
        cost_estimate=cost(2 * height * total, 12 * height * total),
    )(*views)


def adam_rows(kinds, params, moments, slot, partial, arrived):
    count = len(kinds)
    views = [row_view(kind, one) for kind, one in zip(kinds, params)]
    moment_views = [row_view(kind, one) for kind, one in zip(kinds, moments)]
    parts = views[0].shape[0] // STEP_ROWS

    def kernel(slot_ref, *refs):
        param_refs, refs = refs[:count], refs[count:]
        moment_refs, refs = refs[:count], refs[count:]
        grad_refs, refs = refs[:3], refs[3:]
        for place, kind in enumerate(kinds):
            next_ref, grad_ref, moved_ref = refs[3 * place : 3 * place + 3]
            param_ref, moment_ref = param_refs[place], moment_refs[place]
            for stream in range(2):
                for index in range(param_ref.shape[2 if kind == "hidden" else 1]):
                    one, two = plane(kind, stream, index)
                    gradient = jnp.concatenate(
                        [
                            sum(
                                ref[stream, :, there : there + size].astype(F32)
                                for ref in grad_refs
                            )
                            for there, _, size in pieces(kind, index)
                        ],
                        axis=1,
                    )
                    result, first_moment, second_moment = adam_step(
                        param_ref[:, one, two],
                        (moment_ref[0, :, one, two], moment_ref[1, :, one, two]),
                        gradient,
                    )
                    next_ref[:, one, two] = result
                    grad_ref[:, one, two] = gradient
                    moved_ref[0, :, one, two] = first_moment
                    moved_ref[1, :, one, two] = second_moment

    param_specs = [
        pl.BlockSpec((STEP_ROWS, *view.shape[1:]), lambda i, slot: (i, 0, 0, 0)) for view in views
    ]
    moment_specs = [
        pl.BlockSpec((2, STEP_ROWS, *view.shape[1:]), lambda i, slot: (0, i, 0, 0, 0))
        for view in views
    ]
    total = partial.shape[2]
    grad_spec = pl.BlockSpec((2, STEP_ROWS, total), lambda i, slot: (0, i, 0))
    own_spec = pl.BlockSpec((2, STEP_ROWS, total), lambda i, slot: (0, slot[0] * parts + i, 0))
    out_specs, out_shape = [], []
    for place, view in enumerate(views):
        out_specs += [param_specs[place], param_specs[place], moment_specs[place]]
        out_shape += [
            jax.ShapeDtypeStruct(one.shape, F32) for one in (view, view, moment_views[place])
        ]
    size = sum(view.size for view in views)
    results = pl.pallas_call(
        kernel,
        grid_spec=pltpu.PrefetchScalarGridSpec(
            num_scalar_prefetch=1,
            grid=(parts,),
            in_specs=[*param_specs, *moment_specs, own_spec, grad_spec, grad_spec],
            out_specs=out_specs,
        ),
        out_shape=out_shape,
        compiler_params=kernel_params(),
        cost_estimate=cost(20 * size, 40 * size),
    )(slot, *views, *moment_views, partial, *arrived)
    return [
        [row_unview(kind, one) for one in results[3 * place : 3 * place + 3]]
        for place, kind in enumerate(kinds)
    ]


def adam_modulation(param, moments, rows, table):
    view, moment_view = (row_view("modulation", param), row_view("modulation", moments))
    height, count, streams, width = view.shape
    turned = jnp.swapaxes(table, 1, 2).reshape(table.shape[0], count * streams * width)

    def kernel(rows_ref, table_ref, param_ref, moment_ref, next_ref, grad_ref, *moved_refs):
        for index in range(count):
            for stream in range(streams):
                low = (index * streams + stream) * width
                gradient = jnp.dot(
                    rows_ref[...], table_ref[:, low : low + width], preferred_element_type=F32
                )
                result, first_moment, second_moment = adam_step(
                    param_ref[:, index, stream],
                    (moment_ref[0, :, index, stream], moment_ref[1, :, index, stream]),
                    gradient,
                )
                next_ref[:, index, stream] = result
                grad_ref[:, index, stream] = gradient
                moved_refs[0][:, index, stream] = first_moment
                moved_refs[1][:, index, stream] = second_moment

    param_spec = pl.BlockSpec((STEP_ROWS, count, streams, width), lambda i: (i, 0, 0, 0))
    moment_spec = pl.BlockSpec((2, STEP_ROWS, count, streams, width), lambda i: (0, i, 0, 0, 0))
    shape = jax.ShapeDtypeStruct(view.shape, F32)
    results = pl.pallas_call(
        kernel,
        grid=(height // STEP_ROWS,),
        in_specs=[
            pl.BlockSpec((STEP_ROWS, rows.shape[0]), lambda i: (i, 0)),
            whole(turned.shape),
            param_spec,
            moment_spec,
        ],
        out_specs=[param_spec] * 4,
        out_shape=[shape] * 4,
        compiler_params=kernel_params(),
        cost_estimate=cost(20 * view.size, 40 * view.size),
    )(rows.T, turned, view, moment_view)
    return [row_unview("modulation", one) for one in results]


def kernel_params():
    return pltpu.CompilerParams(vmem_limit_bytes=VMEM_BYTES)


def cost(flops, nbytes, transcendentals=0):
    return pl.CostEstimate(flops=flops // COST_SHARE, bytes_accessed=nbytes // COST_SHARE, transcendentals=transcendentals)


def whole(shape):
    return pl.BlockSpec(shape, lambda j: (0,) * len(shape))


def arrivals_of(refs):
    count = len(refs) - 1
    half_way = count // 2
    offsets = [offset for offset in range(count) if offset != half_way]
    moves = [(offset, ref, 0, 2) for offset, ref in zip(offsets, refs)]
    return moves + [(half_way, refs[-2], 0, 1), (half_way, refs[-1], 1, 1)]


def matmul_rows(acts, blocks, slots, span, epilogue, extras, extra_specs, out_types, out_specs):
    rows, depth = acts.shape
    count = len(blocks)
    height = blocks[0].shape[1]
    first, width = (span[0], span[1] - span[0])
    tile = 384
    tiles = width // tile

    def kernel(slots_ref, acts_ref, *refs):
        block_refs, refs = refs[:count], refs[count:]
        refs, weight, arrivals = refs[:-2], refs[-2], refs[-1]

        moves = arrivals_of(block_refs)

        def copy(index, part):
            offset, ref, stream, streams = moves[index]
            row = pl.multiple_of(slots_ref[offset] * height, height)
            return pltpu.make_async_copy(
                ref.at[:, :, pl.ds(first + part * tile, tile)],
                weight.at[part, pl.ds(stream, streams), pl.ds(row, height), :],
                arrivals.at[part, index],
            )

        step = pl.program_id(0)

        @pl.when(step == 0)
        def _():
            for part in range(tiles):
                for index in range(count):
                    copy(index, part).start()

        for part in range(tiles):

            @pl.when(step == part)
            def _():
                for index in range(count):
                    copy(index, part).wait()

        for stream, low, high in STREAM_ROWS:
            product = jnp.dot(
                acts_ref[low:high], weight[step, stream], preferred_element_type=F32
            )
            epilogue(product, stream, low, high, *refs)

    return pl.pallas_call(
        kernel,
        grid=(tiles,),
        in_specs=[
            pl.BlockSpec(memory_space=pltpu.SMEM),
            whole((rows, depth)),
            *[pl.BlockSpec(memory_space=pl.ANY)] * count,
            *extra_specs,
        ],
        out_specs=out_specs,
        out_shape=out_types,
        scratch_shapes=[
            pltpu.VMEM((tiles, 2, depth, tile), BF16),
            pltpu.SemaphoreType.DMA((tiles, count)),
        ],
        compiler_params=kernel_params(),
        cost_estimate=cost(
            2 * rows * depth * width, 2 * (rows * depth + 2 * depth * width + rows * width)
        ),
    )(slots, acts, *blocks, *extras)


def column_spec(leading, tile=384):
    return pl.BlockSpec((leading, tile), lambda j: (0, j))


def project_triple(acts, blocks, slots, span, bias):
    def epilogue(product, stream, low, high, bias_ref, out_ref):
        out_ref[low:high] = (product + bias_ref[stream : stream + 1]).astype(BF16)

    rows, width = (acts.shape[0], span[1] - span[0])
    return matmul_rows(
        acts,
        blocks,
        slots,
        span,
        epilogue,
        [bias],
        [column_spec(2)],
        jax.ShapeDtypeStruct((rows, width), BF16),
        column_spec(rows),
    )


def raise_hidden(acts, blocks, slots, span, bias):
    def epilogue(product, stream, low, high, bias_ref, act_ref, slope_ref):
        inputs = product + bias_ref[stream : stream + 1]
        square = inputs * inputs
        tangent = jnp.tanh(GELU_COEF * inputs * (1.0 + GELU_CUBE * square))
        act_ref[low:high] = (0.5 * inputs * (1.0 + tangent)).astype(BF16)
        slope_ref[low:high] = 0.5 * (1.0 + tangent) + 0.5 * inputs * (
            1.0 - tangent * tangent
        ) * GELU_COEF * (1.0 + 3.0 * GELU_CUBE * square)

    rows, width = (acts.shape[0], span[1] - span[0])
    return matmul_rows(
        acts,
        blocks,
        slots,
        span,
        epilogue,
        [bias],
        [column_spec(2)],
        [jax.ShapeDtypeStruct((rows, width), BF16), jax.ShapeDtypeStruct((rows, width), F32)],
        [column_spec(rows), column_spec(rows)],
    )


def hidden_gradient(acts, blocks, slots, span, slope):
    def epilogue(product, stream, low, high, slope_ref, out_ref, sum_ref):
        gradient = product * slope_ref[low:high]
        out_ref[low:high] = gradient.astype(BF16)
        sum_ref[stream : stream + 1] = jnp.sum(gradient, axis=0, keepdims=True)

    rows, width = (acts.shape[0], span[1] - span[0])
    return matmul_rows(
        acts,
        blocks,
        slots,
        span,
        epilogue,
        [slope],
        [column_spec(rows)],
        [jax.ShapeDtypeStruct((rows, width), BF16), jax.ShapeDtypeStruct((2, width), F32)],
        [column_spec(rows), column_spec(2)],
    )


def attended_gradient(acts, blocks, slots, span):
    def epilogue(product, stream, low, high, out_ref):
        out_ref[low:high] = product.astype(BF16)

    rows, width = (acts.shape[0], span[1] - span[0])
    return matmul_rows(
        acts,
        blocks,
        slots,
        span,
        epilogue,
        [],
        [],
        jax.ShapeDtypeStruct((rows, width), BF16),
        column_spec(rows),
    )


def matmul_back(acts, blocks, slots, span, parity):
    rows, depth = acts.shape
    count = len(blocks)
    height = blocks[0].shape[1]
    share = (count - 1) // 4
    tile = share * height

    def kernel(slots_ref, acts_ref, *refs):
        block_refs, (*out_refs, weight, arrivals) = refs[:count], refs[count:]

        moves = arrivals_of(block_refs)

        def copy(index):
            offset, ref, stream, streams = moves[index]
            slot = slots_ref[offset]
            row = pl.multiple_of(slot % share * height, height)
            return pltpu.make_async_copy(
                ref.at[:, :, pl.ds(span[0], depth)],
                weight.at[slot // share // 2, pl.ds(stream, streams), pl.ds(row, height), :],
                arrivals.at[index],
            )

        def each(action, wanted):
            for index in range(count):
                pl.when(wanted(slots_ref[moves[index][0]] // share))(
                    lambda index=index: action(copy(index))
                )

        step = pl.program_id(0)

        @pl.when(step == 0)
        def _():
            for part in range(2):
                each(lambda job: job.start(), lambda group: group == 2 * part + parity)

        each(lambda job: job.wait(), lambda group: group == 2 * step + parity)
        for part, out_ref in enumerate(out_refs):

            @pl.when(step == part)
            def _():
                for stream, low, high in STREAM_ROWS:
                    out_ref[low:high] = lax.dot_general(
                        acts_ref[low:high],
                        weight[part, stream],
                        (((1,), (1,)), ((), ())),
                        preferred_element_type=F32,
                    ).astype(BF16)

    return pl.pallas_call(
        kernel,
        grid=(2,),
        in_specs=[
            pl.BlockSpec(memory_space=pltpu.SMEM),
            whole((rows, depth)),
            *[pl.BlockSpec(memory_space=pl.ANY)] * count,
        ],
        out_specs=[whole((rows, tile))] * 2,
        out_shape=[jax.ShapeDtypeStruct((rows, tile), BF16)] * 2,
        scratch_shapes=[
            pltpu.VMEM((2, 2, tile, depth), BF16),
            pltpu.SemaphoreType.DMA((count,)),
        ],
        compiler_params=kernel_params(),
        cost_estimate=cost(
            4 * rows * depth * tile, 2 * (rows * depth + 4 * depth * tile + 2 * rows * tile)
        ),
    )(slots, acts, *blocks)


def weight_gradient(outer, inner, full_width, first=0, *so_far, tile=384):
    rows, height = outer.shape
    width = inner.shape[1]

    def kernel(outer_ref, inner_ref, *refs):
        out_ref = refs[-1]
        for stream, low, high in STREAM_ROWS:
            out_ref[stream] = lax.dot_general(
                outer_ref[low:high],
                inner_ref[low:high],
                (((0,), (0,)), ((), ())),
                preferred_element_type=F32,
            ).astype(BF16)

    return pl.pallas_call(
        kernel,
        grid=(height // tile,),
        in_specs=[
            column_spec(rows, tile),
            whole((rows, width)),
            *[pl.BlockSpec(memory_space=pl.ANY)] * len(so_far),
        ],
        out_specs=pl.BlockSpec((2, tile, width), lambda j: (0, j, first // width)),
        out_shape=jax.ShapeDtypeStruct((2, height, full_width), BF16),
        input_output_aliases={2 + index: index for index in range(len(so_far))},
        compiler_params=kernel_params(),
        cost_estimate=cost(
            2 * rows * height * width, 2 * (rows * height + rows * width + 2 * height * width)
        ),
    )(outer, inner, *so_far)


def row_chunks(rows, size=256):
    return [(low, min(low + size, rows)) for low in range(0, rows, size)]


def attention(triple, first, last, *so_far):
    rows, width = triple.shape
    pairs = width // (3 * PAIR)
    scale = HEAD_FEATURES ** (-0.5)

    def kernel(triple_ref, *refs):
        out_ref, total_ref = refs[-2:]
        lane = lax.broadcasted_iota(jnp.int32, (1, PAIR), 1) // HEAD_FEATURES
        feature = lax.broadcasted_iota(jnp.int32, (PAIR, 1), 0) // HEAD_FEATURES
        key_index = lax.broadcasted_iota(jnp.int32, (rows, 1), 0)
        keys = triple_ref[:, PAIR : 2 * PAIR]
        values_turned = triple_ref[:, 2 * PAIR : 3 * PAIR].T
        for low, high in row_chunks(rows):
            queries = triple_ref[low:high, 0:PAIR] * jnp.asarray(scale, BF16)
            mixed = []
            for head in range(2):
                own = jnp.where(lane == head, queries, jnp.zeros_like(queries))
                scores = lax.dot_general(
                    keys, own, (((1,), (1,)), ((), ())), preferred_element_type=F32
                )
                scores = jnp.where(key_index < TOKENS, scores, -1e30)
                highest = jnp.max(scores, axis=0, keepdims=True)
                weights = jnp.exp(scores - highest)
                total = jnp.sum(weights, axis=0, keepdims=True)
                total_ref[0, head : head + 1, low:high] = highest + jnp.log(total)
                mixed.append(
                    jnp.dot(values_turned, weights.astype(BF16), preferred_element_type=F32)
                    / total
                )
            out_ref[low:high] = jnp.where(feature == 0, mixed[0], mixed[1]).T.astype(BF16)

    return pl.pallas_call(
        kernel,
        grid=(last - first,),
        in_specs=[
            pl.BlockSpec((rows, 3 * PAIR), lambda p: (0, p + first)),
            *[pl.BlockSpec(memory_space=pl.ANY)] * len(so_far),
        ],
        input_output_aliases={1 + index: index for index in range(len(so_far))},
        out_specs=[
            pl.BlockSpec((rows, PAIR), lambda p: (0, p + first)),
            pl.BlockSpec((1, 2, rows), lambda p: (p + first, 0, 0)),
        ],
        out_shape=[
            jax.ShapeDtypeStruct((rows, pairs * PAIR), BF16),
            jax.ShapeDtypeStruct((pairs, 2, rows), F32),
        ],
        compiler_params=kernel_params(),
        cost_estimate=cost(
            16 * pairs * PAIR * rows * rows, 8 * rows * width, 2 * pairs * rows * rows
        ),
    )(triple, *so_far)


def attention_back(triple, totals, grad_mix, first, last, *so_far):
    rows, width = triple.shape
    pairs = width // (3 * PAIR)
    scale = HEAD_FEATURES ** (-0.5)

    def kernel(triple_ref, total_ref, grad_ref, *refs):
        out_ref, sum_ref, key_acc, value_acc = refs[-4:]
        lane = lax.broadcasted_iota(jnp.int32, (1, PAIR), 1) // HEAD_FEATURES
        feature = lax.broadcasted_iota(jnp.int32, (PAIR, 1), 0) // HEAD_FEATURES
        key_index = lax.broadcasted_iota(jnp.int32, (rows, 1), 0)
        keys = triple_ref[:, PAIR : 2 * PAIR]
        values = triple_ref[:, 2 * PAIR : 3 * PAIR]
        keys_turned = keys.T
        query_sums = [jnp.zeros((1, PAIR), F32), jnp.zeros((1, PAIR), F32)]
        for step, (low, high) in enumerate(row_chunks(rows)):
            queries = triple_ref[low:high, 0:PAIR] * jnp.asarray(scale, BF16)
            grads = grad_ref[low:high]
            turned = []
            for head in range(2):
                own = jnp.where(lane == head, queries, jnp.zeros_like(queries))
                own_grad = jnp.where(lane == head, grads, jnp.zeros_like(grads))
                scores = lax.dot_general(
                    keys, own, (((1,), (1,)), ((), ())), preferred_element_type=F32
                )
                soft = jnp.exp(scores - total_ref[0, head : head + 1, low:high])
                soft = jnp.where(key_index < TOKENS, soft, 0.0)
                grad_soft = lax.dot_general(
                    values, own_grad, (((1,), (1,)), ((), ())), preferred_element_type=F32
                )
                delta = jnp.sum(soft * grad_soft, axis=0, keepdims=True)
                score_round = (soft * (grad_soft - delta)).astype(BF16)
                turned.append(jnp.dot(keys_turned, score_round, preferred_element_type=F32))
                key_part = jnp.dot(score_round, own, preferred_element_type=F32)
                value_part = jnp.dot(soft.astype(BF16), own_grad, preferred_element_type=F32)
                if step == 0 and head == 0:
                    key_acc[...] = key_part
                    value_acc[...] = value_part
                else:
                    key_acc[...] += key_part
                    value_acc[...] += value_part
            grad_query = (jnp.where(feature == 0, turned[0], turned[1]) * scale).T
            out_ref[low:high, 0:PAIR] = grad_query.astype(BF16)
            stream = 0 if high <= IMAGE_TOKENS else 1
            query_sums[stream] += jnp.sum(grad_query, axis=0, keepdims=True)
        out_ref[:, PAIR : 2 * PAIR] = key_acc[...].astype(BF16)
        out_ref[:, 2 * PAIR : 3 * PAIR] = value_acc[...].astype(BF16)
        for stream, low, high in STREAM_ROWS:
            sum_ref[0, stream : stream + 1, 0:PAIR] = query_sums[stream]
            sum_ref[0, stream : stream + 1, PAIR : 2 * PAIR] = jnp.sum(
                value_acc[low:high], axis=0, keepdims=True
            )

    return pl.pallas_call(
        kernel,
        grid=(last - first,),
        in_specs=[
            pl.BlockSpec((rows, 3 * PAIR), lambda p: (0, p + first)),
            pl.BlockSpec((1, 2, rows), lambda p: (p + first, 0, 0)),
            pl.BlockSpec((rows, PAIR), lambda p: (0, p + first)),
            *[pl.BlockSpec(memory_space=pl.ANY)] * len(so_far),
        ],
        input_output_aliases={3 + index: index for index in range(len(so_far))},
        out_specs=[
            pl.BlockSpec((rows, 3 * PAIR), lambda p: (0, p + first)),
            pl.BlockSpec((1, 2, 2 * PAIR), lambda p: (p + first, 0, 0)),
        ],
        out_shape=[
            jax.ShapeDtypeStruct((rows, width), BF16),
            jax.ShapeDtypeStruct((pairs, 2, 2 * PAIR), F32),
        ],
        scratch_shapes=[pltpu.VMEM((rows, PAIR), F32), pltpu.VMEM((rows, PAIR), F32)],
        compiler_params=kernel_params(),
        cost_estimate=cost(
            40 * pairs * PAIR * rows * rows, 8 * rows * width, 2 * pairs * rows * rows
        ),
    )(triple, totals, grad_mix, *so_far)


def per_token(table):
    row = lax.broadcasted_iota(jnp.int32, (PADDED, 1), 0)
    return jnp.where(row < IMAGE_TOKENS, table[0][None], table[1][None])


def stream_sums(values):
    return jnp.stack([jnp.sum(values[low:high], axis=0) for _, low, high in STREAM_ROWS])


def row_stats(total, square):
    center = total / D
    return (center, lax.rsqrt(square / D - center * center + NORM_EPS))


def join_tokens(image, text):
    blank = jnp.zeros((PADDED - TOKENS, image.shape[2]), image.dtype)
    return jnp.concatenate([image[0], text[0], blank], axis=0)


def add_halves(kept, arrived):
    own, other = [one.astype(F32) + two.astype(F32) for one, two in zip(kept, arrived)]
    return (own, narrow(other))


def make_shards(row_count, col_count):
    order = list(range(0, row_count, 2)) + list(range(row_count - 1, 0, -2))
    place = [order.index(device) for device in range(row_count)]
    ahead = [(order[i], order[(i + 1) % row_count]) for i in range(row_count)]
    behind = [(target, sender) for sender, target in ahead]
    near = [(device, device ^ 1) for device in range(col_count)]
    far = [(device, device ^ 2) for device in range(col_count)]
    across = [(device, device ^ 3) for device in range(col_count)]
    share = row_count // col_count
    half_way = row_count // 2

    slots = [
        [
            [
                (row // share ^ col) * share + row % share
                for row in (order[(place[here] + offset) % row_count] for offset in range(row_count))
            ]
            for col in range(col_count)
        ]
        for here in range(row_count)
    ]

    class Order:
        def __init__(self):
            self.last = []

        def tie(self, *values):
            if self.last:
                values, _ = lax.optimization_barrier((values, tuple(self.last)))
            return values

        def mark(self, *values):
            self.last = list(values)

        def add(self, *values):
            self.last += values

        def run(self, step, *values):
            result = step(*self.tie(*values))
            self.mark(*jax.tree.leaves(result))
            return result

    class Swap:
        def __init__(self, steps, value, pairs):
            (value,) = steps.tie(value)
            self.steps = steps
            self.value = lax.ppermute(value, "cols", pairs)

        def land(self):
            (self.value,) = self.steps.tie(self.value)
            self.steps.mark(self.value)
            return self.value

    def shift_pairs(offset):
        return [(row, (row + offset) % row_count) for row in range(row_count)]

    def rotate(values, start):
        return lax.dynamic_slice_in_dim(
            jnp.concatenate([values, values]), start, values.shape[0], 0
        )

    class Ring:
        def __init__(self, order_of_steps, slot_row):
            self.steps = order_of_steps
            self.slot_row = slot_row
            self.hops = {1: half_way, -1: half_way}
            self.done = {1: 0, -1: 0}
            self.held = {}

        def send(self, way):
            (value,) = self.steps.tie(self.held[way])
            self.held[way] = lax.ppermute(value, "rows", ahead if way == 1 else behind)

        def land(self, way, value):
            self.held[way] = value
            self.done[way] += 1
            self.take(way)

        def left(self):
            return max(self.hops[way] - self.done[way] for way in (1, -1))

        def slot(self, offset):
            return self.slot_row[offset % row_count]

    class Lanes:
        def __init__(self):
            self.queue = {1: [], -1: []}
            self.flying = {}

        def push(self, ring, ahead_of=None):
            for way in (1, -1):
                queue = self.queue[way]
                place_at = queue.index(ahead_of) if ahead_of in queue else len(queue)
                queue[place_at:place_at] = [ring] * ring.hops[way]

        def tick(self):
            flying, self.flying = list(self.flying.items()), {}
            if flying:
                steps = flying[0][1].steps
                values = steps.tie(*[ring.held[way] for way, ring in flying])
                steps.mark(*values)
                for (way, ring), value in zip(flying, values):
                    ring.land(way, value)
            for way in (1, -1):
                if self.queue[way]:
                    self.flying[way] = self.queue[way].pop(0)
                    self.flying[way].send(way)

        def until(self, ring, left=0):
            while ring.left() > left:
                self.tick()

    class RingGather(Ring):
        def __init__(self, order_of_steps, slot_row, block):
            super().__init__(order_of_steps, slot_row)
            self.blocks = [block] * row_count
            self.halves = {}
            self.held = {1: block, -1: block}

        def take(self, way):
            if self.done[way] == half_way:
                self.halves[way] = self.held[way]
                return
            self.blocks[-way * self.done[way] % row_count] = self.held[way]
            if self.done[way] == half_way - 1:
                stream = 0 if way == 1 else 1
                self.held[way] = self.held[way][stream : stream + 1]

        def arrays(self):
            whole_blocks = self.blocks[:half_way] + self.blocks[half_way + 1 :]
            return [*whole_blocks, self.halves[1], self.halves[-1]]

    class RingScatter(Ring):
        def __init__(self, order_of_steps, slot_row, partial, long_way=None):
            super().__init__(order_of_steps, slot_row)
            self.partial = partial
            self.height = partial.shape[1] // row_count
            self.halved = long_way is None
            if self.halved:
                starts = (self.part(half_way, 0, 1), self.part(-half_way, 1, 1))
            else:
                self.hops[-long_way] -= 1
                starts = [self.part(way * self.hops[way]) for way in (1, -1)]
            starts = self.steps.tie(*starts)
            self.steps.mark(*starts)
            self.held = dict(zip((1, -1), starts))

        def part(self, offset, stream=0, streams=2):
            return lax.dynamic_slice(
                self.partial,
                (stream, self.slot(offset) * self.height, 0),
                (streams, self.height, self.partial.shape[2]),
            )

        def take(self, way):
            left = self.hops[way] - self.done[way]
            if not left:
                return
            own = self.part(way * left).astype(F32)
            arrived = self.held[way].astype(F32)
            if self.halved and self.done[way] == 1:
                stream = 0 if way == 1 else 1
                with_arrived = own[stream : stream + 1] + arrived
                other = own[1 - stream : 2 - stream]
                pair = (with_arrived, other) if stream == 0 else (other, with_arrived)
                self.held[way] = narrow(jnp.concatenate(pair))
            else:
                self.held[way] = narrow(own + arrived)
            self.steps.add(self.held[way])

    def shards(
        x_img,
        x_txt,
        cond,
        back_img,
        back_txt,
        w_mod,
        w_qkv,
        w_proj,
        w_up,
        w_down,
        biases,
        moments_mod,
        moments_qkv,
        moments_proj,
        moments_up,
        moments_down,
        moments_bias,
    ):
        local_rows = w_qkv.shape[0]
        width = w_qkv.shape[3]
        pairs = width // PAIR
        slot_row = lax.dynamic_slice(
            jnp.asarray(slots, jnp.int32),
            (lax.axis_index("rows"), lax.axis_index("cols"), 0),
            (1, 1, row_count),
        )[0, 0]
        slot_list = [slot_row[offset] for offset in range(row_count)]
        steps = Order()

        def gather(block):
            return RingGather(steps, slot_list, block)

        def scatter(partial, long_way=None):
            return RingScatter(steps, slot_list, partial, long_way)

        def update(kinds, ring, params, moments):
            return steps.run(
                lambda params, moments, *values: adam_rows(
                    kinds, params, moments, ring.slot(0).reshape(1), values[0], values[1:]
                ),
                params,
                moments,
                ring.partial,
                ring.held[1],
                ring.held[-1],
            )

        def far_swap(value):
            return Swap(steps, value, far)

        def near_swap(value):
            return Swap(steps, value, near)

        def send_around(value):
            return [value] + [Swap(steps, value, pairs) for pairs in (near, far, across)]

        def land_around(parts):
            return [parts[0]] + [part.land() for part in parts[1:]]

        def total_around(parts):
            one, two, three, four = land_around(parts)
            return (one + two) + (three + four)

        triple_span, attended_span, hidden_span = (
            (0, 3 * width),
            (3 * width, 4 * width),
            (0, 4 * width),
        )

        def run(step, acts, ring, span, *rest):
            return steps.run(
                lambda acts, *rest: step(acts, ring.arrays(), slot_row, span, *rest), acts, *rest
            )

        def weight_part(outer, inner, *rest):
            return steps.run(
                lambda a, b, *so_far: weight_gradient(a, b, 4 * width, *rest[:1], *so_far),
                outer,
                inner,
                *rest[1:],
            )

        def send_halves(acts, ring, span, between=lambda: None):
            leaving = run(lambda *args: matmul_back(*args, 1), acts, ring, span)
            between()
            arriving = [near_swap(half) for half in leaving]
            return run(lambda *args: matmul_back(*args, 0), acts, ring, span), arriving

        def send_away(kept, arriving):
            own, other = steps.run(add_halves, kept, [half.land() for half in arriving])
            return own, far_swap(other)

        def start_width(value):
            return (value, far_swap(value), near_swap(value))

        def middle_width(parts):
            return (*parts, near_swap(parts[1].land()))

        def end_width(parts):
            value, away, beside, diagonal = parts
            diagonal.land()
            beside.land()
            return jnp.concatenate(
                [value, beside.value, away.value, diagonal.value], axis=-1
            )

        lanes = Lanes()

        def queued(ring, ahead_of=None):
            lanes.push(ring, ahead_of)
            return ring

        ring_first = queued(
            gather(
                steps.run(
                    lambda *weights: travel_rows(("triple", "attended"), weights), w_qkv, w_proj
                )
            )
        )
        lanes.tick()
        silu_cond = narrow(jax.nn.silu(cond))
        mod_round = narrow(w_mod)
        mod_terms = steps.run(
            lambda rows, weight: jnp.einsum(
                "bd,dsic->bsic", rows, weight, preferred_element_type=F32
            ),
            silu_cond,
            mod_round,
        )
        mod_parts = lax.all_to_all(mod_terms, "rows", 0, 0, tiled=True)
        source_round = steps.run(join_tokens, x_img, x_txt)
        source_parts = start_width(source_round)
        steps.add(mod_parts)
        modulation = jnp.sum(mod_parts, axis=0) + biases[:, 0:6]
        mod_around = send_around(modulation)
        lanes.tick()
        modulation_full = jnp.concatenate(land_around(mod_around), axis=-1)
        source_parts = middle_width(source_parts)
        source_full = end_width(source_parts).astype(F32)
        scale_one, gate_one, scale_two, gate_two = [
            per_token(modulation[:, slot_index]) for slot_index in (1, 2, 4, 5)
        ]
        shift_two = per_token(modulation[:, 3])
        source = source_round.astype(F32)

        def first_norm(full, full_modulation):
            center, inverse = row_stats(
                jnp.sum(full, axis=1, keepdims=True),
                jnp.sum(full * full, axis=1, keepdims=True),
            )
            normed = narrow(
                (full - center) * inverse * (1.0 + per_token(full_modulation[:, 1]))
                + per_token(full_modulation[:, 0])
            )
            return center, inverse, normed

        center_one, inverse_one, normed_one = steps.run(first_norm, source_full, modulation_full)
        cotangent_round = steps.run(join_tokens, back_img, back_txt)
        cotangent = cotangent_round.astype(F32)
        unit_one = (source - center_one) * inverse_one
        lanes.tick()
        cotangent_parts = start_width(cotangent_round)
        ring_up = queued(
            gather(steps.run(lambda w: travel_rows(("hidden",), (w,)), w_up))
        )
        ring_down = queued(
            gather(steps.run(lambda w: travel_rows(("hidden",), (w,)), w_down))
        )
        lanes.tick()
        cotangent_parts = middle_width(cotangent_parts)
        lanes.until(ring_first)
        cotangent_full = end_width(cotangent_parts)
        triple_bias = (
            jnp.stack([biases[:, 6], jnp.zeros_like(biases[:, 6]), biases[:, 7]], axis=1)
            .reshape(2, 3, pairs, PAIR)
            .swapaxes(1, 2)
            .reshape(2, 3 * width)
        )
        triple = run(project_triple, normed_one, ring_first, triple_span, triple_bias)
        so_far = ()
        for pair in range(pairs):
            so_far = steps.run(
                lambda t, *rest, pair=pair: attention(t, pair, pair + 1, *rest), triple, *so_far
            )
            if pair == 0:
                lanes.tick()
        attended, log_totals = so_far
        halves = send_halves(attended, ring_first, attended_span, lanes.tick)
        own, away = send_away(*halves)
        lanes.tick()

        def residual_terms(own, away, source):
            projected = own + away.astype(F32) + per_token(biases[:, 8])
            residual = source + gate_one * projected
            sums = jnp.stack([jnp.sum(residual, axis=1), jnp.sum(residual * residual, axis=1)])
            return projected, residual, sums

        projected, residual, sums = steps.run(residual_terms, own, away.land(), source)
        sums_around = send_around(sums)
        lanes.tick()
        totals_two = total_around(sums_around)
        center_two, inverse_two = row_stats(totals_two[0][:, None], totals_two[1][:, None])
        unit_two = (residual - center_two) * inverse_two
        normed_own = narrow(unit_two * (1.0 + scale_two) + shift_two)
        steps.mark(normed_own)
        normed_parts = start_width(normed_own)
        lanes.tick()
        lanes.until(ring_up)
        lowered_full = steps.run(
            lambda full, gate: narrow(full.astype(F32) * per_token(gate)),
            cotangent_full,
            modulation_full[:, 5],
        )
        normed_two = end_width(middle_width(normed_parts))
        hidden_act, hidden_slope = run(
            raise_hidden, normed_two, ring_up, hidden_span, biases[:, 9:13].reshape(2, 4 * width)
        )
        lanes.tick()
        ring_grad_down = queued(
            scatter(weight_part(lowered_full, hidden_act), 1)
        )
        lanes.until(ring_down)
        hidden_round, hidden_sums = run(
            hidden_gradient, lowered_full, ring_down, hidden_span, hidden_slope
        )
        halves = send_halves(hidden_round, ring_up, hidden_span, lanes.tick)
        own, away = send_away(*halves)
        ring_grad_up = queued(
            scatter(weight_part(normed_two, hidden_round), -1)
        )
        lanes.tick()

        def back_sums(grad_unit, unit_rows):
            return jnp.stack([jnp.sum(grad_unit, axis=1), jnp.sum(grad_unit * unit_rows, axis=1)])

        def normalize_back(grad_unit, unit_rows, inverse, totals):
            return inverse * (
                grad_unit - totals[0][:, None] / D - unit_rows * (totals[1][:, None] / D)
            )

        grad_normed_two = own + away.land().astype(F32)
        grad_unit_two = grad_normed_two * (1.0 + scale_two)
        sums = back_sums(grad_unit_two, unit_two)
        steps.mark(sums)
        sums_around = send_around(sums)
        lanes.tick()
        totals = total_around(sums_around)
        grad_residual = cotangent + normalize_back(grad_unit_two, unit_two, inverse_two, totals)
        grad_projected = gate_one * grad_residual
        projected_own = narrow(grad_projected)
        steps.mark(projected_own)
        projected_parts = start_width(projected_own)
        lowered_leaving = run(
            lambda *args: matmul_back(*args, 1), hidden_act, ring_down, hidden_span
        )
        lowered_kept = run(
            lambda *args: matmul_back(*args, 0), hidden_act, ring_down, hidden_span
        )
        arriving = [near_swap(half) for half in lowered_leaving]
        lanes.tick()
        projected_full = end_width(middle_width(projected_parts))
        grad_attended = run(attended_gradient, projected_full, ring_first, attended_span)
        so_far = ()
        for pair in range(pairs):
            so_far = steps.run(
                lambda t, l, g, *rest, pair=pair: attention_back(t, l, g, pair, pair + 1, *rest),
                triple,
                log_totals,
                grad_attended,
                *so_far,
            )
            if pair == 0:
                own_lowered, away_lowered = send_away(lowered_kept, arriving)
                lanes.tick()
        lowered_away = away_lowered.land()
        lanes.tick()
        triple_round, triple_sums = so_far
        partial_first = weight_part(normed_one, triple_round, 0)
        partial_first = weight_part(projected_full, attended, 3 * width, partial_first)
        ring_grad_first = queued(scatter(partial_first), ring_grad_up)
        halves = send_halves(triple_round, ring_first, triple_span, lanes.tick)
        own, away = send_away(*halves)
        lanes.tick()
        ((next_down, grad_down, moved_down),) = update(
            ("hidden",), ring_grad_down, (w_down,), (moments_down,)
        )
        lanes.until(ring_grad_up)
        lowered = own_lowered + lowered_away.astype(F32) + per_token(biases[:, 13])
        grad_lowered = gate_two * cotangent
        grad_normed_one = own + away.land().astype(F32)
        grad_unit_one = grad_normed_one * (1.0 + scale_one)
        sums = back_sums(grad_unit_one, unit_one)
        steps.mark(sums)
        sums_around = send_around(sums)
        head_sums = triple_sums.reshape(pairs, 2, 2, PAIR).transpose(1, 2, 0, 3)
        part = jnp.concatenate(
            [
                stream_sums(grad_normed_one)[:, None],
                stream_sums(grad_normed_one * unit_one)[:, None],
                stream_sums(grad_residual * projected)[:, None],
                stream_sums(grad_normed_two)[:, None],
                stream_sums(grad_normed_two * unit_two)[:, None],
                stream_sums(cotangent * lowered)[:, None],
                head_sums.reshape(2, 2, width),
                stream_sums(grad_projected)[:, None],
                hidden_sums.reshape(2, 4, width),
                stream_sums(grad_lowered)[:, None],
            ],
            axis=1,
        )
        steps.mark(part)
        lanes.tick()
        (part,) = steps.tie(part)
        part_all = lax.all_to_all(
            jnp.broadcast_to(part[None], (row_count,) + part.shape), "rows", 0, 0, tiled=True
        )
        steps.mark(part_all)
        totals = total_around(sums_around)
        grad_source = grad_residual + normalize_back(grad_unit_one, unit_one, inverse_one, totals)
        steps.add(grad_source)
        table_round = narrow(part_all[:, :, 0:6])
        grad_bias = jnp.sum(part_all, axis=0)
        silu_terms = jnp.einsum("bsic,dsic->bd", table_round, mod_round, preferred_element_type=F32)
        steps.mark(silu_terms)
        silu_around = send_around(silu_terms)
        grad_silu = total_around(silu_around)
        sigmoid_cond = jax.nn.sigmoid(cond)
        grad_cond = grad_silu * sigmoid_cond * (1.0 + cond * (1.0 - sigmoid_cond))
        next_bias, first_bias, second_bias = adam_step(biases, moments_bias, grad_bias)
        steps.add(next_bias, first_bias, second_bias, grad_cond)
        ((next_up, grad_up, moved_up),) = update(
            ("hidden",), ring_grad_up, (w_up,), (moments_up,)
        )
        lanes.until(ring_grad_first, 1)
        own_lowered, lowered_away = steps.tie(own_lowered, lowered_away)
        output = narrow(
            residual
            + gate_two * (own_lowered + lowered_away.astype(F32) + per_token(biases[:, 13]))
        )
        steps.add(output, grad_source)
        next_mod, grad_mod, first_mod, second_mod = steps.run(
            adam_modulation, w_mod, moments_mod, silu_cond, table_round
        )
        lanes.until(ring_grad_first)
        (next_qkv, grad_qkv, moved_qkv), (next_proj, grad_proj, moved_proj) = update(
            ("triple", "attended"),
            ring_grad_first,
            (w_qkv, w_proj),
            (moments_qkv, moments_proj),
        )
        return (
            output[None, :IMAGE_TOKENS],
            output[None, IMAGE_TOKENS:TOKENS],
            grad_source[None, :IMAGE_TOKENS],
            grad_source[None, IMAGE_TOKENS:TOKENS],
            grad_cond,
            grad_mod,
            grad_qkv,
            grad_proj,
            grad_up,
            grad_down,
            grad_bias,
            next_mod,
            next_qkv,
            next_proj,
            next_up,
            next_down,
            next_bias,
            first_mod,
            second_mod,
            moved_qkv,
            moved_proj,
            moved_up,
            moved_down,
            first_bias,
            second_bias,
        )

    return shards


def solution(mesh):
    in_specs = (
        P("rows", None, "cols"),
        P("rows", None, "cols"),
        P(None, "rows"),
        P("rows", None, "cols"),
        P("rows", None, "cols"),
        P("rows", None, None, "cols"),
        P("rows", None, None, "cols"),
        P("rows", None, "cols"),
        P("rows", None, None, "cols"),
        P("rows", None, None, "cols"),
        P(None, None, "cols"),
        P(None, "rows", None, None, "cols"),
        P(None, "rows", None, None, "cols"),
        P(None, "rows", None, "cols"),
        P(None, "rows", None, None, "cols"),
        P(None, "rows", None, None, "cols"),
        P(None, None, None, "cols"),
    )
    out_specs = (
        P("rows", None, "cols"),
        P("rows", None, "cols"),
        P("rows", None, "cols"),
        P("rows", None, "cols"),
        P(None, "rows"),
        P("rows", None, None, "cols"),
        P("rows", None, None, "cols"),
        P("rows", None, "cols"),
        P("rows", None, None, "cols"),
        P("rows", None, None, "cols"),
        P(None, None, "cols"),
        P("rows", None, None, "cols"),
        P("rows", None, None, "cols"),
        P("rows", None, "cols"),
        P("rows", None, None, "cols"),
        P("rows", None, None, "cols"),
        P(None, None, "cols"),
        P("rows", None, None, "cols"),
        P("rows", None, None, "cols"),
        P(None, "rows", None, None, "cols"),
        P(None, "rows", None, "cols"),
        P(None, "rows", None, None, "cols"),
        P(None, "rows", None, None, "cols"),
        P(None, None, "cols"),
        P(None, None, "cols"),
    )
    shards = make_shards(mesh.shape["rows"], mesh.shape["cols"])
    return jax.shard_map(shards, mesh=mesh, in_specs=in_specs, out_specs=out_specs, check_vma=False)
```

```python
import jax
import jax.numpy as jnp
from jax import lax
from jax.experimental import pallas as pl
from jax.experimental.pallas import tpu as pltpu
from jax.sharding import PartitionSpec as P

D = 1536
HEAD_FEATURES = 64
IMAGE_TOKENS = 1024
TXT = 154
STEP = 2


BETA_ONE = 0.9
BETA_TWO = 0.95
LEARN_RATE = 0.02
DECAY_RATE = 0.1
ADAM_EPS = 1e-08
NORM_EPS = 1e-06
GELU_COEF = 0.7978845608028654
GELU_CUBE = 0.044715
PADDED = IMAGE_TOKENS + (TXT + 15) // 16 * 16
TOKENS = IMAGE_TOKENS + TXT
STREAM_ROWS = ((0, 0, IMAGE_TOKENS), (1, IMAGE_TOKENS, PADDED))
PAIR = 2 * HEAD_FEATURES
VMEM_BYTES = 56 * 1024 * 1024
F32 = jnp.float32
BF16 = jnp.bfloat16
COST_SHARE = 1000


def narrow(values):
    return values.astype(jnp.bfloat16)


def gelu_value(inputs):
    return (
        0.5 * inputs * (1.0 + jnp.tanh(GELU_COEF * (inputs + GELU_CUBE * inputs * inputs * inputs)))
    )


def gelu_slope(inputs):
    tangent = jnp.tanh(GELU_COEF * (inputs + GELU_CUBE * inputs * inputs * inputs))
    return 0.5 * (1.0 + tangent) + 0.5 * inputs * (1.0 - tangent * tangent) * GELU_COEF * (
        1.0 + 3.0 * GELU_CUBE * inputs * inputs
    )


def adam_step(param, moments, gradient):
    first_moment = BETA_ONE * moments[0] + (1.0 - BETA_ONE) * gradient
    second_moment = BETA_TWO * moments[1] + (1.0 - BETA_TWO) * gradient * gradient
    update = (
        first_moment
        / (1.0 - BETA_ONE**STEP)
        / (jnp.sqrt(second_moment / (1.0 - BETA_TWO**STEP)) + ADAM_EPS)
    )
    return (param - LEARN_RATE * (update + DECAY_RATE * param), first_moment, second_moment)


def rows_per_step(height):
    return 96 if height % 96 == 0 else 48


def pieces(kind, index):
    if kind == "triple":
        return [((3 * pair + index) * PAIR, pair * PAIR, PAIR) for pair in range(3)]
    if kind == "attended":
        return [(9 * PAIR, 0, 3 * PAIR)]
    return [(index * 3 * PAIR, 0, 3 * PAIR)]


def plane(kind, stream, index):
    return (stream, index) if kind == "hidden" else (index, stream)


def row_view(kind, weight):
    if kind == "attended":
        return jnp.expand_dims(weight, -3)
    return weight if kind == "hidden" else jnp.swapaxes(weight, -3, -2)


def row_unview(kind, weight):
    if kind == "attended":
        return jnp.squeeze(weight, -3)
    return weight if kind == "hidden" else jnp.swapaxes(weight, -3, -2)


def travel_rows(kinds, weights):
    views = [row_view(kind, weight) for kind, weight in zip(kinds, weights)]
    height = views[0].shape[0]
    step_rows = rows_per_step(height)

    def kernel(*refs):
        out_ref = refs[-1]
        for kind, ref in zip(kinds, refs):
            for stream in range(2):
                for index in range(ref.shape[1 if kind != "hidden" else 2]):
                    one, two = plane(kind, stream, index)
                    for there, here, size in pieces(kind, index):
                        out_ref[stream, :, there : there + size] = ref[
                            :, one, two, here : here + size
                        ].astype(BF16)

    total = 12 * PAIR
    return pl.pallas_call(
        kernel,
        grid=(height // step_rows,),
        in_specs=[
            pl.BlockSpec((step_rows, *view.shape[1:]), lambda i: (i, 0, 0, 0)) for view in views
        ],
        out_specs=pl.BlockSpec((2, step_rows, total), lambda i: (0, i, 0)),
        out_shape=jax.ShapeDtypeStruct((2, height, total), BF16),
        compiler_params=kernel_params(),
        cost_estimate=cost(2 * height * total, 12 * height * total),
    )(*views)


def adam_rows(kinds, params, moments, slot, partial, arrived):
    count = len(kinds)
    views = [row_view(kind, one) for kind, one in zip(kinds, params)]
    moment_views = [row_view(kind, one) for kind, one in zip(kinds, moments)]
    step_rows = rows_per_step(views[0].shape[0])
    parts = views[0].shape[0] // step_rows

    def kernel(slot_ref, *refs):
        param_refs, refs = refs[:count], refs[count:]
        moment_refs, refs = refs[:count], refs[count:]
        grad_refs, refs = refs[:3], refs[3:]
        for place, kind in enumerate(kinds):
            next_ref, grad_ref, moved_ref = refs[3 * place : 3 * place + 3]
            param_ref, moment_ref = param_refs[place], moment_refs[place]
            for stream in range(2):
                for index in range(param_ref.shape[2 if kind == "hidden" else 1]):
                    one, two = plane(kind, stream, index)
                    gradient = jnp.concatenate(
                        [
                            sum(
                                ref[stream, :, there : there + size].astype(F32)
                                for ref in grad_refs
                            )
                            for there, _, size in pieces(kind, index)
                        ],
                        axis=1,
                    )
                    result, first_moment, second_moment = adam_step(
                        param_ref[:, one, two],
                        (moment_ref[0, :, one, two], moment_ref[1, :, one, two]),
                        gradient,
                    )
                    next_ref[:, one, two] = result
                    grad_ref[:, one, two] = gradient
                    moved_ref[0, :, one, two] = first_moment
                    moved_ref[1, :, one, two] = second_moment

    param_specs = [
        pl.BlockSpec((step_rows, *view.shape[1:]), lambda i, slot: (i, 0, 0, 0)) for view in views
    ]
    moment_specs = [
        pl.BlockSpec((2, step_rows, *view.shape[1:]), lambda i, slot: (0, i, 0, 0, 0))
        for view in views
    ]
    total = partial.shape[2]
    grad_spec = pl.BlockSpec((2, step_rows, total), lambda i, slot: (0, i, 0))
    own_spec = pl.BlockSpec((2, step_rows, total), lambda i, slot: (0, slot[0] * parts + i, 0))
    out_specs, out_shape = [], []
    for place, view in enumerate(views):
        out_specs += [param_specs[place], param_specs[place], moment_specs[place]]
        out_shape += [
            jax.ShapeDtypeStruct(one.shape, F32) for one in (view, view, moment_views[place])
        ]
    size = sum(view.size for view in views)
    results = pl.pallas_call(
        kernel,
        grid_spec=pltpu.PrefetchScalarGridSpec(
            num_scalar_prefetch=1,
            grid=(parts,),
            in_specs=[*param_specs, *moment_specs, own_spec, grad_spec, grad_spec],
            out_specs=out_specs,
        ),
        out_shape=out_shape,
        compiler_params=kernel_params(),
        cost_estimate=cost(20 * size, 40 * size),
    )(slot, *views, *moment_views, partial, *arrived)
    return [
        [row_unview(kind, one) for one in results[3 * place : 3 * place + 3]]
        for place, kind in enumerate(kinds)
    ]


def adam_modulation(param, moments, rows, table):
    view, moment_view = (row_view("modulation", param), row_view("modulation", moments))
    height, count, streams, width = view.shape
    step_rows = rows_per_step(height)
    turned = jnp.swapaxes(table, 1, 2).reshape(table.shape[0], count * streams * width)

    def kernel(rows_ref, table_ref, param_ref, moment_ref, next_ref, grad_ref, *moved_refs):
        for index in range(count):
            for stream in range(streams):
                low = (index * streams + stream) * width
                gradient = jnp.dot(
                    rows_ref[...], table_ref[:, low : low + width], preferred_element_type=F32
                )
                result, first_moment, second_moment = adam_step(
                    param_ref[:, index, stream],
                    (moment_ref[0, :, index, stream], moment_ref[1, :, index, stream]),
                    gradient,
                )
                next_ref[:, index, stream] = result
                grad_ref[:, index, stream] = gradient
                moved_refs[0][:, index, stream] = first_moment
                moved_refs[1][:, index, stream] = second_moment

    param_spec = pl.BlockSpec((step_rows, count, streams, width), lambda i: (i, 0, 0, 0))
    moment_spec = pl.BlockSpec((2, step_rows, count, streams, width), lambda i: (0, i, 0, 0, 0))
    shape = jax.ShapeDtypeStruct(view.shape, F32)
    results = pl.pallas_call(
        kernel,
        grid=(height // step_rows,),
        in_specs=[
            pl.BlockSpec((step_rows, rows.shape[0]), lambda i: (i, 0)),
            whole(turned.shape),
            param_spec,
            moment_spec,
        ],
        out_specs=[param_spec] * 4,
        out_shape=[shape] * 4,
        compiler_params=kernel_params(),
        cost_estimate=cost(20 * view.size, 40 * view.size),
    )(rows.T, turned, view, moment_view)
    return [row_unview("modulation", one) for one in results]


def kernel_params():
    return pltpu.CompilerParams(vmem_limit_bytes=VMEM_BYTES)


def cost(flops, nbytes, transcendentals=0):
    return pl.CostEstimate(flops=flops // COST_SHARE, bytes_accessed=nbytes // COST_SHARE, transcendentals=transcendentals)


def whole(shape):
    return pl.BlockSpec(shape, lambda j: (0,) * len(shape))


def arrivals_of(refs):
    count = len(refs) - 1
    half_way = count // 2
    offsets = [offset for offset in range(count) if offset != half_way]
    moves = [(offset, ref, 0, 2) for offset, ref in zip(offsets, refs)]
    return moves + [(half_way, refs[-2], 0, 1), (half_way, refs[-1], 1, 1)]


def matmul_rows(acts, blocks, slots, span, epilogue, extras, extra_specs, out_types, out_specs):
    rows, depth = acts.shape
    count = len(blocks)
    height = blocks[0].shape[1]
    first, width = (span[0], span[1] - span[0])
    tile = 384
    tiles = width // tile

    def kernel(slots_ref, acts_ref, *refs):
        block_refs, refs = refs[:count], refs[count:]
        refs, weight, arrivals = refs[:-2], refs[-2], refs[-1]

        moves = arrivals_of(block_refs)

        def copy(index, part):
            offset, ref, stream, streams = moves[index]
            row = pl.multiple_of(slots_ref[offset] * height, height)
            return pltpu.make_async_copy(
                ref.at[:, :, pl.ds(first + part * tile, tile)],
                weight.at[part, pl.ds(stream, streams), pl.ds(row, height), :],
                arrivals.at[part, index],
            )

        step = pl.program_id(0)

        @pl.when(step == 0)
        def _():
            for part in range(tiles):
                for index in range(count):
                    copy(index, part).start()

        for part in range(tiles):

            @pl.when(step == part)
            def _():
                for index in range(count):
                    copy(index, part).wait()

        for stream, low, high in STREAM_ROWS:
            product = jnp.dot(
                acts_ref[low:high], weight[step, stream], preferred_element_type=F32
            )
            epilogue(product, stream, low, high, *refs)

    return pl.pallas_call(
        kernel,
        grid=(tiles,),
        in_specs=[
            pl.BlockSpec(memory_space=pltpu.SMEM),
            whole((rows, depth)),
            *[pl.BlockSpec(memory_space=pl.ANY)] * count,
            *extra_specs,
        ],
        out_specs=out_specs,
        out_shape=out_types,
        scratch_shapes=[
            pltpu.VMEM((tiles, 2, depth, tile), BF16),
            pltpu.SemaphoreType.DMA((tiles, count)),
        ],
        compiler_params=kernel_params(),
        cost_estimate=cost(
            2 * rows * depth * width, 2 * (rows * depth + 2 * depth * width + rows * width)
        ),
    )(slots, acts, *blocks, *extras)


def column_spec(leading, tile=384):
    return pl.BlockSpec((leading, tile), lambda j: (0, j))


def project_triple(acts, blocks, slots, span, bias):
    def epilogue(product, stream, low, high, bias_ref, out_ref):
        out_ref[low:high] = (product + bias_ref[stream : stream + 1]).astype(BF16)

    rows, width = (acts.shape[0], span[1] - span[0])
    return matmul_rows(
        acts,
        blocks,
        slots,
        span,
        epilogue,
        [bias],
        [column_spec(2)],
        jax.ShapeDtypeStruct((rows, width), BF16),
        column_spec(rows),
    )


def raise_hidden(acts, blocks, slots, span, bias):
    def epilogue(product, stream, low, high, bias_ref, act_ref, slope_ref):
        inputs = product + bias_ref[stream : stream + 1]
        square = inputs * inputs
        tangent = jnp.tanh(GELU_COEF * inputs * (1.0 + GELU_CUBE * square))
        act_ref[low:high] = (0.5 * inputs * (1.0 + tangent)).astype(BF16)
        slope_ref[low:high] = 0.5 * (1.0 + tangent) + 0.5 * inputs * (
            1.0 - tangent * tangent
        ) * GELU_COEF * (1.0 + 3.0 * GELU_CUBE * square)

    rows, width = (acts.shape[0], span[1] - span[0])
    return matmul_rows(
        acts,
        blocks,
        slots,
        span,
        epilogue,
        [bias],
        [column_spec(2)],
        [jax.ShapeDtypeStruct((rows, width), BF16), jax.ShapeDtypeStruct((rows, width), F32)],
        [column_spec(rows), column_spec(rows)],
    )


def hidden_gradient(acts, blocks, slots, span, slope):
    def epilogue(product, stream, low, high, slope_ref, out_ref, sum_ref):
        gradient = product * slope_ref[low:high]
        out_ref[low:high] = gradient.astype(BF16)
        sum_ref[stream : stream + 1] = jnp.sum(gradient, axis=0, keepdims=True)

    rows, width = (acts.shape[0], span[1] - span[0])
    return matmul_rows(
        acts,
        blocks,
        slots,
        span,
        epilogue,
        [slope],
        [column_spec(rows)],
        [jax.ShapeDtypeStruct((rows, width), BF16), jax.ShapeDtypeStruct((2, width), F32)],
        [column_spec(rows), column_spec(2)],
    )


def attended_gradient(acts, blocks, slots, span):
    def epilogue(product, stream, low, high, out_ref):
        out_ref[low:high] = product.astype(BF16)

    rows, width = (acts.shape[0], span[1] - span[0])
    return matmul_rows(
        acts,
        blocks,
        slots,
        span,
        epilogue,
        [],
        [],
        jax.ShapeDtypeStruct((rows, width), BF16),
        column_spec(rows),
    )


def matmul_back(acts, blocks, slots, span, parity):
    rows, depth = acts.shape
    count = len(blocks)
    height = blocks[0].shape[1]
    share = (count - 1) // 4
    tile = share * height

    def kernel(slots_ref, acts_ref, *refs):
        block_refs, (*out_refs, weight, arrivals) = refs[:count], refs[count:]

        moves = arrivals_of(block_refs)

        def copy(index):
            offset, ref, stream, streams = moves[index]
            slot = slots_ref[offset]
            row = pl.multiple_of(slot % share * height, height)
            return pltpu.make_async_copy(
                ref.at[:, :, pl.ds(span[0], depth)],
                weight.at[slot // share // 2, pl.ds(stream, streams), pl.ds(row, height), :],
                arrivals.at[index],
            )

        def each(action, wanted):
            for index in range(count):
                pl.when(wanted(slots_ref[moves[index][0]] // share))(
                    lambda index=index: action(copy(index))
                )

        step = pl.program_id(0)

        @pl.when(step == 0)
        def _():
            for part in range(2):
                each(lambda job: job.start(), lambda group: group == 2 * part + parity)

        each(lambda job: job.wait(), lambda group: group == 2 * step + parity)
        for part, out_ref in enumerate(out_refs):

            @pl.when(step == part)
            def _():
                for stream, low, high in STREAM_ROWS:
                    out_ref[low:high] = lax.dot_general(
                        acts_ref[low:high],
                        weight[part, stream],
                        (((1,), (1,)), ((), ())),
                        preferred_element_type=F32,
                    ).astype(BF16)

    return pl.pallas_call(
        kernel,
        grid=(2,),
        in_specs=[
            pl.BlockSpec(memory_space=pltpu.SMEM),
            whole((rows, depth)),
            *[pl.BlockSpec(memory_space=pl.ANY)] * count,
        ],
        out_specs=[whole((rows, tile))] * 2,
        out_shape=[jax.ShapeDtypeStruct((rows, tile), BF16)] * 2,
        scratch_shapes=[
            pltpu.VMEM((2, 2, tile, depth), BF16),
            pltpu.SemaphoreType.DMA((count,)),
        ],
        compiler_params=kernel_params(),
        cost_estimate=cost(
            4 * rows * depth * tile, 2 * (rows * depth + 4 * depth * tile + 2 * rows * tile)
        ),
    )(slots, acts, *blocks)


def weight_gradient(outer, inner, full_width, first=0, *so_far, tile=384):
    rows, height = outer.shape
    width = inner.shape[1]

    def kernel(outer_ref, inner_ref, *refs):
        out_ref = refs[-1]
        for stream, low, high in STREAM_ROWS:
            out_ref[stream] = lax.dot_general(
                outer_ref[low:high],
                inner_ref[low:high],
                (((0,), (0,)), ((), ())),
                preferred_element_type=F32,
            ).astype(BF16)

    return pl.pallas_call(
        kernel,
        grid=(height // tile,),
        in_specs=[
            column_spec(rows, tile),
            whole((rows, width)),
            *[pl.BlockSpec(memory_space=pl.ANY)] * len(so_far),
        ],
        out_specs=pl.BlockSpec((2, tile, width), lambda j: (0, j, first // width)),
        out_shape=jax.ShapeDtypeStruct((2, height, full_width), BF16),
        input_output_aliases={2 + index: index for index in range(len(so_far))},
        compiler_params=kernel_params(),
        cost_estimate=cost(
            2 * rows * height * width, 2 * (rows * height + rows * width + 2 * height * width)
        ),
    )(outer, inner, *so_far)


def row_chunks(rows, size=256):
    return [(low, min(low + size, rows)) for low in range(0, rows, size)]


def attention(triple, first, last, *so_far):
    rows, width = triple.shape
    pairs = width // (3 * PAIR)
    scale = HEAD_FEATURES ** (-0.5)

    def kernel(triple_ref, *refs):
        out_ref, total_ref = refs[-2:]
        lane = lax.broadcasted_iota(jnp.int32, (1, PAIR), 1) // HEAD_FEATURES
        feature = lax.broadcasted_iota(jnp.int32, (PAIR, 1), 0) // HEAD_FEATURES
        key_index = lax.broadcasted_iota(jnp.int32, (rows, 1), 0)
        keys = triple_ref[:, PAIR : 2 * PAIR]
        values_turned = triple_ref[:, 2 * PAIR : 3 * PAIR].T
        for low, high in row_chunks(rows):
            queries = triple_ref[low:high, 0:PAIR] * jnp.asarray(scale, BF16)
            mixed = []
            for head in range(2):
                own = jnp.where(lane == head, queries, jnp.zeros_like(queries))
                scores = lax.dot_general(
                    keys, own, (((1,), (1,)), ((), ())), preferred_element_type=F32
                )
                scores = jnp.where(key_index < TOKENS, scores, -1e30)
                highest = jnp.max(scores, axis=0, keepdims=True)
                weights = jnp.exp(scores - highest)
                total = jnp.sum(weights, axis=0, keepdims=True)
                total_ref[0, head : head + 1, low:high] = highest + jnp.log(total)
                mixed.append(
                    jnp.dot(values_turned, weights.astype(BF16), preferred_element_type=F32)
                    / total
                )
            out_ref[low:high] = jnp.where(feature == 0, mixed[0], mixed[1]).T.astype(BF16)

    return pl.pallas_call(
        kernel,
        grid=(last - first,),
        in_specs=[
            pl.BlockSpec((rows, 3 * PAIR), lambda p: (0, p + first)),
            *[pl.BlockSpec(memory_space=pl.ANY)] * len(so_far),
        ],
        input_output_aliases={1 + index: index for index in range(len(so_far))},
        out_specs=[
            pl.BlockSpec((rows, PAIR), lambda p: (0, p + first)),
            pl.BlockSpec((1, 2, rows), lambda p: (p + first, 0, 0)),
        ],
        out_shape=[
            jax.ShapeDtypeStruct((rows, pairs * PAIR), BF16),
            jax.ShapeDtypeStruct((pairs, 2, rows), F32),
        ],
        compiler_params=kernel_params(),
        cost_estimate=cost(
            16 * pairs * PAIR * rows * rows, 8 * rows * width, 2 * pairs * rows * rows
        ),
    )(triple, *so_far)


def attention_back(triple, totals, grad_mix, first, last, *so_far):
    rows, width = triple.shape
    pairs = width // (3 * PAIR)
    scale = HEAD_FEATURES ** (-0.5)

    def kernel(triple_ref, total_ref, grad_ref, *refs):
        out_ref, sum_ref, key_acc, value_acc = refs[-4:]
        lane = lax.broadcasted_iota(jnp.int32, (1, PAIR), 1) // HEAD_FEATURES
        feature = lax.broadcasted_iota(jnp.int32, (PAIR, 1), 0) // HEAD_FEATURES
        key_index = lax.broadcasted_iota(jnp.int32, (rows, 1), 0)
        keys = triple_ref[:, PAIR : 2 * PAIR]
        values = triple_ref[:, 2 * PAIR : 3 * PAIR]
        keys_turned = keys.T
        query_sums = [jnp.zeros((1, PAIR), F32), jnp.zeros((1, PAIR), F32)]
        for step, (low, high) in enumerate(row_chunks(rows)):
            queries = triple_ref[low:high, 0:PAIR] * jnp.asarray(scale, BF16)
            grads = grad_ref[low:high]
            turned = []
            for head in range(2):
                own = jnp.where(lane == head, queries, jnp.zeros_like(queries))
                own_grad = jnp.where(lane == head, grads, jnp.zeros_like(grads))
                scores = lax.dot_general(
                    keys, own, (((1,), (1,)), ((), ())), preferred_element_type=F32
                )
                soft = jnp.exp(scores - total_ref[0, head : head + 1, low:high])
                soft = jnp.where(key_index < TOKENS, soft, 0.0)
                grad_soft = lax.dot_general(
                    values, own_grad, (((1,), (1,)), ((), ())), preferred_element_type=F32
                )
                delta = jnp.sum(soft * grad_soft, axis=0, keepdims=True)
                score_round = (soft * (grad_soft - delta)).astype(BF16)
                turned.append(jnp.dot(keys_turned, score_round, preferred_element_type=F32))
                key_part = jnp.dot(score_round, own, preferred_element_type=F32)
                value_part = jnp.dot(soft.astype(BF16), own_grad, preferred_element_type=F32)
                if step == 0 and head == 0:
                    key_acc[...] = key_part
                    value_acc[...] = value_part
                else:
                    key_acc[...] += key_part
                    value_acc[...] += value_part
            grad_query = (jnp.where(feature == 0, turned[0], turned[1]) * scale).T
            out_ref[low:high, 0:PAIR] = grad_query.astype(BF16)
            stream = 0 if high <= IMAGE_TOKENS else 1
            query_sums[stream] += jnp.sum(grad_query, axis=0, keepdims=True)
        out_ref[:, PAIR : 2 * PAIR] = key_acc[...].astype(BF16)
        out_ref[:, 2 * PAIR : 3 * PAIR] = value_acc[...].astype(BF16)
        for stream, low, high in STREAM_ROWS:
            sum_ref[0, stream : stream + 1, 0:PAIR] = query_sums[stream]
            sum_ref[0, stream : stream + 1, PAIR : 2 * PAIR] = jnp.sum(
                value_acc[low:high], axis=0, keepdims=True
            )

    return pl.pallas_call(
        kernel,
        grid=(last - first,),
        in_specs=[
            pl.BlockSpec((rows, 3 * PAIR), lambda p: (0, p + first)),
            pl.BlockSpec((1, 2, rows), lambda p: (p + first, 0, 0)),
            pl.BlockSpec((rows, PAIR), lambda p: (0, p + first)),
            *[pl.BlockSpec(memory_space=pl.ANY)] * len(so_far),
        ],
        input_output_aliases={3 + index: index for index in range(len(so_far))},
        out_specs=[
            pl.BlockSpec((rows, 3 * PAIR), lambda p: (0, p + first)),
            pl.BlockSpec((1, 2, 2 * PAIR), lambda p: (p + first, 0, 0)),
        ],
        out_shape=[
            jax.ShapeDtypeStruct((rows, width), BF16),
            jax.ShapeDtypeStruct((pairs, 2, 2 * PAIR), F32),
        ],
        scratch_shapes=[pltpu.VMEM((rows, PAIR), F32), pltpu.VMEM((rows, PAIR), F32)],
        compiler_params=kernel_params(),
        cost_estimate=cost(
            40 * pairs * PAIR * rows * rows, 8 * rows * width, 2 * pairs * rows * rows
        ),
    )(triple, totals, grad_mix, *so_far)


def per_token(table):
    row = lax.broadcasted_iota(jnp.int32, (PADDED, 1), 0)
    return jnp.where(row < IMAGE_TOKENS, table[0][None], table[1][None])


def stream_sums(values):
    return jnp.stack([jnp.sum(values[low:high], axis=0) for _, low, high in STREAM_ROWS])


def row_stats(total, square):
    center = total / D
    return (center, lax.rsqrt(square / D - center * center + NORM_EPS))


def join_tokens(image, text):
    blank = jnp.zeros((PADDED - TOKENS, image.shape[2]), image.dtype)
    return jnp.concatenate([image[0], text[0], blank], axis=0)


def add_halves(kept, arrived):
    own, other = [one.astype(F32) + two.astype(F32) for one, two in zip(kept, arrived)]
    return (own, narrow(other))


def make_shards(row_count, col_count):
    order = list(range(0, row_count, 2)) + list(range(row_count - 1, 0, -2))
    place = [order.index(device) for device in range(row_count)]
    ahead = [(order[i], order[(i + 1) % row_count]) for i in range(row_count)]
    behind = [(target, sender) for sender, target in ahead]
    near = [(device, device ^ 1) for device in range(col_count)]
    far = [(device, device ^ 2) for device in range(col_count)]
    across = [(device, device ^ 3) for device in range(col_count)]
    share = row_count // col_count
    half_way = row_count // 2

    slots = [
        [
            [
                (row // share ^ col) * share + row % share
                for row in (order[(place[here] + offset) % row_count] for offset in range(row_count))
            ]
            for col in range(col_count)
        ]
        for here in range(row_count)
    ]

    class Order:
        def __init__(self):
            self.last = []

        def tie(self, *values):
            if self.last:
                values, _ = lax.optimization_barrier((values, tuple(self.last)))
            return values

        def mark(self, *values):
            self.last = list(values)

        def add(self, *values):
            self.last += values

        def run(self, step, *values):
            result = step(*self.tie(*values))
            self.mark(*jax.tree.leaves(result))
            return result

    class Swap:
        def __init__(self, steps, value, pairs):
            (value,) = steps.tie(value)
            self.steps = steps
            self.value = lax.ppermute(value, "cols", pairs)

        def land(self):
            (self.value,) = self.steps.tie(self.value)
            self.steps.mark(self.value)
            return self.value

    def shift_pairs(offset):
        return [(row, (row + offset) % row_count) for row in range(row_count)]

    def rotate(values, start):
        return lax.dynamic_slice_in_dim(
            jnp.concatenate([values, values]), start, values.shape[0], 0
        )

    class Ring:
        def __init__(self, order_of_steps, slot_row):
            self.steps = order_of_steps
            self.slot_row = slot_row
            self.hops = {1: half_way, -1: half_way}
            self.done = {1: 0, -1: 0}
            self.held = {}

        def send(self, way):
            (value,) = self.steps.tie(self.held[way])
            self.held[way] = lax.ppermute(value, "rows", ahead if way == 1 else behind)

        def land(self, way, value):
            self.held[way] = value
            self.done[way] += 1
            self.take(way)

        def left(self):
            return max(self.hops[way] - self.done[way] for way in (1, -1))

        def slot(self, offset):
            return self.slot_row[offset % row_count]

    class Lanes:
        def __init__(self):
            self.queue = {1: [], -1: []}
            self.flying = {}

        def push(self, ring, ahead_of=None):
            for way in (1, -1):
                queue = self.queue[way]
                place_at = queue.index(ahead_of) if ahead_of in queue else len(queue)
                queue[place_at:place_at] = [ring] * ring.hops[way]

        def tick(self):
            flying, self.flying = list(self.flying.items()), {}
            if flying:
                steps = flying[0][1].steps
                values = steps.tie(*[ring.held[way] for way, ring in flying])
                steps.mark(*values)
                for (way, ring), value in zip(flying, values):
                    ring.land(way, value)
            for way in (1, -1):
                if self.queue[way]:
                    self.flying[way] = self.queue[way].pop(0)
                    self.flying[way].send(way)

        def until(self, ring, left=0):
            while ring.left() > left:
                self.tick()

    class RingGather(Ring):
        def __init__(self, order_of_steps, slot_row, block):
            super().__init__(order_of_steps, slot_row)
            self.blocks = [block] * row_count
            self.halves = {}
            self.held = {1: block, -1: block}

        def take(self, way):
            if self.done[way] == half_way:
                self.halves[way] = self.held[way]
                return
            self.blocks[-way * self.done[way] % row_count] = self.held[way]
            if self.done[way] == half_way - 1:
                stream = 0 if way == 1 else 1
                self.held[way] = self.held[way][stream : stream + 1]

        def arrays(self):
            whole_blocks = self.blocks[:half_way] + self.blocks[half_way + 1 :]
            return [*whole_blocks, self.halves[1], self.halves[-1]]

    class RingScatter(Ring):
        def __init__(self, order_of_steps, slot_row, partial, long_way=None):
            super().__init__(order_of_steps, slot_row)
            self.partial = partial
            self.height = partial.shape[1] // row_count
            self.halved = long_way is None
            if self.halved:
                starts = (self.part(half_way, 0, 1), self.part(-half_way, 1, 1))
            else:
                self.hops[-long_way] -= 1
                starts = [self.part(way * self.hops[way]) for way in (1, -1)]
            starts = self.steps.tie(*starts)
            self.steps.mark(*starts)
            self.held = dict(zip((1, -1), starts))

        def part(self, offset, stream=0, streams=2):
            return lax.dynamic_slice(
                self.partial,
                (stream, self.slot(offset) * self.height, 0),
                (streams, self.height, self.partial.shape[2]),
            )

        def take(self, way):
            left = self.hops[way] - self.done[way]
            if not left:
                return
            own = self.part(way * left).astype(F32)
            arrived = self.held[way].astype(F32)
            if self.halved and self.done[way] == 1:
                stream = 0 if way == 1 else 1
                with_arrived = own[stream : stream + 1] + arrived
                other = own[1 - stream : 2 - stream]
                pair = (with_arrived, other) if stream == 0 else (other, with_arrived)
                self.held[way] = narrow(jnp.concatenate(pair))
            else:
                self.held[way] = narrow(own + arrived)
            self.steps.add(self.held[way])

    def shards(
        x_img,
        x_txt,
        cond,
        back_img,
        back_txt,
        w_mod,
        w_qkv,
        w_proj,
        w_up,
        w_down,
        biases,
        moments_mod,
        moments_qkv,
        moments_proj,
        moments_up,
        moments_down,
        moments_bias,
    ):
        local_rows = w_qkv.shape[0]
        width = w_qkv.shape[3]
        pairs = width // PAIR
        slot_row = lax.dynamic_slice(
            jnp.asarray(slots, jnp.int32),
            (lax.axis_index("rows"), lax.axis_index("cols"), 0),
            (1, 1, row_count),
        )[0, 0]
        slot_list = [slot_row[offset] for offset in range(row_count)]
        steps = Order()

        def gather(block):
            return RingGather(steps, slot_list, block)

        def scatter(partial, long_way=None):
            return RingScatter(steps, slot_list, partial, long_way)

        def update(kinds, ring, params, moments):
            return steps.run(
                lambda params, moments, *values: adam_rows(
                    kinds, params, moments, ring.slot(0).reshape(1), values[0], values[1:]
                ),
                params,
                moments,
                ring.partial,
                ring.held[1],
                ring.held[-1],
            )

        def far_swap(value):
            return Swap(steps, value, far)

        def near_swap(value):
            return Swap(steps, value, near)

        def send_around(value):
            return [value] + [Swap(steps, value, pairs) for pairs in (near, far, across)]

        def land_around(parts):
            return [parts[0]] + [part.land() for part in parts[1:]]

        def total_around(parts):
            one, two, three, four = land_around(parts)
            return (one + two) + (three + four)

        triple_span, attended_span, hidden_span = (
            (0, 3 * width),
            (3 * width, 4 * width),
            (0, 4 * width),
        )

        def run(step, acts, ring, span, *rest):
            return steps.run(
                lambda acts, *rest: step(acts, ring.arrays(), slot_row, span, *rest), acts, *rest
            )

        def weight_part(outer, inner, *rest):
            return steps.run(
                lambda a, b, *so_far: weight_gradient(a, b, 4 * width, *rest[:1], *so_far),
                outer,
                inner,
                *rest[1:],
            )

        def send_halves(acts, ring, span, between=lambda: None):
            leaving = run(lambda *args: matmul_back(*args, 1), acts, ring, span)
            between()
            arriving = [near_swap(half) for half in leaving]
            return run(lambda *args: matmul_back(*args, 0), acts, ring, span), arriving

        def send_away(kept, arriving):
            own, other = steps.run(add_halves, kept, [half.land() for half in arriving])
            return own, far_swap(other)

        def start_width(value):
            return (value, far_swap(value), near_swap(value))

        def middle_width(parts):
            return (*parts, near_swap(parts[1].land()))

        def end_width(parts):
            value, away, beside, diagonal = parts
            diagonal.land()
            beside.land()
            return jnp.concatenate(
                [value, beside.value, away.value, diagonal.value], axis=-1
            )

        lanes = Lanes()

        def queued(ring, ahead_of=None):
            lanes.push(ring, ahead_of)
            return ring

        ring_first = queued(
            gather(
                steps.run(
                    lambda *weights: travel_rows(("triple", "attended"), weights), w_qkv, w_proj
                )
            )
        )
        lanes.tick()
        silu_cond = narrow(jax.nn.silu(cond))
        mod_round = narrow(w_mod)
        mod_terms = steps.run(
            lambda rows, weight: jnp.einsum(
                "bd,dsic->bsic", rows, weight, preferred_element_type=F32
            ),
            silu_cond,
            mod_round,
        )
        mod_parts = lax.all_to_all(mod_terms, "rows", 0, 0, tiled=True)
        source_round = steps.run(join_tokens, x_img, x_txt)
        source_parts = start_width(source_round)
        steps.add(mod_parts)
        modulation = jnp.sum(mod_parts, axis=0) + biases[:, 0:6]
        mod_around = send_around(modulation)
        lanes.tick()
        modulation_full = jnp.concatenate(land_around(mod_around), axis=-1)
        source_parts = middle_width(source_parts)
        source_full = end_width(source_parts).astype(F32)
        scale_one, gate_one, scale_two, gate_two = [
            per_token(modulation[:, slot_index]) for slot_index in (1, 2, 4, 5)
        ]
        shift_two = per_token(modulation[:, 3])
        source = source_round.astype(F32)

        def first_norm(full, full_modulation):
            center, inverse = row_stats(
                jnp.sum(full, axis=1, keepdims=True),
                jnp.sum(full * full, axis=1, keepdims=True),
            )
            normed = narrow(
                (full - center) * inverse * (1.0 + per_token(full_modulation[:, 1]))
                + per_token(full_modulation[:, 0])
            )
            return center, inverse, normed

        center_one, inverse_one, normed_one = steps.run(first_norm, source_full, modulation_full)
        cotangent_round = steps.run(join_tokens, back_img, back_txt)
        cotangent = cotangent_round.astype(F32)
        unit_one = (source - center_one) * inverse_one
        lanes.tick()
        cotangent_parts = start_width(cotangent_round)
        ring_up = queued(
            gather(steps.run(lambda w: travel_rows(("hidden",), (w,)), w_up))
        )
        ring_down = queued(
            gather(steps.run(lambda w: travel_rows(("hidden",), (w,)), w_down))
        )
        lanes.tick()
        cotangent_parts = middle_width(cotangent_parts)
        lanes.until(ring_first)
        cotangent_full = end_width(cotangent_parts)
        triple_bias = (
            jnp.stack([biases[:, 6], jnp.zeros_like(biases[:, 6]), biases[:, 7]], axis=1)
            .reshape(2, 3, pairs, PAIR)
            .swapaxes(1, 2)
            .reshape(2, 3 * width)
        )
        triple = run(project_triple, normed_one, ring_first, triple_span, triple_bias)
        so_far = ()
        for pair in range(pairs):
            so_far = steps.run(
                lambda t, *rest, pair=pair: attention(t, pair, pair + 1, *rest), triple, *so_far
            )
            if pair == 0:
                lanes.tick()
        attended, log_totals = so_far
        halves = send_halves(attended, ring_first, attended_span, lanes.tick)
        own, away = send_away(*halves)
        lanes.tick()

        def residual_terms(own, away, source):
            projected = own + away.astype(F32) + per_token(biases[:, 8])
            residual = source + gate_one * projected
            sums = jnp.stack([jnp.sum(residual, axis=1), jnp.sum(residual * residual, axis=1)])
            return projected, residual, sums

        projected, residual, sums = steps.run(residual_terms, own, away.land(), source)
        sums_around = send_around(sums)
        lanes.tick()
        totals_two = total_around(sums_around)
        center_two, inverse_two = row_stats(totals_two[0][:, None], totals_two[1][:, None])
        unit_two = (residual - center_two) * inverse_two
        normed_own = narrow(unit_two * (1.0 + scale_two) + shift_two)
        steps.mark(normed_own)
        normed_parts = start_width(normed_own)
        lanes.tick()
        lanes.until(ring_up)
        lowered_full = steps.run(
            lambda full, gate: narrow(full.astype(F32) * per_token(gate)),
            cotangent_full,
            modulation_full[:, 5],
        )
        normed_two = end_width(middle_width(normed_parts))
        hidden_act, hidden_slope = run(
            raise_hidden, normed_two, ring_up, hidden_span, biases[:, 9:13].reshape(2, 4 * width)
        )
        lanes.tick()
        ring_grad_down = queued(
            scatter(weight_part(lowered_full, hidden_act), 1)
        )
        lanes.until(ring_down)
        hidden_round, hidden_sums = run(
            hidden_gradient, lowered_full, ring_down, hidden_span, hidden_slope
        )
        halves = send_halves(hidden_round, ring_up, hidden_span, lanes.tick)
        own, away = send_away(*halves)
        ring_grad_up = queued(
            scatter(weight_part(normed_two, hidden_round), -1)
        )
        lanes.tick()

        def back_sums(grad_unit, unit_rows):
            return jnp.stack([jnp.sum(grad_unit, axis=1), jnp.sum(grad_unit * unit_rows, axis=1)])

        def normalize_back(grad_unit, unit_rows, inverse, totals):
            return inverse * (
                grad_unit - totals[0][:, None] / D - unit_rows * (totals[1][:, None] / D)
            )

        grad_normed_two = own + away.land().astype(F32)
        grad_unit_two = grad_normed_two * (1.0 + scale_two)
        sums = back_sums(grad_unit_two, unit_two)
        steps.mark(sums)
        sums_around = send_around(sums)
        lanes.tick()
        totals = total_around(sums_around)
        grad_residual = cotangent + normalize_back(grad_unit_two, unit_two, inverse_two, totals)
        grad_projected = gate_one * grad_residual
        projected_own = narrow(grad_projected)
        steps.mark(projected_own)
        projected_parts = start_width(projected_own)
        lowered_leaving = run(
            lambda *args: matmul_back(*args, 1), hidden_act, ring_down, hidden_span
        )
        lowered_kept = run(
            lambda *args: matmul_back(*args, 0), hidden_act, ring_down, hidden_span
        )
        arriving = [near_swap(half) for half in lowered_leaving]
        lanes.tick()
        projected_full = end_width(middle_width(projected_parts))
        grad_attended = run(attended_gradient, projected_full, ring_first, attended_span)
        so_far = ()
        for pair in range(pairs):
            so_far = steps.run(
                lambda t, l, g, *rest, pair=pair: attention_back(t, l, g, pair, pair + 1, *rest),
                triple,
                log_totals,
                grad_attended,
                *so_far,
            )
            if pair == 0:
                own_lowered, away_lowered = send_away(lowered_kept, arriving)
                lanes.tick()
        lowered_away = away_lowered.land()
        lanes.tick()
        triple_round, triple_sums = so_far
        partial_first = weight_part(normed_one, triple_round, 0)
        partial_first = weight_part(projected_full, attended, 3 * width, partial_first)
        ring_grad_first = queued(scatter(partial_first), ring_grad_up)
        halves = send_halves(triple_round, ring_first, triple_span, lanes.tick)
        own, away = send_away(*halves)
        lanes.tick()
        ((next_down, grad_down, moved_down),) = update(
            ("hidden",), ring_grad_down, (w_down,), (moments_down,)
        )
        lanes.until(ring_grad_up)
        lowered = own_lowered + lowered_away.astype(F32) + per_token(biases[:, 13])
        grad_lowered = gate_two * cotangent
        grad_normed_one = own + away.land().astype(F32)
        grad_unit_one = grad_normed_one * (1.0 + scale_one)
        sums = back_sums(grad_unit_one, unit_one)
        steps.mark(sums)
        sums_around = send_around(sums)
        head_sums = triple_sums.reshape(pairs, 2, 2, PAIR).transpose(1, 2, 0, 3)
        part = jnp.concatenate(
            [
                stream_sums(grad_normed_one)[:, None],
                stream_sums(grad_normed_one * unit_one)[:, None],
                stream_sums(grad_residual * projected)[:, None],
                stream_sums(grad_normed_two)[:, None],
                stream_sums(grad_normed_two * unit_two)[:, None],
                stream_sums(cotangent * lowered)[:, None],
                head_sums.reshape(2, 2, width),
                stream_sums(grad_projected)[:, None],
                hidden_sums.reshape(2, 4, width),
                stream_sums(grad_lowered)[:, None],
            ],
            axis=1,
        )
        steps.mark(part)
        lanes.tick()
        (part,) = steps.tie(part)
        part_all = lax.all_to_all(
            jnp.broadcast_to(part[None], (row_count,) + part.shape), "rows", 0, 0, tiled=True
        )
        steps.mark(part_all)
        totals = total_around(sums_around)
        grad_source = grad_residual + normalize_back(grad_unit_one, unit_one, inverse_one, totals)
        steps.add(grad_source)
        table_round = narrow(part_all[:, :, 0:6])
        grad_bias = jnp.sum(part_all, axis=0)
        silu_terms = jnp.einsum("bsic,dsic->bd", table_round, mod_round, preferred_element_type=F32)
        steps.mark(silu_terms)
        silu_around = send_around(silu_terms)
        grad_silu = total_around(silu_around)
        sigmoid_cond = jax.nn.sigmoid(cond)
        grad_cond = grad_silu * sigmoid_cond * (1.0 + cond * (1.0 - sigmoid_cond))
        next_bias, first_bias, second_bias = adam_step(biases, moments_bias, grad_bias)
        steps.add(next_bias, first_bias, second_bias, grad_cond)
        ((next_up, grad_up, moved_up),) = update(
            ("hidden",), ring_grad_up, (w_up,), (moments_up,)
        )
        lanes.until(ring_grad_first, 1)
        own_lowered, lowered_away = steps.tie(own_lowered, lowered_away)
        output = narrow(
            residual
            + gate_two * (own_lowered + lowered_away.astype(F32) + per_token(biases[:, 13]))
        )
        steps.add(output, grad_source)
        next_mod, grad_mod, first_mod, second_mod = steps.run(
            adam_modulation, w_mod, moments_mod, silu_cond, table_round
        )
        lanes.until(ring_grad_first)
        (next_qkv, grad_qkv, moved_qkv), (next_proj, grad_proj, moved_proj) = update(
            ("triple", "attended"),
            ring_grad_first,
            (w_qkv, w_proj),
            (moments_qkv, moments_proj),
        )
        return (
            output[None, :IMAGE_TOKENS],
            output[None, IMAGE_TOKENS:TOKENS],
            grad_source[None, :IMAGE_TOKENS],
            grad_source[None, IMAGE_TOKENS:TOKENS],
            grad_cond,
            grad_mod,
            grad_qkv,
            grad_proj,
            grad_up,
            grad_down,
            grad_bias,
            next_mod,
            next_qkv,
            next_proj,
            next_up,
            next_down,
            next_bias,
            first_mod,
            second_mod,
            moved_qkv,
            moved_proj,
            moved_up,
            moved_down,
            first_bias,
            second_bias,
        )

    return shards


def solution(mesh):
    in_specs = (
        P("rows", None, "cols"),
        P("rows", None, "cols"),
        P(None, "rows"),
        P("rows", None, "cols"),
        P("rows", None, "cols"),
        P("rows", None, None, "cols"),
        P("rows", None, None, "cols"),
        P("rows", None, "cols"),
        P("rows", None, None, "cols"),
        P("rows", None, None, "cols"),
        P(None, None, "cols"),
        P(None, "rows", None, None, "cols"),
        P(None, "rows", None, None, "cols"),
        P(None, "rows", None, "cols"),
        P(None, "rows", None, None, "cols"),
        P(None, "rows", None, None, "cols"),
        P(None, None, None, "cols"),
    )
    out_specs = (
        P("rows", None, "cols"),
        P("rows", None, "cols"),
        P("rows", None, "cols"),
        P("rows", None, "cols"),
        P(None, "rows"),
        P("rows", None, None, "cols"),
        P("rows", None, None, "cols"),
        P("rows", None, "cols"),
        P("rows", None, None, "cols"),
        P("rows", None, None, "cols"),
        P(None, None, "cols"),
        P("rows", None, None, "cols"),
        P("rows", None, None, "cols"),
        P("rows", None, "cols"),
        P("rows", None, None, "cols"),
        P("rows", None, None, "cols"),
        P(None, None, "cols"),
        P("rows", None, None, "cols"),
        P("rows", None, None, "cols"),
        P(None, "rows", None, None, "cols"),
        P(None, "rows", None, "cols"),
        P(None, "rows", None, None, "cols"),
        P(None, "rows", None, None, "cols"),
        P(None, None, "cols"),
        P(None, None, "cols"),
    )
    shards = make_shards(mesh.shape["rows"], mesh.shape["cols"])
    return jax.shard_map(shards, mesh=mesh, in_specs=in_specs, out_specs=out_specs, check_vma=False)
```
